32 devices in a mesh: blk: 8 (over z, y), rhs: 4 (over x, core).
Axes of the slice: x: 2, y: 2, z: 4, core: 2. Of those that a mesh axis runs over, the one named last changes fastest.
Arguments:
- charges: bfloat16 [64, 16384], P('rhs', 'blk'), may hold values from -6 to 6
- counts: int32 [128], P('blk'), may hold values from 32 to 128
- self_tiles: bfloat16 [128, 128, 128], P('blk'), may hold values from -0.5 to 0.5
- basis: bfloat16 [128, 128, 64], P('blk'), may hold values from -0.5 to 0.5
- near_first: int32 [4096], P('blk'), may hold values from 0 to 127, as said below
- near_second: int32 [4096], P('blk'), may hold values from 0 to 127, as said below
- near_tiles: bfloat16 [4096, 128, 128], P(('blk', 'rhs')), may hold values from -0.125 to 0.125
- far_source: int32 [4096], P('blk'), may hold values from 0 to 127, as said below
- far_target: int32 [4096], P('blk'), may hold values from 0 to 127, as said below
- far_tiles: bfloat16 [4096, 64, 64], P('blk'), may hold values from -0.09375 to 0.09375
Outputs:
- potentials: float32 [64, 16384], P('rhs', 'blk')
The draws below stay inside these ranges and needn't reach their ends.
Inputs may be any that keep to these rules, and one draw needn't show every extreme that they name: Block c holds counts[c] real panels in its first slots; the others are padding. `near_first`: the first block of a pair is one of the 16 blocks of the blk index that holds the pair. `near_second`: the second block lies within 48 blocks of the first, counted cyclically. `far_source`: any cell. `far_target`: the target cell is one of the 16 cells of the blk index that holds the interaction.
All inputs are finite; a program needn't handle non-finite values.
Results may differ from the reference program's by a relative error of at most 0.0012.
Values may be sent and summed in bfloat16 or wider, within the bound.
No kernel may reach another device: no remote copies, remote signals or barrier semaphores. Data moves between devices by JAX's collectives and lax.ppermute only.
A program may use at most 128 MiB of HBM per device.

```python
import jax
import jax.numpy as jnp
from jax import lax

BS = 128
P_SIZE = 64
NRHS = 64
BLK_DEV = 16
PAIR_DEV = 128
FAR_DEV = 512
BLOCKS = 128
PANELS = 16384
NEAR = 4096
FAR = 4096


def near_pairs(key):
    owners = BLOCKS // BLK_DEV
    per_owner = NEAR // owners
    owner = jnp.arange(NEAR, dtype=jnp.int32) // per_owner
    first = owner * BLK_DEV + jax.random.randint(jax.random.fold_in(key, 11), (NEAR,), 0, BLK_DEV, dtype=jnp.int32)
    offset = jax.random.randint(jax.random.fold_in(key, 12), (NEAR,), -3 * BLK_DEV, 3 * BLK_DEV + 1, dtype=jnp.int32)
    second = jnp.mod(first + offset, BLOCKS).astype(jnp.int32)
    return (first.astype(jnp.int32), second)


def draw_near_first(key, part):
    return near_pairs(key)[0]


def draw_near_second(key, part):
    return near_pairs(key)[1]


def draw_far_source(key, part):
    return jax.random.randint(jax.random.fold_in(key, 21), (FAR,), 0, BLOCKS, dtype=jnp.int32)


def draw_far_target(key, part):
    owner = jnp.arange(FAR, dtype=jnp.int32) // FAR_DEV
    local = jax.random.randint(jax.random.fold_in(key, 22), (FAR,), 0, BLK_DEV, dtype=jnp.int32)
    return (owner * BLK_DEV + local).astype(jnp.int32)


def set_ends(drawn, own_key, low, top_value):
    shape = drawn.shape
    spot = [jax.random.randint(jax.random.fold_in(own_key, axis), (), 0, shape[axis]) for axis in range(len(shape))]
    drawn = drawn.at[tuple(spot)].set(low)
    longest = shape.index(max(shape))
    spot[longest] = (spot[longest] + 1) % shape[longest]
    return drawn.at[tuple(spot)].set(top_value)


def block_scale(rng, dims, pieces, low, top_value):
    def one(position, blocks):
        draws = jax.random.uniform(jax.random.fold_in(jax.random.fold_in(rng, 6), position), (blocks,), jnp.float32, low / len(pieces), top_value / len(pieces))
        return jnp.repeat(jnp.exp(draws), dims[position] // blocks).reshape((-1,) + (1,) * (len(dims) - position - 1))

    level = one(*pieces[0])
    for cut in pieces[1:]:
        level = level * one(*cut)
    return level


def bell_draw(stream_key, shape, deviation, bound, pieces=(), kind=jnp.bfloat16):
    factor_of = block_scale(stream_key, shape, pieces, -0.22, 0.18) if pieces else 1.0
    drawn = jax.random.normal(stream_key, shape, jnp.float32) * deviation * factor_of
    return jnp.minimum(jnp.maximum(drawn, -bound), bound).astype(kind)


def setup_inputs(seed: int = 0) -> dict:
    key_list = jax.random.split(jax.random.key(seed), 11)
    charges = bell_draw(key_list[0], (NRHS, PANELS), 1.0, 6.0, ((0, 4), (1, 8)))
    counts = set_ends(jax.random.randint(key_list[1], (BLOCKS,), BS // 4, BS + 1), jax.random.fold_in(key_list[1], 1), BS // 4, BS).astype(jnp.int32)
    self_tiles = bell_draw(key_list[2], (BLOCKS, BS, BS), BS ** -0.5, 0.5, ((0, 8),))
    basis = bell_draw(key_list[3], (BLOCKS, BS, P_SIZE), BS ** -0.5, 0.5, ((0, 8),))
    near_first = draw_near_first(jax.random.fold_in(key_list[10], 71), 0)
    near_second = draw_near_second(jax.random.fold_in(key_list[10], 71), 0)
    near_tiles = bell_draw(key_list[6], (NEAR, BS, BS), (BS * 16) ** -0.5, 0.125, ((0, 32),))
    far_source = draw_far_source(jax.random.fold_in(key_list[10], 71), 0)
    far_target = draw_far_target(jax.random.fold_in(key_list[10], 71), 0)
    far_tiles = bell_draw(key_list[9], (FAR, P_SIZE, P_SIZE), (P_SIZE * 64) ** -0.5, 0.09375, ((0, 8),))
    return dict(charges=charges, counts=counts, self_tiles=self_tiles, basis=basis, near_first=near_first, near_second=near_second, near_tiles=near_tiles, far_source=far_source, far_target=far_target, far_tiles=far_tiles)


def pair_terms(blocks, first, second, tiles):
    hi = lax.Precision.HIGHEST
    tiles32 = tiles.astype(jnp.float32)
    from_second = blocks[:, second].astype(jnp.float32)
    from_first = blocks[:, first].astype(jnp.float32)
    to_first = jnp.einsum('rnj,nij->rni', from_second, tiles32, precision=hi)
    to_second = jnp.einsum('rni,nij->rnj', from_first, tiles32, precision=hi)
    return to_first, to_second


def reference(charges, counts, self_tiles, basis, near_first, near_second, near_tiles, far_source, far_target, far_tiles):
    hi = lax.Precision.HIGHEST
    rows = charges.shape[0]
    valid = (jnp.arange(BS)[None, :] < counts[:, None]).reshape(-1)
    masked = jnp.where(valid[None, :], charges, jnp.zeros_like(charges))
    blocks = masked.reshape(rows, BLOCKS, BS)
    moments = jnp.einsum('rcb,cbp->rcp', blocks.astype(jnp.float32), basis.astype(jnp.float32), precision=hi).astype(jnp.bfloat16)

    def near_step(total, group):
        first, second, tiles = group
        to_first, to_second = pair_terms(blocks, first, second, tiles)
        return total.at[:, first].add(to_first).at[:, second].add(to_second), None

    near_groups = (near_first.reshape(-1, PAIR_DEV), near_second.reshape(-1, PAIR_DEV), near_tiles.reshape(-1, PAIR_DEV, BS, BS))
    near, _ = lax.scan(near_step, jnp.zeros((rows, BLOCKS, BS), jnp.float32), near_groups)

    def far_step(total, group):
        source, target, tiles = group
        to_target, to_source = pair_terms(moments, target, source, tiles)
        return total.at[:, target].add(to_target).at[:, source].add(to_source), None

    far_groups = (far_source.reshape(-1, FAR_DEV), far_target.reshape(-1, FAR_DEV), far_tiles.reshape(-1, FAR_DEV, P_SIZE, P_SIZE))
    fields, _ = lax.scan(far_step, jnp.zeros((rows, BLOCKS, P_SIZE), jnp.float32), far_groups)
    fields = fields.astype(jnp.bfloat16)
    far_part = jnp.einsum('rcp,cbp->rcb', fields.astype(jnp.float32), basis.astype(jnp.float32), precision=hi)
    self_part = jnp.einsum('rcj,cij->rci', blocks.astype(jnp.float32), self_tiles.astype(jnp.float32), precision=hi)
    total = (near + far_part + self_part).reshape(rows, PANELS)
    return jnp.where(valid[None, :], total, jnp.zeros_like(total))
```

```python
import functools

import jax
import jax.numpy as jnp
from jax import lax
from jax.experimental import pallas as pl
from jax.experimental.pallas import tpu as pltpu
from jax.sharding import PartitionSpec as P

F32, BF16, I16, I32 = jnp.float32, jnp.bfloat16, jnp.int16, jnp.int32
GROUP = 16
TOP = 32767.0
VMEM = pl.BlockSpec(memory_space=pltpu.VMEM)
SMEM = pl.BlockSpec(memory_space=pltpu.SMEM)
NAT = (((1,), (0,)), ((), ()))
TRN = (((1,), (1,)), ((), ()))


def params(mib):
    return pltpu.CompilerParams(vmem_limit_bytes=mib << 20)


def dot(lhs, rhs, dims):
    return lax.dot_general(lhs, rhs, dims, preferred_element_type=F32)


def scale_blocks(count):
    return -(-count // GROUP)


def encode(src, out, count, peak, inv):
    peak[...] = jnp.zeros_like(peak)

    def find(b, _):
        peak[pl.ds(b, 1), :] = jnp.max(jnp.abs(src[b]), axis=0, keepdims=True)
        return 0

    lax.fori_loop(0, count, find, 0, unroll=8)
    code = jnp.ceil(jnp.log2(jnp.maximum(peak[...], 1e-30)) * 8.0) + 1.0
    inv[...] = TOP * jnp.exp2(code * -0.125)
    for s in range(scale_blocks(count)):
        out[count + s] = code[s * GROUP : (s + 1) * GROUP].astype(I32).astype(I16)

    def put(b, _):
        out[b] = jnp.round(src[b] * inv[pl.ds(b, 1), :]).astype(I32).astype(I16)
        return 0

    lax.fori_loop(0, count, put, 0, unroll=8)


def decode_scales(coded, count, scale):
    for s in range(scale_blocks(count)):
        code = coded[count + s].astype(I32).astype(F32)
        scale[s * GROUP : (s + 1) * GROUP, :] = jnp.exp2(code * 0.125) * (1.0 / TOP)


def decode(coded, scale, b):
    return coded[b].astype(I32).astype(F32) * scale[pl.ds(b, 1), :]


def prep_kernel(counts, charges, basis_t, out):
    cells, terms, size = basis_t.shape
    rows = charges.shape[0]
    lane = lax.broadcasted_iota(I32, (rows, size), 1)
    moments = []
    for c in range(cells):
        x = charges[:, c * size : (c + 1) * size]
        x = jnp.where(lane < counts[c], x, jnp.zeros_like(x))
        out[c] = x
        moments.append(dot(x, basis_t[c], TRN))
    for k in range(cells // 2):
        out[cells + k] = jnp.concatenate(moments[2 * k : 2 * k + 2], axis=1).astype(BF16)


def far_source_kernel(tgt, pos, mine, tiles, turned, out, flip, lhs, acc):
    step = pl.program_id(0)
    half = mine.shape[2] // 2
    quarter = half // 2
    chunk = tiles.shape[1]
    pairs = half // 2
    cells = 2 * mine.shape[0]

    @pl.when(step == 0)
    def _():
        acc[...] = jnp.zeros_like(acc)
        for k in range(cells // 2):
            x = mine[k]
            for h in range(2):
                y = x[:, h * half : (h + 1) * half]
                lhs[2 * k + h] = jnp.concatenate([y[:, :quarter], y[:, quarter:]], axis=0)

    for i in range(pairs):
        both = jnp.concatenate(
            [tiles[i * half : (i + 1) * half, :], tiles[(i + pairs) * half : (i + pairs + 1) * half, :]], axis=0
        )
        flip[i * chunk : (i + 1) * chunk, :] = both.astype(F32).T

    unroll = 16

    def work(g, _):
        sums = []
        for u in range(unroll):
            e = g * unroll + u
            w = flip[pl.ds(e, pairs, stride=chunk), :].astype(BF16)
            turned[e] = w
            sums.append(dot(lhs[tgt[step * chunk + e]], w, NAT))
        for u in range(unroll):
            acc[pos[step * chunk + g * unroll + u]] += sums[u]
        return 0

    lax.fori_loop(0, chunk // unroll, work, 0)

    @pl.when(step == pl.num_programs(0) - 1)
    def _():
        rows = mine.shape[1]

        def fold(k, _):
            a, b = acc[2 * k], acc[2 * k + 1]
            out[k] = jnp.concatenate(
                [a[:rows, :half] + a[rows:, half:], b[:rows, :half] + b[rows:, half:]], axis=1
            )
            return 0

        lax.fori_loop(0, out.shape[0], fold, 0)


def far_target_kernel(stride, cells, tgt, pos, everyone, turned, out, lhs, acc):
    step = pl.program_id(0)
    rows, lanes = everyone.shape[1], everyone.shape[2]
    half = lanes // 2
    chunk = turned.shape[0]
    owners = everyone.shape[0] // stride

    @pl.when(step == 0)
    def _():
        acc[...] = jnp.zeros_like(acc)
        low = lax.broadcasted_iota(I32, (rows, lanes), 1) < half

        def spread(o, _):
            for k in range(cells // 2):
                x = everyone[o * stride + cells + k]
                y = jnp.concatenate([x[:, half:], x[:, :half]], axis=1)
                zero = jnp.zeros_like(x)
                at = o * cells + 2 * k
                lhs[at] = jnp.concatenate([jnp.where(low, x, zero), jnp.where(low, zero, y)], axis=0)
                lhs[at + 1] = jnp.concatenate([jnp.where(low, y, zero), jnp.where(low, zero, x)], axis=0)
            return 0

        lax.fori_loop(0, owners, spread, 0)

    unroll = 16

    def work(g, _):
        sums = []
        for u in range(unroll):
            e = g * unroll + u
            sums.append(dot(lhs[pos[step * chunk + e]], turned[e], TRN))
        for u in range(unroll):
            acc[tgt[step * chunk + g * unroll + u]] += sums[u]
        return 0

    lax.fori_loop(0, chunk // unroll, work, 0)

    @pl.when(step == pl.num_programs(0) - 1)
    def _():
        for k in range(cells // 2):
            a, b = acc[2 * k], acc[2 * k + 1]
            out[k] = jnp.concatenate([a[:rows], a[rows:], b[:rows], b[rows:]], axis=1)


def near_loop(step, chunk, base, lhs, lhs_at, tiles, dims, acc, acc_at):
    unroll = 16

    def work(g, _):
        sums = []
        for u in range(unroll):
            n = g * unroll + u
            sums.append(dot(lhs[lhs_at[base + n]], tiles[n], dims))
        for u in range(unroll):
            acc[acc_at[base + g * unroll + u]] += sums[u]
        return 0

    lax.fori_loop(0, chunk // unroll, work, 0)


def near_second_kernel(first, second, mine, theirs, tiles, other, keep, send, lhs, acc, peak, inv):
    step = pl.program_id(0)
    steps = pl.num_programs(0) // 2
    rows = mine.shape[1]
    chunk = tiles.shape[0]
    total = keep.shape[0]

    @pl.when(step == 0)
    def _():
        acc[...] = jnp.zeros_like(acc)
        for c in range(lhs.shape[0]):
            lhs[c] = jnp.concatenate([mine[c], theirs[c]], axis=0)

    @pl.when(step < steps)
    def _():
        near_loop(step, chunk, step * chunk, lhs, first, tiles, NAT, acc, second)

    @pl.when(step >= steps)
    def _():
        near_loop(step, chunk, step * chunk, lhs, first, other, NAT, acc, second)

    @pl.when(step == 2 * steps - 1)
    def _():
        def split(b, _):
            keep[b] = acc[b, :rows, :]
            return 0

        lax.fori_loop(0, total, split, 0, unroll=8)
        encode(acc.at[:, rows:, :], send, total, peak, inv)


def near_first_kernel(stride, cells, first, second, everyone, theirs, tiles, other, keep, send, lhs, acc):
    step = pl.program_id(0)
    steps = pl.num_programs(0) // 2
    rows = everyone.shape[1]
    chunk = tiles.shape[0]

    @pl.when(step == 0)
    def _():
        acc[...] = jnp.zeros_like(acc)

        def fill(o, _):
            for c in range(cells):
                lhs[o * cells + c] = jnp.concatenate([everyone[o * stride + c], theirs[o * cells + c]], axis=0)
            return 0

        lax.fori_loop(0, everyone.shape[0] // stride, fill, 0)

    @pl.when(step < steps)
    def _():
        near_loop(step, chunk, step * chunk, lhs, second, tiles, TRN, acc, first)

    @pl.when(step >= steps)
    def _():
        near_loop(step, chunk, step * chunk, lhs, second, other, TRN, acc, first)

    @pl.when(step == 2 * steps - 1)
    def _():
        for c in range(cells):
            keep[c] = acc[c, :rows, :]
            send[c] = acc[c, rows:, :]


def meet_kernel(cells, mine, coded, far, keep, send, acc, scale, peak, inv):
    total = mine.shape[0]
    near_b, far_b = cells, cells // 2
    stride = near_b + far_b
    owners = total // cells
    decode_scales(coded, total, scale)

    def owner(o, dst, at):
        def near_part(c, _):
            b = o * near_b + c
            dst[at * stride + c] = mine[b] + decode(coded, scale, b)
            return 0

        lax.fori_loop(0, near_b, near_part, 0, unroll=8)
        for c in range(far_b):
            dst[at * stride + near_b + c] = far[o * far_b + c]

    for o in range(owners // 2):
        owner(o, keep, o)
        owner(o + owners // 2, acc, o)
    encode(acc, send, acc.shape[0], peak, inv)


def add_kernel(mine, coded, keep, send, acc, scale, peak, inv):
    total = mine.shape[0]
    half = total // 2
    decode_scales(coded, total, scale)

    def one(b, _):
        keep[b] = mine[b] + decode(coded, scale, b)
        acc[b] = mine[half + b] + decode(coded, scale, half + b)
        return 0

    lax.fori_loop(0, half, one, 0, unroll=8)
    encode(acc, send, half, peak, inv)


def final_kernel(counts, mine, coded, first, first_other, target, moved, self_tiles, basis_t, out, scale):
    cells, terms, size = basis_t.shape
    rows = out.shape[0]
    decode_scales(coded, mine.shape[0], scale)
    lane = lax.broadcasted_iota(I32, (rows, size), 1)
    for k in range(cells // 2):
        b = cells + k
        fields = (mine[b] + decode(coded, scale, b) + target[k]).astype(BF16)
        for h in range(2):
            c = 2 * k + h
            near = mine[c] + decode(coded, scale, c) + first[c] + first_other[c]
            far = dot(fields[:, h * terms : (h + 1) * terms], basis_t[c], NAT)
            own = dot(moved[c], self_tiles[c], TRN)
            total = near + far + own
            out[:, c * size : (c + 1) * size] = jnp.where(lane < counts[c], total, jnp.zeros_like(total))


def body(
    charges,
    counts,
    self_tiles,
    basis,
    near_first,
    near_second,
    near_tiles,
    far_source,
    far_target,
    far_tiles,
):
    blks = lax.axis_size("blk")
    ranks = lax.axis_size("rhs")
    me = lax.axis_index("blk")
    rank = lax.axis_index("rhs")
    cells, size, _ = self_tiles.shape
    terms = basis.shape[2]
    rows = charges.shape[0]
    pairs = near_tiles.shape[0]
    fars = far_tiles.shape[0]
    bits = blks.bit_length() - 1
    order = [*range(1, bits), 0]
    halfc = cells // 2
    stride = cells + halfc
    total = blks * cells

    def swap_rank(x, d):
        return lax.ppermute(x, "rhs", [(i, i ^ d) for i in range(ranks)])

    def swap_blk(x, bit):
        return lax.ppermute(x, "blk", [(i, i ^ (1 << bit)) for i in range(blks)])

    def place(block):
        other = (block // cells) ^ me
        at = sum(((other >> bit) & 1) << s for s, bit in enumerate(order))
        return at * cells + block % cells

    def shape(n, dtype, r=rows):
        return jax.ShapeDtypeStruct((n, r, size), dtype)

    def scratch(n, r=rows):
        return pltpu.VMEM((n, r, size), F32)

    def scales(n):
        return pltpu.VMEM((scale_blocks(n) * GROUP, size), F32)

    other_tiles = swap_rank(near_tiles, 1)
    basis_t = jnp.swapaxes(basis, 1, 2)

    own = pl.pallas_call(
        prep_kernel,
        in_specs=[SMEM, VMEM, VMEM],
        out_specs=VMEM,
        out_shape=shape(stride, BF16),
        compiler_params=params(16),
        name="prep",
    )(counts, charges, basis_t)
    charge_own = own[:cells]
    charge_other = swap_rank(charge_own, 2)

    gathered = own
    for bit in order:
        gathered = jnp.concatenate([gathered, swap_blk(gathered, bit)], axis=0)

    def pick(x):
        return jnp.concatenate(
            [lax.dynamic_slice(x, (r * pairs,), (pairs,)) for r in (rank, rank ^ 1)]
        )

    first = pick(near_first % cells)
    second = pick(place(near_second))
    tgt = far_target % cells
    src = place(far_source)

    fchunk = 128
    tiles_ij = jnp.transpose(far_tiles, (1, 2, 0)).reshape(terms * terms, fars)
    turned, far_part = pl.pallas_call(
        far_source_kernel,
        grid_spec=pltpu.PrefetchScalarGridSpec(
            num_scalar_prefetch=2,
            grid=(fars // fchunk,),
            in_specs=[
                pl.BlockSpec((halfc, rows, size), lambda i, *_: (0, 0, 0)),
                pl.BlockSpec((terms * terms, fchunk), lambda i, *_: (0, i)),
            ],
            out_specs=[
                pl.BlockSpec((fchunk, terms // 2, size), lambda i, *_: (i, 0, 0)),
                pl.BlockSpec((total // 2, rows, size), lambda i, *_: (0, 0, 0)),
            ],
            scratch_shapes=[
                pltpu.VMEM((terms // 2 * fchunk, size), F32),
                pltpu.VMEM((cells, 2 * rows, terms // 2), BF16),
                scratch(total, 2 * rows),
            ],
        ),
        out_shape=[shape(fars, BF16, terms // 2), shape(total // 2, F32)],
        compiler_params=params(32),
        cost_estimate=pl.CostEstimate(flops=2 * fars * rows * terms * terms, bytes_accessed=10 << 20, transcendentals=0),
        name="far_source",
    )(tgt, src, own[cells:], tiles_ij)

    chunk = 32
    steps = pairs // chunk

    def whole(n, r=rows):
        return pl.BlockSpec((n, r, size), lambda i, *_: (0, 0, 0))

    tile_specs = [
        pl.BlockSpec((chunk, size, size), lambda i, *_: (jnp.minimum(i, steps - 1), 0, 0)),
        pl.BlockSpec((chunk, size, size), lambda i, *_: (jnp.maximum(i - steps, 0), 0, 0)),
    ]
    near_cost = pl.CostEstimate(flops=8 * pairs * rows * size * size, bytes_accessed=12 << 20, transcendentals=0)
    keep, send = pl.pallas_call(
        near_second_kernel,
        grid_spec=pltpu.PrefetchScalarGridSpec(
            num_scalar_prefetch=2,
            grid=(2 * steps,),
            in_specs=[whole(cells), whole(cells), *tile_specs],
            out_specs=[whole(total), whole(total + scale_blocks(total))],
            scratch_shapes=[
                pltpu.VMEM((cells, 2 * rows, size), BF16),
                scratch(total, 2 * rows),
                scales(total),
                scales(total),
            ],
        ),
        out_shape=[shape(total, F32), shape(total + scale_blocks(total), I16)],
        compiler_params=params(48),
        cost_estimate=near_cost,
        name="near_second",
    )(first, second, charge_own, charge_other, near_tiles, other_tiles)

    coded = swap_rank(send, 2)
    half = blks // 2 * stride
    keep, send = pl.pallas_call(
        functools.partial(meet_kernel, cells),
        in_specs=[VMEM] * 3,
        out_specs=[VMEM] * 2,
        out_shape=[shape(half, F32), shape(half + scale_blocks(half), I16)],
        scratch_shapes=[scratch(half), scales(total), scales(half), scales(half)],
        compiler_params=params(48),
        name="meet",
    )(keep, coded, far_part)
    coded = swap_blk(send, order[-1])

    for bit in reversed(order[:-1]):
        now, half = half, half // 2
        keep, send = pl.pallas_call(
            add_kernel,
            in_specs=[VMEM] * 2,
            out_specs=[VMEM] * 2,
            out_shape=[shape(half, F32), shape(half + scale_blocks(half), I16)],
            scratch_shapes=[scratch(half), scales(now), scales(half), scales(half)],
            compiler_params=params(32),
            name="add",
        )(keep, coded)
        coded = swap_blk(send, bit)

    charge_all_other = swap_rank(
        gathered.reshape(blks, stride, rows, size)[:, :cells].reshape(total, rows, size), 2
    )
    target_part = pl.pallas_call(
        functools.partial(far_target_kernel, stride, cells),
        grid_spec=pltpu.PrefetchScalarGridSpec(
            num_scalar_prefetch=2,
            grid=(fars // fchunk,),
            in_specs=[
                whole(blks * stride),
                pl.BlockSpec((fchunk, terms // 2, size), lambda i, *_: (i, 0, 0)),
            ],
            out_specs=whole(halfc),
            scratch_shapes=[
                pltpu.VMEM((total, 2 * rows, size), BF16),
                pltpu.VMEM((cells, 2 * rows, terms // 2), F32),
            ],
        ),
        out_shape=shape(halfc, F32),
        compiler_params=params(32),
        cost_estimate=pl.CostEstimate(flops=2 * fars * rows * terms * terms, bytes_accessed=6 << 20, transcendentals=0),
        name="far_target",
    )(tgt, src, gathered, turned)

    first_own, first_send = pl.pallas_call(
        functools.partial(near_first_kernel, stride, cells),
        grid_spec=pltpu.PrefetchScalarGridSpec(
            num_scalar_prefetch=2,
            grid=(2 * steps,),
            in_specs=[whole(blks * stride), whole(total), *tile_specs],
            out_specs=[whole(cells), whole(cells)],
            scratch_shapes=[
                pltpu.VMEM((total, 2 * rows, size), BF16),
                scratch(cells, 2 * rows),
            ],
        ),
        out_shape=[shape(cells, F32), shape(cells, F32)],
        compiler_params=params(32),
        cost_estimate=near_cost,
        name="near_first",
    )(first, second, gathered, charge_all_other, near_tiles, other_tiles)
    first_other = swap_rank(first_send, 2)

    return pl.pallas_call(
        final_kernel,
        in_specs=[SMEM] + [VMEM] * 8,
        out_specs=VMEM,
        out_shape=jax.ShapeDtypeStruct(charges.shape, F32),
        scratch_shapes=[scales(stride)],
        compiler_params=params(16),
        name="final",
    )(counts, keep, coded, first_own, first_other, target_part, charge_own, self_tiles, basis_t)


def solution(mesh):
    in_specs = (
        P("rhs", "blk"),
        P("blk"),
        P("blk", None, None),
        P("blk", None, None),
        P("blk"),
        P("blk"),
        P(("blk", "rhs"), None, None),
        P("blk"),
        P("blk"),
        P("blk", None, None),
    )
    out_specs = P("rhs", "blk")
    return jax.shard_map(body, mesh=mesh, in_specs=in_specs, out_specs=out_specs, check_vma=False)
```

```python
import functools

import jax
import jax.numpy as jnp
from jax import lax
from jax.experimental import pallas as pl
from jax.experimental.pallas import tpu as pltpu
from jax.sharding import PartitionSpec as P

F32, BF16, I16, I32 = jnp.float32, jnp.bfloat16, jnp.int16, jnp.int32
GROUP = 16
TOP = 32767.0
VMEM = pl.BlockSpec(memory_space=pltpu.VMEM)
SMEM = pl.BlockSpec(memory_space=pltpu.SMEM)
HBM = pl.BlockSpec(memory_space=pltpu.HBM)
NAT = (((1,), (0,)), ((), ()))
TRN = (((1,), (1,)), ((), ()))


def params(mib):
    return pltpu.CompilerParams(vmem_limit_bytes=mib << 20)


def dot(lhs, rhs, dims):
    return lax.dot_general(lhs, rhs, dims, preferred_element_type=F32)


def scale_blocks(count):
    return -(-count // GROUP)


def encode(src, out, count, peak, inv):
    peak[...] = jnp.zeros_like(peak)

    def find(b, _):
        peak[pl.ds(b, 1), :] = jnp.max(jnp.abs(src[b]), axis=0, keepdims=True)
        return 0

    lax.fori_loop(0, count, find, 0, unroll=8)
    code = jnp.ceil(jnp.log2(jnp.maximum(peak[...], 1e-30)) * 8.0) + 1.0
    inv[...] = TOP * jnp.exp2(code * -0.125)
    for s in range(scale_blocks(count)):
        out[count + s] = code[s * GROUP : (s + 1) * GROUP].astype(I32).astype(I16)

    def put(b, _):
        out[b] = jnp.round(src[b] * inv[pl.ds(b, 1), :]).astype(I32).astype(I16)
        return 0

    lax.fori_loop(0, count, put, 0, unroll=8)


def decode_scales(coded, count, scale):
    for s in range(scale_blocks(count)):
        code = coded[count + s].astype(I32).astype(F32)
        scale[s * GROUP : (s + 1) * GROUP, :] = jnp.exp2(code * 0.125) * (1.0 / TOP)


def decode(coded, scale, b):
    return coded[b].astype(I32).astype(F32) * scale[pl.ds(b, 1), :]


def prep_kernel(counts_in, charges_in, basis_in, out, counts, charges, basis_t, sems):
    copies = [
        pltpu.make_async_copy(src, dst, sems.at[i])
        for i, (src, dst) in enumerate(((counts_in, counts), (charges_in, charges), (basis_in, basis_t)))
    ]
    for copy in copies:
        copy.start()
    for copy in copies:
        copy.wait()
    cells, terms, size = basis_t.shape
    rows = charges.shape[0]
    lane = lax.broadcasted_iota(I32, (rows, size), 1)
    moments = []
    for c in range(cells):
        x = charges[:, c * size : (c + 1) * size]
        x = jnp.where(lane < counts[c], x, jnp.zeros_like(x))
        out[c] = x
        moments.append(dot(x, basis_t[c], TRN))
    for k in range(cells // 2):
        out[cells + k] = jnp.concatenate(moments[2 * k : 2 * k + 2], axis=1).astype(BF16)


PITCH = 136
FAR_UNROLL = 32


def far_source_kernel(offs, tgt, pos, mine, theirs, tiles, turned, keep, send, flip, lhs, acc):
    step = pl.program_id(0)
    rows, lanes = mine.shape[1:]
    half = lanes // 2
    pairs = half // 2
    chunk = tiles.shape[1]
    base = (offs[0] * pl.num_programs(0) + step) * chunk

    @pl.when(step == 0)
    def _():
        acc[...] = jnp.zeros_like(acc)
        for k in range(mine.shape[0]):
            x, y = mine[k], theirs[k]
            for h in range(2):
                at = h * half
                parts = [z[:, at + q * pairs : at + (q + 1) * pairs] for q in range(2) for z in (x, y)]
                lhs[2 * k + h] = jnp.concatenate(parts, axis=0)

    for i in range(pairs):
        both = jnp.concatenate(
            [tiles[i * half : (i + 1) * half, :], tiles[(i + pairs) * half : (i + pairs + 1) * half, :]], axis=0
        )
        flip[i * PITCH : i * PITCH + chunk, :] = both.astype(F32).T

    def work(g, _):
        sums = []
        for u in range(FAR_UNROLL):
            e = g * FAR_UNROLL + u
            w = flip[pl.ds(e, pairs, stride=PITCH), :].astype(BF16)
            turned[e] = w
            sums.append(dot(lhs[tgt[base + e]], w, NAT))
        for u in range(FAR_UNROLL):
            acc[pos[base + g * FAR_UNROLL + u]] += sums[u]
        return 0

    lax.fori_loop(0, chunk // FAR_UNROLL, work, 0)

    @pl.when(step == pl.num_programs(0) - 1)
    def _():
        def fold(k, _):
            a, b = acc[2 * k], acc[2 * k + 1]
            for r, out in enumerate((keep, send)):
                low, high = r * rows, (2 + r) * rows
                out[k] = jnp.concatenate(
                    [x[low : low + rows, :half] + x[high : high + rows, half:] for x in (a, b)], axis=1
                )
            return 0

        lax.fori_loop(0, keep.shape[0], fold, 0, unroll=4)


def far_target_kernel(stride, cells, offs, tgt, pos, everyone, theirs, turned, keep, send, lhs, acc):
    step = pl.program_id(0)
    rows, lanes = everyone.shape[1], everyone.shape[2]
    half = lanes // 2
    chunk = turned.shape[0]
    owners = everyone.shape[0] // stride
    base = (offs[0] * pl.num_programs(0) + step) * chunk

    @pl.when(step == 0)
    def _():
        acc[...] = jnp.zeros_like(acc)
        low = lax.broadcasted_iota(I32, (2 * rows, lanes), 1) < half

        def spread(o, _):
            for k in range(cells // 2):
                x = jnp.concatenate([everyone[o * stride + cells + k], theirs[o * (cells // 2) + k]], axis=0)
                y = jnp.concatenate([x[:, half:], x[:, :half]], axis=1)
                zero = jnp.zeros_like(x)
                at = o * cells + 2 * k
                lhs[at] = jnp.concatenate([jnp.where(low, x, zero), jnp.where(low, zero, y)], axis=0)
                lhs[at + 1] = jnp.concatenate([jnp.where(low, y, zero), jnp.where(low, zero, x)], axis=0)
            return 0

        lax.fori_loop(0, owners, spread, 0)

    def work(g, _):
        sums = []
        for u in range(FAR_UNROLL):
            e = g * FAR_UNROLL + u
            sums.append(dot(lhs[pos[base + e]], turned[e], TRN))
        for u in range(FAR_UNROLL):
            acc[tgt[base + g * FAR_UNROLL + u]] += sums[u]
        return 0

    lax.fori_loop(0, chunk // FAR_UNROLL, work, 0)

    @pl.when(step == pl.num_programs(0) - 1)
    def _():
        for k in range(cells // 2):
            a, b = acc[2 * k], acc[2 * k + 1]
            for r, out in enumerate((keep, send)):
                low, high = r * rows, (2 + r) * rows
                out[k] = jnp.concatenate([x[i : i + rows] for x in (a, b) for i in (low, high)], axis=1)


def near_loop(offs, lhs, lhs_at, tiles, other, dims, acc, acc_at, buf, sems, setup):
    chunk = buf.shape[1]
    each = tiles.shape[0] // chunk
    steps = 2 * each
    copies = [
        pltpu.make_async_copy((tiles, other)[k // each].at[pl.ds(k % each * chunk, chunk)], buf.at[k], sems.at[k])
        for k in range(steps)
    ]
    for copy in copies:
        copy.start()
    setup()
    for k in range(steps):
        copies[k].wait()
        base = offs[k // each] + k % each * chunk
        sums = [dot(lhs[lhs_at[base + n]], buf[k, n], dims) for n in range(chunk)]
        for n in range(chunk):
            acc[acc_at[base + n]] += sums[n]


def near_second_kernel(offs, first, second, mine, theirs, tiles, other, keep, send, lhs, acc, buf, peak, inv, sems):
    rows = mine.shape[1]
    total = keep.shape[0]

    def setup():
        acc[...] = jnp.zeros_like(acc)
        for c in range(lhs.shape[0]):
            lhs[c] = jnp.concatenate([mine[c], theirs[c]], axis=0)

    near_loop(offs, lhs, first, tiles, other, NAT, acc, second, buf, sems, setup)

    def split(b, _):
        keep[b] = acc[b, :rows, :]
        return 0

    lax.fori_loop(0, total, split, 0, unroll=8)
    encode(acc.at[:, rows:, :], send, total, peak, inv)


def near_first_kernel(stride, cells, offs, first, second, everyone, *refs):
    *parts, tiles, other, keep, send, lhs, acc, buf, sems = refs
    rows = everyone.shape[1]

    def setup():
        acc[...] = jnp.zeros_like(acc)
        start = 0
        for part in parts:
            count = part.shape[0] // cells

            def fill(o, _, part=part, start=start):
                for c in range(cells):
                    at = start + o
                    lhs[at * cells + c] = jnp.concatenate(
                        [everyone[at * stride + c], part[o * cells + c]], axis=0
                    )
                return 0

            lax.fori_loop(0, count, fill, 0)
            start += count

    near_loop(offs, lhs, second, tiles, other, TRN, acc, first, buf, sems, setup)
    for c in range(cells):
        keep[c] = acc[c, :rows, :]
        send[c] = acc[c, rows:, :]


def meet_kernel(cells, mine, coded, far, far_other, keep, send, acc, scale, peak, inv):
    total = mine.shape[0]
    near_b, far_b = cells, cells // 2
    stride = near_b + far_b
    owners = total // cells
    decode_scales(coded, total, scale)

    def owner(o, dst, at):
        def near_part(c, _):
            b = o * near_b + c
            dst[at * stride + c] = mine[b] + decode(coded, scale, b)
            return 0

        lax.fori_loop(0, near_b, near_part, 0, unroll=8)
        for c in range(far_b):
            dst[at * stride + near_b + c] = far[o * far_b + c] + far_other[o * far_b + c]

    for o in range(owners // 2):
        owner(o, keep, o)
        owner(o + owners // 2, acc, o)
    encode(acc, send, acc.shape[0], peak, inv)


def add_kernel(mine, coded, keep, send, acc, scale, peak, inv):
    total = mine.shape[0]
    half = total // 2
    decode_scales(coded, total, scale)

    def one(b, _):
        keep[b] = mine[b] + decode(coded, scale, b)
        acc[b] = mine[half + b] + decode(coded, scale, half + b)
        return 0

    lax.fori_loop(0, half, one, 0, unroll=8)
    encode(acc, send, half, peak, inv)


def final_kernel(
    counts, mine, coded, first, first_other, target, target_other, moved, self_tiles, basis_t, out, scale
):
    cells, terms, size = basis_t.shape
    rows = out.shape[0]
    decode_scales(coded, mine.shape[0], scale)
    lane = lax.broadcasted_iota(I32, (rows, size), 1)
    for k in range(cells // 2):
        b = cells + k
        fields = (mine[b] + decode(coded, scale, b) + target[k] + target_other[k]).astype(BF16)
        for h in range(2):
            c = 2 * k + h
            near = mine[c] + decode(coded, scale, c) + first[c] + first_other[c]
            far = dot(fields[:, h * terms : (h + 1) * terms], basis_t[c], NAT)
            own = dot(moved[c], self_tiles[c], TRN)
            total = near + far + own
            out[:, c * size : (c + 1) * size] = jnp.where(lane < counts[c], total, jnp.zeros_like(total))


def body(
    charges,
    counts,
    self_tiles,
    basis,
    near_first,
    near_second,
    near_tiles,
    far_source,
    far_target,
    far_tiles,
):
    blks = lax.axis_size("blk")
    ranks = lax.axis_size("rhs")
    me = lax.axis_index("blk")
    rank = lax.axis_index("rhs")
    cells, size, _ = self_tiles.shape
    terms = basis.shape[2]
    rows = charges.shape[0]
    pairs = near_tiles.shape[0]
    fars = far_tiles.shape[0]
    bits = blks.bit_length() - 1
    order = [*reversed(range(bits))]
    halfc = cells // 2
    stride = cells + halfc
    total = blks * cells

    def swap_rank(x, d):
        return lax.ppermute(x, "rhs", [(i, i ^ d) for i in range(ranks)])

    def swap_blk(x, bit):
        return lax.ppermute(x, "blk", [(i, i ^ (1 << bit)) for i in range(blks)])

    def place(block):
        other = (block // cells) ^ me
        at = sum(((other >> bit) & 1) << s for s, bit in enumerate(order))
        return at * cells + block % cells

    def shape(n, dtype, r=rows):
        return jax.ShapeDtypeStruct((n, r, size), dtype)

    def scratch(n, r=rows, dtype=F32):
        return pltpu.VMEM((n, r, size), dtype)

    def scales(n):
        return pltpu.VMEM((scale_blocks(n) * GROUP, size), F32)

    def whole(n, r=rows):
        return pl.BlockSpec((n, r, size), lambda i, *_: (0, 0, 0))

    def owners(x, low, high, begin, end):
        return x.reshape(-1, stride, rows, size)[low:high, begin:end].reshape(-1, rows, size)

    other_tiles = swap_rank(near_tiles, 1)
    basis_t = jnp.swapaxes(basis, 1, 2)

    own = pl.pallas_call(
        prep_kernel,
        in_specs=[HBM] * 3,
        out_specs=VMEM,
        out_shape=shape(stride, BF16),
        scratch_shapes=[
            pltpu.SMEM(counts.shape, I32),
            pltpu.VMEM(charges.shape, BF16),
            pltpu.VMEM(basis_t.shape, BF16),
            pltpu.SemaphoreType.DMA((3,)),
        ],
        compiler_params=params(8),
        name="prep",
    )(counts, charges, basis_t)
    charge_own = own[:cells]
    moment_own = own[cells:]
    moment_pair = swap_rank(moment_own, 1)

    gathered = own
    others = [swap_rank(charge_own, 2)]
    sent = 1
    for s, bit in enumerate(order):
        gathered = jnp.concatenate([gathered, swap_blk(gathered, bit)], axis=0)
        if s >= bits - 2:
            others.append(swap_rank(owners(gathered, sent, 2 << s, 0, cells), 2))
            sent = 2 << s

    first = near_first % cells
    second = place(near_second)
    tgt = far_target % cells
    src = place(far_source)
    offs = jnp.stack([rank * pairs, (rank ^ 1) * pairs])
    part = (rank & 1).reshape(1)

    fchunk = min(128, fars // 2)
    fsteps = fars // 2 // fchunk
    far_cost = pl.CostEstimate(flops=2 * fars * rows * terms * terms, bytes_accessed=6 << 20, transcendentals=0)
    tiles_ij = jnp.transpose(far_tiles, (1, 2, 0)).reshape(terms * terms, fars)
    turned, far_keep, far_send = pl.pallas_call(
        far_source_kernel,
        grid_spec=pltpu.PrefetchScalarGridSpec(
            num_scalar_prefetch=3,
            grid=(fsteps,),
            in_specs=[
                whole(halfc),
                whole(halfc),
                pl.BlockSpec((terms * terms, fchunk), lambda i, at, *_: (0, at[0] * fsteps + i)),
            ],
            out_specs=[
                pl.BlockSpec((fchunk, terms // 2, size), lambda i, *_: (i, 0, 0)),
                whole(total // 2),
                whole(total // 2),
            ],
            scratch_shapes=[
                pltpu.VMEM((terms // 2 * PITCH, size), F32),
                pltpu.VMEM((cells, 4 * rows, terms // 2), BF16),
                scratch(total, 4 * rows),
            ],
        ),
        out_shape=[shape(fars // 2, BF16, terms // 2), shape(total // 2, F32), shape(total // 2, F32)],
        compiler_params=params(16 + total // 16),
        cost_estimate=far_cost,
        name="far_source",
    )(part, tgt, src, moment_own, moment_pair, tiles_ij)
    far_other = swap_rank(far_send, 1)

    chunk = min(64, pairs)
    steps = 2 * pairs // chunk
    near_cost = pl.CostEstimate(flops=8 * pairs * rows * size * size, bytes_accessed=12 << 20, transcendentals=0)
    buffers = [pltpu.VMEM((steps, chunk, size, size), BF16)]
    keep, send = pl.pallas_call(
        near_second_kernel,
        in_specs=[SMEM, SMEM, SMEM, VMEM, VMEM, HBM, HBM],
        out_specs=[VMEM, VMEM],
        out_shape=[shape(total, F32), shape(total + scale_blocks(total), I16)],
        scratch_shapes=[
            scratch(cells, 2 * rows, BF16),
            scratch(total, 2 * rows),
            *buffers,
            scales(total),
            scales(total),
            pltpu.SemaphoreType.DMA((steps,)),
        ],
        compiler_params=params(16 + total // 16),
        cost_estimate=near_cost,
        name="near_second",
    )(offs, first, second, charge_own, others[0], near_tiles, other_tiles)

    coded = swap_rank(send, 2)
    half = blks // 2 * stride
    keep, send = pl.pallas_call(
        functools.partial(meet_kernel, cells),
        in_specs=[VMEM] * 4,
        out_specs=[VMEM] * 2,
        out_shape=[shape(half, F32), shape(half + scale_blocks(half), I16)],
        scratch_shapes=[scratch(half), scales(total), scales(half), scales(half)],
        compiler_params=params(8 + total // 16),
        name="meet",
    )(keep, coded, far_keep, far_other)
    coded = swap_blk(send, order[-1])

    for bit in reversed(order[:-1]):
        now, half = half, half // 2
        keep, send = pl.pallas_call(
            add_kernel,
            in_specs=[VMEM] * 2,
            out_specs=[VMEM] * 2,
            out_shape=[shape(half, F32), shape(half + scale_blocks(half), I16)],
            scratch_shapes=[scratch(half), scales(now), scales(half), scales(half)],
            compiler_params=params(8 + total // 16),
            name="add",
        )(keep, coded)
        coded = swap_blk(send, bit)

    moment_all_pair = swap_rank(owners(gathered, 0, blks, cells, stride), 1)
    target_keep, target_send = pl.pallas_call(
        functools.partial(far_target_kernel, stride, cells),
        grid_spec=pltpu.PrefetchScalarGridSpec(
            num_scalar_prefetch=3,
            grid=(fsteps,),
            in_specs=[
                whole(blks * stride),
                whole(total // 2),
                pl.BlockSpec((fchunk, terms // 2, size), lambda i, *_: (i, 0, 0)),
            ],
            out_specs=[whole(halfc), whole(halfc)],
            scratch_shapes=[
                scratch(total, 4 * rows, BF16),
                pltpu.VMEM((cells, 4 * rows, terms // 2), F32),
            ],
        ),
        out_shape=[shape(halfc, F32), shape(halfc, F32)],
        compiler_params=params(12 + total // 16),
        cost_estimate=far_cost,
        name="far_target",
    )(part, tgt, src, gathered, moment_all_pair, turned)
    target_other = swap_rank(target_send, 1)

    first_keep, first_send = pl.pallas_call(
        functools.partial(near_first_kernel, stride, cells),
        in_specs=[SMEM] * 3 + [VMEM] * (1 + len(others)) + [HBM] * 2,
        out_specs=[VMEM, VMEM],
        out_shape=[shape(cells, F32), shape(cells, F32)],
        scratch_shapes=[
            scratch(total, 2 * rows, BF16),
            scratch(cells, 2 * rows),
            *buffers,
            pltpu.SemaphoreType.DMA((steps,)),
        ],
        compiler_params=params(16 + total // 16),
        cost_estimate=near_cost,
        name="near_first",
    )(offs, first, second, gathered, *others, near_tiles, other_tiles)
    first_other = swap_rank(first_send, 2)

    return pl.pallas_call(
        final_kernel,
        in_specs=[SMEM] + [VMEM] * 9,
        out_specs=VMEM,
        out_shape=jax.ShapeDtypeStruct(charges.shape, F32),
        scratch_shapes=[scales(stride)],
        compiler_params=params(8),
        name="final",
    )(
        counts, keep, coded, first_keep, first_other, target_keep, target_other, charge_own, self_tiles, basis_t
    )


def solution(mesh):
    in_specs = (
        P("rhs", "blk"),
        P("blk"),
        P("blk", None, None),
        P("blk", None, None),
        P("blk"),
        P("blk"),
        P(("blk", "rhs"), None, None),
        P("blk"),
        P("blk"),
        P("blk", None, None),
    )
    out_specs = P("rhs", "blk")
    return jax.shard_map(body, mesh=mesh, in_specs=in_specs, out_specs=out_specs, check_vma=False)
```

```python
import functools

import jax
import jax.numpy as jnp
from jax import lax
from jax.experimental import pallas as pl
from jax.experimental.pallas import tpu as pltpu
from jax.sharding import PartitionSpec as P

F32, BF16, I16, I32 = jnp.float32, jnp.bfloat16, jnp.int16, jnp.int32
REACH = 48
GROUP = 16
TOP = 32767.0
VMEM = pl.BlockSpec(memory_space=pltpu.VMEM)
SMEM = pl.BlockSpec(memory_space=pltpu.SMEM)
HBM = pl.BlockSpec(memory_space=pltpu.HBM)
NAT = (((1,), (0,)), ((), ()))
TRN = (((1,), (1,)), ((), ()))


def params(mib):
    return pltpu.CompilerParams(vmem_limit_bytes=mib << 20)


def in_hbm(x):
    return pltpu.with_memory_space_constraint(x, pltpu.HBM)


def dot(lhs, rhs, dims):
    return lax.dot_general(lhs, rhs, dims, preferred_element_type=F32)


def scale_blocks(count):
    return -(-count // GROUP)


def encode(get, out, outer, inner, peak, inv):
    count = outer * inner
    peak[...] = jnp.zeros_like(peak)

    def find(o, _):
        for i in range(inner):
            peak[pl.ds(o * inner + i, 1), :] = jnp.max(jnp.abs(get(o, i)), axis=0, keepdims=True)
        return 0

    lax.fori_loop(0, outer, find, 0)
    code = jnp.ceil(jnp.log2(jnp.maximum(peak[...], 1e-30)) * 8.0) + 1.0
    inv[...] = TOP * jnp.exp2(code * -0.125)
    for s in range(scale_blocks(count)):
        out[count + s] = code[s * GROUP : (s + 1) * GROUP].astype(I32).astype(I16)

    def put(o, _):
        for i in range(inner):
            b = o * inner + i
            out[b] = jnp.round(get(o, i) * inv[pl.ds(b, 1), :]).astype(I32).astype(I16)
        return 0

    lax.fori_loop(0, outer, put, 0)


def decode_scales(coded, count, scale):
    for s in range(scale_blocks(count)):
        code = coded[count + s].astype(I32).astype(F32)
        scale[s * GROUP : (s + 1) * GROUP, :] = jnp.exp2(code * 0.125) * (1.0 / TOP)


def decode(coded, scale, b):
    return coded[b].astype(I32).astype(F32) * scale[pl.ds(b, 1), :]


def prep_kernel(
    place, low, counts_in, charges_in, basis_in, near_first, near_second, far_source, far_target,
    out, idx, counts, charges, basis_t, lists, counts_row, sems,
):
    pairs = [(counts_in.at[0], counts), (charges_in, charges), (basis_in, basis_t), (counts_in, counts_row)]
    pairs += [
        (src, lists.at[pl.ds(i, 1)]) for i, src in enumerate((near_first, near_second, far_source, far_target))
    ]
    copies = [pltpu.make_async_copy(src, dst, sems.at[i]) for i, (src, dst) in enumerate(pairs)]
    for copy in copies:
        copy.start()
    for copy in copies:
        copy.wait()
    cells, terms, size = basis_t.shape
    rows = charges.shape[0]
    lane = lax.broadcasted_iota(I32, (rows, size), 1)
    moments = []
    for c in range(cells):
        x = charges[:, c * size : (c + 1) * size]
        x = jnp.where(lane < counts[c], x, jnp.zeros_like(x))
        out[c] = x
        moments.append(dot(x, basis_t[c], TRN))
    for k in range(cells // 2):
        out[cells + k] = jnp.concatenate(moments[2 * k : 2 * k + 2], axis=1).astype(BF16)
    first, second, source, target = (lists[i : i + 1, :] for i in range(4))
    reduce_at = place(second, 1)
    for row, value in (
        (FIRST, lax.rem(first, cells)),
        (SECOND, place(second, 0)),
        (SECOND_REDUCE, jnp.where(reduce_at < cells, reduce_at, reduce_at - (low - 1) * cells)),
        (SOURCE, place(source, 0)),
        (SOURCE_REDUCE, place(source, 1)),
        (TARGET, lax.rem(target, cells)),
    ):
        idx[row : row + 1, :] = value
    idx[COUNT : COUNT + 1, :cells] = counts_row[...]


FIRST, SECOND, SECOND_REDUCE, SOURCE, SOURCE_REDUCE, TARGET, COUNT = range(7)
PITCH = 136
FAR_UNROLL = 64
FAR_STEPS = 2
NEAR_UNROLL = 64
PARTS = 4


def far_source_kernel(idx, mine, theirs, tiles, turned, keep, *refs):
    *sends, flip, lhs, acc = refs
    rows, lanes = mine.shape[1:]
    half = lanes // 2
    pairs = half // 2
    total = turned.shape[0]
    chunk = total // FAR_STEPS
    acc[...] = jnp.zeros_like(acc)
    for k in range(mine.shape[0]):
        x, y = mine[k], theirs[k]
        for h in range(2):
            at = h * half
            lhs[2 * k + h] = jnp.concatenate([x[:, at : at + half], y[:, at : at + half]], axis=0)
    for step in range(FAR_STEPS):
        base = (lax.axis_index("rhs") & 1) * total + step * chunk
        span = pl.ds(pl.multiple_of(base, chunk), chunk)
        for i in range(pairs):
            both = [tiles[(i + h * pairs) * half : (i + h * pairs + 1) * half, span] for h in range(2)]
            flip[step, i * PITCH : i * PITCH + chunk, :] = jnp.concatenate(both, axis=0).astype(F32).T

        def work(g, _, step=step, base=base):
            sums = []
            at = g * FAR_UNROLL
            for u in range(FAR_UNROLL):
                w = flip[step, pl.ds(at + u, pairs, stride=PITCH), :]
                turned[step * chunk + at + u] = w.astype(BF16)
                moved = pltpu.roll(w, half, 1)
                w = jnp.concatenate([w[:, :half], moved[:, :half]], axis=0).astype(BF16)
                sums.append(dot(lhs[idx[TARGET, base + at + u]], w, NAT))
            for u in range(FAR_UNROLL):
                acc[idx[SOURCE_REDUCE, base + at + u]] += sums[u]
            return 0

        lax.fori_loop(0, chunk // FAR_UNROLL, work, 0)
    count = sends[0].shape[0]
    for q, send in enumerate(sends):

        def fold(k, _, q=q, send=send):
            for u in range(4):
                at = q * count + 4 * k + u
                both = jnp.concatenate([acc[2 * at], acc[2 * at + 1]], axis=1)
                keep[at] = both[:rows]
                send[4 * k + u] = both[rows:]
            return 0

        lax.fori_loop(0, count // 4, fold, 0)


def far_target_kernel(stride, cells, idx, everyone, theirs, turned, keep, send, lhs, acc):
    rows, lanes = everyone.shape[1], everyone.shape[2]
    half = lanes // 2
    chunk = turned.shape[0]
    owners = everyone.shape[0] // stride
    acc[...] = jnp.zeros_like(acc)
    low = lax.broadcasted_iota(I32, (2 * rows, lanes), 1) < half

    def spread(o, _):
        for k in range(cells // 2):
            x = jnp.concatenate([everyone[o * stride + cells + k], theirs[o * (cells // 2) + k]], axis=0)
            y = jnp.concatenate([x[:, half:], x[:, :half]], axis=1)
            zero = jnp.zeros_like(x)
            at = o * cells + 2 * k
            lhs[at] = jnp.concatenate([jnp.where(low, x, zero), jnp.where(low, zero, y)], axis=0)
            lhs[at + 1] = jnp.concatenate([jnp.where(low, y, zero), jnp.where(low, zero, x)], axis=0)
        return 0

    lax.fori_loop(0, owners, spread, 0)
    base = (lax.axis_index("rhs") & 1) * chunk

    def work(g, _):
        sums = []
        for u in range(FAR_UNROLL):
            e = g * FAR_UNROLL + u
            sums.append(dot(lhs[idx[SOURCE, base + e]], turned[e], TRN))
        for u in range(FAR_UNROLL):
            acc[idx[TARGET, base + g * FAR_UNROLL + u]] += sums[u]
        return 0

    lax.fori_loop(0, chunk // FAR_UNROLL, work, 0)
    for k in range(cells // 2):
        a, b = acc[2 * k], acc[2 * k + 1]
        for r, out in enumerate((keep, send)):
            at = (r * rows, (2 + r) * rows)
            out[k] = jnp.concatenate([x[i : i + rows] for x in (a, b) for i in at], axis=1)


def near_loop(idx, lhs, lhs_at, tiles, flip, dims, acc, acc_at):
    pairs = tiles.shape[0]
    base = (lax.axis_index("rhs") ^ flip) * pairs
    group = min(NEAR_UNROLL, pairs)
    for low in range(0, pairs, group):
        span = range(low, low + group)
        sums = [dot(lhs[idx[lhs_at, base + n]], tiles[n], dims) for n in span]
        for n in span:
            acc[idx[acc_at, base + n]] += sums[n - low]


def near_second_a_kernel(idx, mine, theirs, tiles, acc, both):
    rows, size = mine.shape[1:]

    acc[...] = jnp.zeros_like(acc)
    lane = lax.broadcasted_iota(I32, (rows, size), 1)
    for c in range(both.shape[0]):
        x = theirs[:, c * size : (c + 1) * size]
        x = jnp.where(lane < idx[COUNT, c], x, jnp.zeros_like(x))
        both[c] = jnp.concatenate([mine[c], x], axis=0)
    near_loop(idx, both, FIRST, tiles, 0, NAT, acc, SECOND_REDUCE)


def near_second_b_kernel(
    cells, idx, both, other, before, acc, keep_a, send_a, keep_b, send_b, peak, inv
):
    rows = both.shape[1] // 2
    half = cells // 2
    owners = acc.shape[0] // cells
    stay = keep_b.shape[0] // half
    near_loop(idx, both, FIRST, other, 1, NAT, acc, SECOND_REDUCE)
    encode(lambda o, c: acc[o * cells + c, rows:, :], send_a, owners, half, peak, inv)

    def part_b(o, i):
        return acc[(stay + o) * cells + half + i // 2, i % 2 * rows : (i % 2 + 1) * rows, :]

    encode(part_b, send_b, owners - stay, 2 * half, peak, inv)

    def own_a(o, _):
        for c in range(half):
            keep_a[o * half + c] = acc[o * cells + c, :rows, :]
        return 0

    def own_b(o, _):
        for c in range(half):
            keep_b[o * half + c] = acc[o * cells + half + c]
        return 0

    lax.fori_loop(0, owners, own_a, 0)
    lax.fori_loop(0, stay, own_b, 0)


def near_first_kernel(stride, cells, starts, idx, everyone, both, *refs):
    *parts, tiles, other, keep, send, lhs, acc = refs
    rows = everyone.shape[1]

    acc[...] = jnp.zeros_like(acc)
    lhs[:cells] = both[...]
    for start, part in zip(starts, parts):
        count = part.shape[0] // cells

        def fill(o, _, part=part, start=start):
            for c in range(cells):
                at = start + o
                lhs[at * cells + c] = jnp.concatenate([everyone[at * stride + c], part[o * cells + c]], axis=0)
            return 0

        lax.fori_loop(0, count, fill, 0)
    near_loop(idx, lhs, SECOND, tiles, 0, TRN, acc, FIRST)
    near_loop(idx, lhs, SECOND, other, 1, TRN, acc, FIRST)
    for c in range(cells):
        keep[c] = acc[c, :rows, :]
        send[c] = acc[c, rows:, :]


def join_kernel(mine, coded, out, scale):
    count = out.shape[0]
    decode_scales(coded, count, scale)

    def one(o, _):
        for i in range(8):
            b = o * 8 + i
            out[b] = mine[b] + decode(coded, scale, b)
        return 0

    lax.fori_loop(0, count // 8, one, 0)


def meet_a_kernel(half, low, mine, far, *refs):
    *far_others, keep, send, acc, peak, inv = refs
    count = far_others[0].shape[0]
    owners = far.shape[0] // half
    stay = owners // 2
    for p in range(owners):
        dst, at = (keep, p) if p < stay else (acc, p - stay)
        for c in range(half):
            if p == 0 or p >= low:
                near = mine[(p - low + 1 if p else 0) * half + c]
            else:
                near = jnp.zeros_like(mine[0])
            dst[at * 2 * half + c] = near
            b = p * half + c
            dst[at * 2 * half + half + c] = far[b] + far_others[b // count][b % count]
    encode(lambda o, i: acc[o * 8 + i], send, acc.shape[0] // 8, 8, peak, inv)


def meet_b_kernel(half, low, mine, coded, keep, send, acc, scale, peak, inv):
    rows = keep.shape[1]
    owners = keep.shape[0] // half
    decode_scales(coded, 2 * keep.shape[0], scale)
    for p in range(owners):
        for c in range(half):
            b = p * half + c
            both = [decode(coded, scale, 2 * b), decode(coded, scale, 2 * b + 1)]
            if p == 0 or p >= low:
                at = (p - low + 1 if p else 0) * half + c
                both = [both[0] + mine[at, :rows, :], both[1] + mine[at, rows:, :]]
            keep[b], acc[b] = both
    encode(lambda o, i: acc[o * 8 + i], send, acc.shape[0] // 8, 8, peak, inv)


def meet_kernel(half, mine_a, coded_a, mine_b, coded_b, keep, send, acc, scale_a, scale_b, peak, inv):
    owners = mine_b.shape[0] // half
    stay = owners // 2
    decode_scales(coded_a, mine_a.shape[0], scale_a)
    decode_scales(coded_b, mine_b.shape[0], scale_b)
    for p in range(owners):
        dst, at = (keep, p * 3) if p < stay else (acc, (p - stay) * 3)
        for c in range(half):
            a, b = p * 2 * half + c, p * half + c
            dst[at * half + c] = mine_a[a] + decode(coded_a, scale_a, a)
            dst[(at + 1) * half + c] = mine_b[b] + decode(coded_b, scale_b, b)
            a = a + half
            dst[(at + 2) * half + c] = mine_a[a] + decode(coded_a, scale_a, a)
    encode(lambda o, i: acc[o * 8 + i], send, acc.shape[0] // 8, 8, peak, inv)


def add_kernel(mine, coded, keep, send, acc, scale, peak, inv):
    total = mine.shape[0]
    half = total // 2
    decode_scales(coded, total, scale)

    def one(b, _):
        keep[b] = mine[b] + decode(coded, scale, b)
        acc[b] = mine[half + b] + decode(coded, scale, half + b)
        return 0

    lax.fori_loop(0, half, one, 0, unroll=8)
    encode(lambda o, i: acc[o * 8 + i], send, half // 8, 8, peak, inv)


def self_kernel(moved, self_tiles, out):
    for c in range(out.shape[0]):
        out[c] = dot(moved[c], self_tiles[c], TRN)


def final_kernel(
    counts, mine, coded, first, first_other, target, target_other, own, basis_t, out, scale
):
    cells, terms, size = basis_t.shape
    rows = out.shape[0]
    decode_scales(coded, mine.shape[0], scale)
    lane = lax.broadcasted_iota(I32, (rows, size), 1)
    for k in range(cells // 2):
        b = cells + k
        fields = (mine[b] + decode(coded, scale, b) + target[k] + target_other[k]).astype(BF16)
        for h in range(2):
            c = 2 * k + h
            near = mine[c] + decode(coded, scale, c) + first[c] + first_other[c]
            far = dot(fields[:, h * terms : (h + 1) * terms], basis_t[c], NAT)
            total = near + far + own[c]
            out[:, c * size : (c + 1) * size] = jnp.where(lane < counts[c], total, jnp.zeros_like(total))


def body(
    charges,
    counts,
    self_tiles,
    basis,
    near_first,
    near_second,
    near_tiles,
    far_source,
    far_target,
    far_tiles,
):
    blks = lax.axis_size("blk")
    ranks = lax.axis_size("rhs")
    me = lax.axis_index("blk")
    rank = lax.axis_index("rhs")
    cells, size, _ = self_tiles.shape
    terms = basis.shape[2]
    rows = charges.shape[0]
    pairs = near_tiles.shape[0]
    fars = far_tiles.shape[0]
    bits = blks.bit_length() - 1
    gather_order = [0, *range(bits - 1, 0, -1)]
    reduce_order = [*range(bits - 1, -1, -1)]
    halfc = cells // 2
    stride = cells + halfc
    total = blks * cells

    reach = -(-REACH // cells)
    masks = [sum(((p >> s) & 1) << bit for s, bit in enumerate(reduce_order)) for p in range(blks)]
    gaps = [min(min((o - (o ^ m)) % blks, ((o ^ m) - o) % blks) for o in range(blks)) for m in masks]
    low = 1
    kept = blks - low + 1

    def swap_rank(x, d):
        return lax.ppermute(x, "rhs", [(i, i ^ d) for i in range(ranks)])

    def swap_blk(x, bit):
        return lax.ppermute(x, "blk", [(i, i ^ (1 << bit)) for i in range(blks)])

    def place(block, reduce):
        other = lax.div(block, cells) ^ lax.axis_index("blk")
        order = reduce_order if reduce else gather_order
        at = sum(((other >> bit) & 1) << s for s, bit in enumerate(order))
        return at * cells + lax.rem(block, cells)

    def shape(n, dtype, r=rows):
        return jax.ShapeDtypeStruct((n, r, size), dtype)

    def scratch(n, r=rows, dtype=F32):
        return pltpu.VMEM((n, r, size), dtype)

    def scales(n):
        return pltpu.VMEM((scale_blocks(n) * GROUP, size), F32)

    def whole(n, r=rows):
        return pl.BlockSpec((n, r, size), lambda i, *_: (0, 0, 0))

    def owners(x, low, high, begin, end):
        return x.reshape(-1, stride, rows, size)[low:high, begin:end].reshape(-1, rows, size)

    other_tiles = swap_rank(near_tiles, 1)
    charge_other = swap_rank(charges, 2)
    basis_t = jnp.swapaxes(basis, 1, 2)

    width = max(near_first.shape[0], fars)
    lists = [x.reshape(1, -1) for x in (near_first, near_second, far_source, far_target)]
    own, idx = pl.pallas_call(
        functools.partial(prep_kernel, place, low),
        in_specs=[HBM] * 7,
        out_specs=[VMEM] * 2,
        out_shape=[shape(stride, BF16), jax.ShapeDtypeStruct((7, width), I32)],
        scratch_shapes=[
            pltpu.SMEM(counts.shape, I32),
            pltpu.VMEM(charges.shape, BF16),
            pltpu.VMEM(basis_t.shape, BF16),
            pltpu.VMEM((4, width), I32),
            pltpu.VMEM((1, cells), I32),
            pltpu.SemaphoreType.DMA((8,)),
        ],
        compiler_params=params(8),
        cost_estimate=pl.CostEstimate(flops=0, bytes_accessed=12 << 20, transcendentals=0),
        name="prep",
    )(*[in_hbm(x) for x in (counts.reshape(1, -1), charges, basis_t, *lists)])
    charge_own = own[:cells]
    moment_own = own[cells:]
    moment_pair = swap_rank(moment_own, 1)

    far_cost = pl.CostEstimate(flops=2 * fars * rows * terms * terms, bytes_accessed=12 << 20, transcendentals=0)
    tiles_ij = jnp.transpose(far_tiles, (1, 2, 0)).reshape(terms * terms, fars)
    near_cost = pl.CostEstimate(flops=4 * pairs * rows * size * size, bytes_accessed=10 << 20, transcendentals=0)
    first_cost = pl.CostEstimate(flops=8 * pairs * rows * size * size, bytes_accessed=20 << 20, transcendentals=0)
    coded_a = kept * halfc
    coded_b = blks // 2 * cells
    stay = kept - blks // 2
    near_acc = shape(kept * cells, F32, 2 * rows)
    near_sum, both = pl.pallas_call(
        near_second_a_kernel,
        in_specs=[SMEM, VMEM, VMEM, VMEM],
        out_specs=[VMEM] * 2,
        out_shape=[near_acc, shape(cells, BF16, 2 * rows)],
        compiler_params=params(4),
        cost_estimate=near_cost,
        name="near_second_a",
    )(idx, charge_own, charge_other, near_tiles)

    received = swap_blk(own, gather_order[0])
    received, near_sum = lax.optimization_barrier((received, near_sum))
    gathered = jnp.concatenate([own, received], axis=0)
    received = swap_blk(gathered, gather_order[1])
    near_sum, _ = lax.optimization_barrier((near_sum, gathered))

    _, keep_a, send_a, keep_b, send_b = pl.pallas_call(
        functools.partial(near_second_b_kernel, cells),
        in_specs=[SMEM, VMEM, VMEM, VMEM],
        out_specs=[VMEM] * 5,
        out_shape=[
            near_acc,
            shape(coded_a, F32),
            shape(coded_a + scale_blocks(coded_a), I16),
            shape(stay * halfc, F32, 2 * rows),
            shape(coded_b + scale_blocks(coded_b), I16),
        ],
        scratch_shapes=[
            scales(max(coded_a, coded_b)),
            scales(max(coded_a, coded_b)),
        ],
        input_output_aliases={3: 0},
        compiler_params=params(8),
        cost_estimate=near_cost,
        name="near_second_b",
    )(idx, both, other_tiles, near_sum)
    moment_late, _ = lax.optimization_barrier((moment_pair, send_a))
    turned, far_keep, *far_sends = pl.pallas_call(
        far_source_kernel,
        in_specs=[SMEM] + [VMEM] * 3,
        out_specs=[VMEM] * (2 + PARTS),
        out_shape=[
            shape(fars // 2, BF16, terms // 2),
            shape(total // 2, F32),
            *[shape(total // 2 // PARTS, F32)] * PARTS,
        ],
        scratch_shapes=[
            pltpu.VMEM((FAR_STEPS, terms // 2 * PITCH, size), F32),
            pltpu.VMEM((cells, 2 * rows, terms), BF16),
            pltpu.VMEM((total, 2 * rows, terms), F32),
        ],
        compiler_params=params(8 + total // 32),
        cost_estimate=far_cost,
        name="far_source",
    )(idx, moment_own, moment_late, tiles_ij)
    received, turned = lax.optimization_barrier((received, turned))
    others, starts = [], []
    for s, bit in enumerate(gather_order):
        if s > 1:
            received = swap_blk(gathered, bit)
        if s == bits - 1:
            received, others[0] = lax.optimization_barrier((received, others[0]))
            starts.append(1 << s)
            others.append(swap_rank(owners(received, 0, 1 << s, 0, cells), 2))
        if s > 0:
            gathered = jnp.concatenate([gathered, received], axis=0)
        if s == bits - 2:
            starts.append(1)
            others.append(swap_rank(owners(gathered, 1, 2 << s, 0, cells), 2))

    far_others = [swap_rank(x, 1) for x in far_sends]

    got_a = swap_rank(send_a, 2)
    got_b = swap_blk(send_b, reduce_order[-1])
    got_b, got_a = lax.optimization_barrier((got_b, got_a))
    half_a = blks // 2 * cells
    half_b = blks // 2 * halfc
    meet_cost = pl.CostEstimate(flops=0, bytes_accessed=3 << 20, transcendentals=0)
    keep_b, send_b = pl.pallas_call(
        functools.partial(meet_b_kernel, halfc, low),
        in_specs=[VMEM] * 2,
        out_specs=[VMEM] * 2,
        out_shape=[shape(half_b, F32), shape(half_b + scale_blocks(half_b), I16)],
        scratch_shapes=[scratch(half_b), scales(coded_b), scales(half_b), scales(half_b)],
        compiler_params=params(8 + total // 16),
        cost_estimate=meet_cost,
        name="meet_b",
    )(keep_b, got_b)
    keep_a, send_b = lax.optimization_barrier((keep_a, send_b))
    got_b = swap_rank(send_b, 2)
    joined = pl.pallas_call(
        join_kernel,
        in_specs=[VMEM] * 2,
        out_specs=VMEM,
        out_shape=shape(coded_a, F32),
        scratch_shapes=[scales(coded_a)],
        compiler_params=params(8),
        cost_estimate=pl.CostEstimate(flops=0, bytes_accessed=3 << 20, transcendentals=0),
        name="join",
    )(keep_a, got_a)
    keep_a, send_a = pl.pallas_call(
        functools.partial(meet_a_kernel, halfc, low),
        in_specs=[VMEM] * (2 + PARTS),
        out_specs=[VMEM] * 2,
        out_shape=[shape(half_a, F32), shape(half_a + scale_blocks(half_a), I16)],
        scratch_shapes=[scratch(half_a), scales(half_a), scales(half_a)],
        compiler_params=params(8 + total // 16),
        cost_estimate=meet_cost,
        name="meet_a",
    )(joined, far_keep, *far_others)
    got_a = swap_blk(send_a, reduce_order[-1])

    moment_all_pair = swap_rank(owners(gathered, 0, blks, cells, stride), 1)
    target_keep, target_send = pl.pallas_call(
        functools.partial(far_target_kernel, stride, cells),
        in_specs=[SMEM] + [VMEM] * 3,
        out_specs=[VMEM] * 2,
        out_shape=[shape(halfc, F32), shape(halfc, F32)],
        scratch_shapes=[
            scratch(total, 4 * rows, BF16),
            pltpu.VMEM((cells, 4 * rows, terms // 2), F32),
        ],
        compiler_params=params(6 + total // 32),
        cost_estimate=far_cost,
        name="far_target",
    )(idx, gathered, moment_all_pair, turned)
    target_other = swap_rank(target_send, 1)
    others[0], _ = lax.optimization_barrier((others[0], target_send))

    got_a, got_b, _ = lax.optimization_barrier((got_a, got_b, target_send))

    half = blks // 4 * stride
    keep, send = pl.pallas_call(
        functools.partial(meet_kernel, halfc),
        in_specs=[VMEM] * 4,
        out_specs=[VMEM] * 2,
        out_shape=[shape(half, F32), shape(half + scale_blocks(half), I16)],
        scratch_shapes=[scratch(half), scales(half_a), scales(half_b), scales(half), scales(half)],
        compiler_params=params(8 + total // 16),
        cost_estimate=meet_cost,
        name="meet",
    )(keep_a, got_a, keep_b, got_b)
    coded = swap_blk(send, reduce_order[-2])

    for bit in reversed(reduce_order[:-2]):
        now, half = half, half // 2
        keep, send = pl.pallas_call(
            add_kernel,
            in_specs=[VMEM] * 2,
            out_specs=[VMEM] * 2,
            out_shape=[shape(half, F32), shape(half + scale_blocks(half), I16)],
            scratch_shapes=[scratch(half), scales(now), scales(half), scales(half)],
            compiler_params=params(8 + total // 16),
            name="add",
        )(keep, coded)
        if bit != reduce_order[0]:
            coded = swap_blk(send, bit)

    first_keep, first_send = pl.pallas_call(
        functools.partial(near_first_kernel, stride, cells, starts),
        in_specs=[SMEM] + [VMEM] * (4 + len(others)),
        out_specs=[VMEM, VMEM],
        out_shape=[shape(cells, F32), shape(cells, F32)],
        scratch_shapes=[
            scratch(total, 2 * rows, BF16),
            scratch(cells, 2 * rows),
        ],
        compiler_params=params(4 + total // 32),
        cost_estimate=first_cost,
        name="near_first",
    )(idx, gathered, both, *others, near_tiles, other_tiles)
    first_send, send = lax.optimization_barrier((first_send, send))
    first_other = swap_rank(first_send, 2)
    coded = swap_blk(send, reduce_order[0])

    own_part = pl.pallas_call(
        self_kernel,
        in_specs=[VMEM] * 2,
        out_specs=VMEM,
        out_shape=shape(cells, F32),
        compiler_params=params(8),
        cost_estimate=meet_cost,
        name="self",
    )(charge_own, self_tiles)

    return pl.pallas_call(
        final_kernel,
        in_specs=[SMEM] + [VMEM] * 8,
        out_specs=VMEM,
        out_shape=jax.ShapeDtypeStruct(charges.shape, F32),
        scratch_shapes=[scales(stride)],
        compiler_params=params(8),
        name="final",
    )(
        counts, keep, coded, first_keep, first_other, target_keep, target_other, own_part, basis_t
    )


def solution(mesh):
    in_specs = (
        P("rhs", "blk"),
        P("blk"),
        P("blk", None, None),
        P("blk", None, None),
        P("blk"),
        P("blk"),
        P(("blk", "rhs"), None, None),
        P("blk"),
        P("blk"),
        P("blk", None, None),
    )
    out_specs = P("rhs", "blk")
    return jax.shard_map(body, mesh=mesh, in_specs=in_specs, out_specs=out_specs, check_vma=False)
```

```python
import functools

import jax
import jax.numpy as jnp
from jax import lax
from jax.experimental import pallas as pl
from jax.experimental.pallas import tpu as pltpu
from jax.sharding import PartitionSpec as P

F32, BF16, I16, I32 = jnp.float32, jnp.bfloat16, jnp.int16, jnp.int32
GROUP = 16
TOP = 32767.0
VMEM = pl.BlockSpec(memory_space=pltpu.VMEM)
SMEM = pl.BlockSpec(memory_space=pltpu.SMEM)
HBM = pl.BlockSpec(memory_space=pltpu.HBM)
NAT = (((1,), (0,)), ((), ()))
TRN = (((1,), (1,)), ((), ()))


def params(mib):
    return pltpu.CompilerParams(vmem_limit_bytes=mib << 20)


def in_hbm(x):
    return pltpu.with_memory_space_constraint(x, pltpu.HBM)


def dot(lhs, rhs, dims):
    return lax.dot_general(lhs, rhs, dims, preferred_element_type=F32)


def scale_blocks(count):
    return -(-count // GROUP)


def encode(get, out, outer, inner, peak, inv):
    count = outer * inner
    peak[...] = jnp.zeros_like(peak)

    def find(o, _):
        for i in range(inner):
            peak[pl.ds(o * inner + i, 1), :] = jnp.max(jnp.abs(get(o, i)), axis=0, keepdims=True)
        return 0

    lax.fori_loop(0, outer, find, 0)
    code = jnp.ceil(jnp.log2(jnp.maximum(peak[...], 1e-30)) * 8.0) + 1.0
    inv[...] = TOP * jnp.exp2(code * -0.125)
    for s in range(scale_blocks(count)):
        out[count + s] = code[s * GROUP : (s + 1) * GROUP].astype(I32).astype(I16)

    def put(o, _):
        for i in range(inner):
            b = o * inner + i
            out[b] = jnp.round(get(o, i) * inv[pl.ds(b, 1), :]).astype(I32).astype(I16)
        return 0

    lax.fori_loop(0, outer, put, 0)


def decode_scales(coded, count, scale):
    for s in range(scale_blocks(count)):
        code = coded[count + s].astype(I32).astype(F32)
        scale[s * GROUP : (s + 1) * GROUP, :] = jnp.exp2(code * 0.125) * (1.0 / TOP)


def decode(coded, scale, b):
    return coded[b].astype(I32).astype(F32) * scale[pl.ds(b, 1), :]


def prep_kernel(
    place, counts_in, charges_in, basis_in, near_first, near_second, far_source, far_target, tiles_in,
    out, idx, tiles, counts, charges, basis_t, lists, counts_row, sems,
):
    pairs = [(counts_in.at[0], counts), (charges_in, charges), (basis_in, basis_t), (counts_in, counts_row)]
    pairs += [
        (src, lists.at[pl.ds(i, 1)]) for i, src in enumerate((near_first, near_second, far_source, far_target))
    ]
    pairs += [(tiles_in.at[pl.ds(0, tiles.shape[0])], tiles)]
    copies = [pltpu.make_async_copy(src, dst, sems.at[i]) for i, (src, dst) in enumerate(pairs)]
    for copy in copies:
        copy.start()
    for copy in copies[:-1]:
        copy.wait()
    cells, terms, size = basis_t.shape
    rows = charges.shape[0]
    lane = lax.broadcasted_iota(I32, (rows, size), 1)
    moments = []
    for c in range(cells):
        x = charges[:, c * size : (c + 1) * size]
        x = jnp.where(lane < counts[c], x, jnp.zeros_like(x))
        out[c] = x
        moments.append(dot(x, basis_t[c], TRN))
    for k in range(cells // 2):
        out[cells + k] = jnp.concatenate(moments[2 * k : 2 * k + 2], axis=1).astype(BF16)
    first, second, source, target = (lists[i : i + 1, :] for i in range(4))
    for row, value in (
        (FIRST, lax.rem(first, cells)),
        (SECOND, place(second, 0)),
        (SECOND_REDUCE, place(second, 1)),
        (SOURCE, place(source, 0)),
        (SOURCE_REDUCE, place(source, 1)),
        (TARGET, lax.rem(target, cells)),
    ):
        idx[row : row + 1, :] = value
    idx[COUNT : COUNT + 1, :cells] = counts_row[...]
    copies[-1].wait()


FIRST, SECOND, SECOND_REDUCE, SOURCE, SOURCE_REDUCE, TARGET, COUNT = range(7)
PITCH = 136
FAR_UNROLL = 64
FAR_STEPS = 2
NEAR_UNROLL = 64
PARTS = 4


def far_source_kernel(idx, mine, theirs, tiles, turned, keep, *refs):
    *sends, flip, lhs, acc = refs
    rows, lanes = mine.shape[1:]
    half = lanes // 2
    pairs = half // 2
    total = turned.shape[0]
    chunk = total // FAR_STEPS
    acc[...] = jnp.zeros_like(acc)
    for k in range(mine.shape[0]):
        x, y = mine[k], theirs[k]
        for h in range(2):
            at = h * half
            lhs[2 * k + h] = jnp.concatenate([x[:, at : at + half], y[:, at : at + half]], axis=0)
    for step in range(FAR_STEPS):
        base = (lax.axis_index("rhs") & 1) * total + step * chunk
        span = pl.ds(pl.multiple_of(base, chunk), chunk)
        for i in range(pairs):
            both = [tiles[(i + h * pairs) * half : (i + h * pairs + 1) * half, span] for h in range(2)]
            flip[step, i * PITCH : i * PITCH + chunk, :] = jnp.concatenate(both, axis=0).astype(F32).T

        def work(g, _, step=step, base=base):
            sums = []
            at = g * FAR_UNROLL
            for u in range(FAR_UNROLL):
                w = flip[step, pl.ds(at + u, pairs, stride=PITCH), :]
                turned[step * chunk + at + u] = w.astype(BF16)
                moved = pltpu.roll(w, half, 1)
                w = jnp.concatenate([w[:, :half], moved[:, :half]], axis=0).astype(BF16)
                sums.append(dot(lhs[idx[TARGET, base + at + u]], w, NAT))
            for u in range(FAR_UNROLL):
                acc[idx[SOURCE_REDUCE, base + at + u]] += sums[u]
            return 0

        lax.fori_loop(0, chunk // FAR_UNROLL, work, 0)
    count = sends[0].shape[0]
    for q, send in enumerate(sends):

        def fold(k, _, q=q, send=send):
            for u in range(4):
                at = q * count + 4 * k + u
                both = jnp.concatenate([acc[2 * at], acc[2 * at + 1]], axis=1)
                keep[at] = both[:rows]
                send[4 * k + u] = both[rows:]
            return 0

        lax.fori_loop(0, count // 4, fold, 0)


def far_target_kernel(stride, cells, idx, everyone, theirs, turned, keep, send, lhs, acc):
    rows, lanes = everyone.shape[1], everyone.shape[2]
    half = lanes // 2
    chunk = turned.shape[0]
    owners = everyone.shape[0] // stride
    acc[...] = jnp.zeros_like(acc)
    low = lax.broadcasted_iota(I32, (2 * rows, lanes), 1) < half

    def spread(o, _):
        for k in range(cells // 2):
            x = jnp.concatenate([everyone[o * stride + cells + k], theirs[o * (cells // 2) + k]], axis=0)
            y = jnp.concatenate([x[:, half:], x[:, :half]], axis=1)
            zero = jnp.zeros_like(x)
            at = o * cells + 2 * k
            lhs[at] = jnp.concatenate([jnp.where(low, x, zero), jnp.where(low, zero, y)], axis=0)
            lhs[at + 1] = jnp.concatenate([jnp.where(low, y, zero), jnp.where(low, zero, x)], axis=0)
        return 0

    lax.fori_loop(0, owners, spread, 0)
    base = (lax.axis_index("rhs") & 1) * chunk

    def work(g, _):
        sums = []
        for u in range(FAR_UNROLL):
            e = g * FAR_UNROLL + u
            sums.append(dot(lhs[idx[SOURCE, base + e]], turned[e], TRN))
        for u in range(FAR_UNROLL):
            acc[idx[TARGET, base + g * FAR_UNROLL + u]] += sums[u]
        return 0

    lax.fori_loop(0, chunk // FAR_UNROLL, work, 0)
    for k in range(cells // 2):
        a, b = acc[2 * k], acc[2 * k + 1]
        for r, out in enumerate((keep, send)):
            at = (r * rows, (2 + r) * rows)
            out[k] = jnp.concatenate([x[i : i + rows] for x in (a, b) for i in at], axis=1)


def near_loop(idx, lhs, lhs_at, tiles, flip, first, pairs, dims, acc, acc_at):
    count = tiles.shape[0]
    base = (lax.axis_index("rhs") ^ flip) * pairs + first
    group = min(NEAR_UNROLL, count)
    for low in range(0, count, group):
        span = range(low, low + group)
        sums = [dot(lhs[idx[lhs_at, base + n]], tiles[n], dims) for n in span]
        for n in span:
            acc[idx[acc_at, base + n]] += sums[n - low]


def near_second_a_kernel(idx, mine, theirs, tiles, rest, acc, both, tiles_high, sem):
    rows, size = mine.shape[1:]

    half, pairs = tiles.shape[0], rest.shape[0]
    copy = pltpu.make_async_copy(rest.at[pl.ds(half, pairs - half)], tiles_high, sem)
    copy.start()
    acc[...] = jnp.zeros_like(acc)
    lane = lax.broadcasted_iota(I32, (rows, size), 1)
    for c in range(both.shape[0]):
        x = theirs[:, c * size : (c + 1) * size]
        x = jnp.where(lane < idx[COUNT, c], x, jnp.zeros_like(x))
        both[c] = jnp.concatenate([mine[c], x], axis=0)
    near_loop(idx, both, FIRST, tiles, 0, 0, pairs, NAT, acc, SECOND_REDUCE)
    copy.wait()
    near_loop(idx, both, FIRST, tiles_high, 0, half, pairs, NAT, acc, SECOND_REDUCE)


def near_second_b_kernel(
    cells, idx, both, other, before, acc, keep_a, send_a, keep_b, send_b, peak, inv
):
    rows = both.shape[1] // 2
    half = cells // 2
    owners = acc.shape[0] // cells
    stay = keep_b.shape[0] // half
    near_loop(idx, both, FIRST, other, 1, 0, other.shape[0], NAT, acc, SECOND_REDUCE)
    encode(lambda o, c: acc[o * cells + c, rows:, :], send_a, owners, half, peak, inv)

    def part_b(o, i):
        return acc[(stay + o) * cells + half + i // 2, i % 2 * rows : (i % 2 + 1) * rows, :]

    encode(part_b, send_b, owners - stay, 2 * half, peak, inv)

    def own_a(o, _):
        for c in range(half):
            keep_a[o * half + c] = acc[o * cells + c, :rows, :]
        return 0

    def own_b(o, _):
        for c in range(half):
            keep_b[o * half + c] = acc[o * cells + half + c]
        return 0

    lax.fori_loop(0, owners, own_a, 0)
    lax.fori_loop(0, stay, own_b, 0)


def near_first_kernel(stride, cells, starts, idx, everyone, both, *refs):
    *parts, tiles, tiles_high, other, keep, send, lhs, acc = refs
    rows = everyone.shape[1]

    acc[...] = jnp.zeros_like(acc)
    lhs[:cells] = both[...]
    for start, part in zip(starts, parts):
        count = part.shape[0] // cells

        def fill(o, _, part=part, start=start):
            for c in range(cells):
                at = start + o
                lhs[at * cells + c] = jnp.concatenate([everyone[at * stride + c], part[o * cells + c]], axis=0)
            return 0

        lax.fori_loop(0, count, fill, 0)
    pairs = other.shape[0]
    near_loop(idx, lhs, SECOND, tiles, 0, 0, pairs, TRN, acc, FIRST)
    near_loop(idx, lhs, SECOND, tiles_high, 0, tiles.shape[0], pairs, TRN, acc, FIRST)
    near_loop(idx, lhs, SECOND, other, 1, 0, pairs, TRN, acc, FIRST)
    for c in range(cells):
        keep[c] = acc[c, :rows, :]
        send[c] = acc[c, rows:, :]


def join_kernel(mine, coded, out, scale):
    count = out.shape[0]
    decode_scales(coded, count, scale)

    def one(o, _):
        for i in range(8):
            b = o * 8 + i
            out[b] = mine[b] + decode(coded, scale, b)
        return 0

    lax.fori_loop(0, count // 8, one, 0)


def meet_a_kernel(half, mine, far, *refs):
    *far_others, keep, send, acc, peak, inv = refs
    count = far_others[0].shape[0]
    owners = far.shape[0] // half
    stay = owners // 2
    for p in range(owners):
        dst, at = (keep, p) if p < stay else (acc, p - stay)
        for c in range(half):
            b = p * half + c
            dst[at * 2 * half + c] = mine[b]
            dst[at * 2 * half + half + c] = far[b] + far_others[b // count][b % count]
    encode(lambda o, i: acc[o * 8 + i], send, acc.shape[0] // 8, 8, peak, inv)


def meet_b_kernel(half, mine, coded, keep, send, acc, scale, peak, inv):
    rows = keep.shape[1]
    owners = keep.shape[0] // half
    decode_scales(coded, 2 * keep.shape[0], scale)
    for p in range(owners):
        for c in range(half):
            b = p * half + c
            keep[b] = mine[b, :rows, :] + decode(coded, scale, 2 * b)
            acc[b] = mine[b, rows:, :] + decode(coded, scale, 2 * b + 1)
    encode(lambda o, i: acc[o * 8 + i], send, acc.shape[0] // 8, 8, peak, inv)


def meet_kernel(half, mine_a, coded_a, mine_b, coded_b, keep, send, acc, scale_a, scale_b, peak, inv):
    owners = mine_b.shape[0] // half
    stay = owners // 2
    decode_scales(coded_a, mine_a.shape[0], scale_a)
    decode_scales(coded_b, mine_b.shape[0], scale_b)
    for p in range(owners):
        dst, at = (keep, p * 3) if p < stay else (acc, (p - stay) * 3)
        for c in range(half):
            a, b = p * 2 * half + c, p * half + c
            dst[at * half + c] = mine_a[a] + decode(coded_a, scale_a, a)
            dst[(at + 1) * half + c] = mine_b[b] + decode(coded_b, scale_b, b)
            a = a + half
            dst[(at + 2) * half + c] = mine_a[a] + decode(coded_a, scale_a, a)
    encode(lambda o, i: acc[o * 8 + i], send, acc.shape[0] // 8, 8, peak, inv)


def add_kernel(mine, coded, keep, send, acc, scale, peak, inv):
    total = mine.shape[0]
    half = total // 2
    decode_scales(coded, total, scale)

    def one(b, _):
        keep[b] = mine[b] + decode(coded, scale, b)
        acc[b] = mine[half + b] + decode(coded, scale, half + b)
        return 0

    lax.fori_loop(0, half, one, 0, unroll=8)
    encode(lambda o, i: acc[o * 8 + i], send, half // 8, 8, peak, inv)


def self_kernel(moved, self_tiles, out):
    for c in range(out.shape[0]):
        out[c] = dot(moved[c], self_tiles[c], TRN)


def final_kernel(
    counts, mine, coded, first, first_other, target, target_other, own, basis_t, out, scale
):
    cells, terms, size = basis_t.shape
    rows = out.shape[0]
    decode_scales(coded, mine.shape[0], scale)
    lane = lax.broadcasted_iota(I32, (rows, size), 1)
    for k in range(cells // 2):
        b = cells + k
        fields = (mine[b] + decode(coded, scale, b) + target[k] + target_other[k]).astype(BF16)
        for h in range(2):
            c = 2 * k + h
            near = mine[c] + decode(coded, scale, c) + first[c] + first_other[c]
            far = dot(fields[:, h * terms : (h + 1) * terms], basis_t[c], NAT)
            total = near + far + own[c]
            out[:, c * size : (c + 1) * size] = jnp.where(lane < counts[c], total, jnp.zeros_like(total))


def body(
    charges,
    counts,
    self_tiles,
    basis,
    near_first,
    near_second,
    near_tiles,
    far_source,
    far_target,
    far_tiles,
):
    blks = lax.axis_size("blk")
    ranks = lax.axis_size("rhs")
    me = lax.axis_index("blk")
    rank = lax.axis_index("rhs")
    cells, size, _ = self_tiles.shape
    terms = basis.shape[2]
    rows = charges.shape[0]
    pairs = near_tiles.shape[0]
    fars = far_tiles.shape[0]
    bits = blks.bit_length() - 1
    gather_order = [0, *range(bits - 1, 0, -1)]
    reduce_order = [*range(bits - 1, -1, -1)]
    halfc = cells // 2
    stride = cells + halfc
    total = blks * cells

    def swap_rank(x, d):
        return lax.ppermute(x, "rhs", [(i, i ^ d) for i in range(ranks)])

    def swap_blk(x, bit):
        return lax.ppermute(x, "blk", [(i, i ^ (1 << bit)) for i in range(blks)])

    def place(block, reduce):
        other = lax.div(block, cells) ^ lax.axis_index("blk")
        order = reduce_order if reduce else gather_order
        at = sum(((other >> bit) & 1) << s for s, bit in enumerate(order))
        return at * cells + lax.rem(block, cells)

    def shape(n, dtype, r=rows):
        return jax.ShapeDtypeStruct((n, r, size), dtype)

    def scratch(n, r=rows, dtype=F32):
        return pltpu.VMEM((n, r, size), dtype)

    def scales(n):
        return pltpu.VMEM((scale_blocks(n) * GROUP, size), F32)

    def whole(n, r=rows):
        return pl.BlockSpec((n, r, size), lambda i, *_: (0, 0, 0))

    def owners(x, low, high, begin, end):
        return x.reshape(-1, stride, rows, size)[low:high, begin:end].reshape(-1, rows, size)

    other_tiles = swap_rank(near_tiles, 1)
    charge_other = swap_rank(charges, 2)
    basis_t = jnp.swapaxes(basis, 1, 2)

    width = max(near_first.shape[0], fars)
    lists = [x.reshape(1, -1) for x in (near_first, near_second, far_source, far_target)]
    own, idx, tiles_low = pl.pallas_call(
        functools.partial(prep_kernel, place),
        in_specs=[HBM] * 8,
        out_specs=[VMEM] * 3,
        out_shape=[
            shape(stride, BF16),
            jax.ShapeDtypeStruct((7, width), I32),
            shape(pairs // 2, BF16, size),
        ],
        scratch_shapes=[
            pltpu.SMEM(counts.shape, I32),
            pltpu.VMEM(charges.shape, BF16),
            pltpu.VMEM(basis_t.shape, BF16),
            pltpu.VMEM((4, width), I32),
            pltpu.VMEM((1, cells), I32),
            pltpu.SemaphoreType.DMA((9,)),
        ],
        compiler_params=params(8),
        cost_estimate=pl.CostEstimate(flops=0, bytes_accessed=12 << 20, transcendentals=0),
        name="prep",
    )(*[in_hbm(x) for x in (counts.reshape(1, -1), charges, basis_t, *lists, near_tiles)])
    charge_own = own[:cells]
    moment_own = own[cells:]
    moment_pair = swap_rank(moment_own, 1)

    far_cost = pl.CostEstimate(flops=2 * fars * rows * terms * terms, bytes_accessed=12 << 20, transcendentals=0)
    tiles_ij = jnp.transpose(far_tiles, (1, 2, 0)).reshape(terms * terms, fars)
    near_cost = pl.CostEstimate(flops=4 * pairs * rows * size * size, bytes_accessed=10 << 20, transcendentals=0)
    first_cost = pl.CostEstimate(flops=8 * pairs * rows * size * size, bytes_accessed=20 << 20, transcendentals=0)
    coded_a = total // 2
    coded_b = blks // 2 * cells
    stay = blks // 2
    near_acc = shape(total, F32, 2 * rows)
    near_sum, both, tiles_high = pl.pallas_call(
        near_second_a_kernel,
        in_specs=[SMEM, VMEM, VMEM, VMEM, HBM],
        out_specs=[VMEM] * 3,
        out_shape=[near_acc, shape(cells, BF16, 2 * rows), shape(pairs - pairs // 2, BF16, size)],
        scratch_shapes=[pltpu.SemaphoreType.DMA],
        compiler_params=params(4),
        cost_estimate=near_cost,
        name="near_second_a",
    )(idx, charge_own, charge_other, tiles_low, in_hbm(near_tiles))

    received = swap_blk(own, gather_order[0])
    received, near_sum = lax.optimization_barrier((received, near_sum))
    gathered = jnp.concatenate([own, received], axis=0)
    received = swap_blk(gathered, gather_order[1])
    near_sum, _ = lax.optimization_barrier((near_sum, gathered))

    _, keep_a, send_a, keep_b, send_b = pl.pallas_call(
        functools.partial(near_second_b_kernel, cells),
        in_specs=[SMEM, VMEM, VMEM, VMEM],
        out_specs=[VMEM] * 5,
        out_shape=[
            near_acc,
            shape(coded_a, F32),
            shape(coded_a + scale_blocks(coded_a), I16),
            shape(stay * halfc, F32, 2 * rows),
            shape(coded_b + scale_blocks(coded_b), I16),
        ],
        scratch_shapes=[
            scales(max(coded_a, coded_b)),
            scales(max(coded_a, coded_b)),
        ],
        input_output_aliases={3: 0},
        compiler_params=params(8),
        cost_estimate=near_cost,
        name="near_second_b",
    )(idx, both, other_tiles, near_sum)
    moment_late, _ = lax.optimization_barrier((moment_pair, send_a))
    turned, far_keep, *far_sends = pl.pallas_call(
        far_source_kernel,
        in_specs=[SMEM] + [VMEM] * 3,
        out_specs=[VMEM] * (2 + PARTS),
        out_shape=[
            shape(fars // 2, BF16, terms // 2),
            shape(total // 2, F32),
            *[shape(total // 2 // PARTS, F32)] * PARTS,
        ],
        scratch_shapes=[
            pltpu.VMEM((FAR_STEPS, terms // 2 * PITCH, size), F32),
            pltpu.VMEM((cells, 2 * rows, terms), BF16),
            pltpu.VMEM((total, 2 * rows, terms), F32),
        ],
        compiler_params=params(8 + total // 32),
        cost_estimate=far_cost,
        name="far_source",
    )(idx, moment_own, moment_late, tiles_ij)
    received, turned = lax.optimization_barrier((received, turned))
    others, starts = [], []
    for s, bit in enumerate(gather_order):
        if s > 1:
            received = swap_blk(gathered, bit)
        if 0 < s < bits - 1:
            gathered = jnp.concatenate([gathered, received], axis=0)
    starts.append(1)
    others.append(swap_rank(owners(gathered, 1, blks // 2, 0, cells), 2))
    far_others = [swap_rank(x, 1) for x in far_sends]

    got_a = swap_rank(send_a, 2)
    got_b = swap_blk(send_b, reduce_order[-1])
    got_b, got_a = lax.optimization_barrier((got_b, got_a))
    half_a = blks // 2 * cells
    half_b = blks // 2 * halfc
    meet_cost = pl.CostEstimate(flops=0, bytes_accessed=1 << 20, transcendentals=0)
    keep_b, send_b = pl.pallas_call(
        functools.partial(meet_b_kernel, halfc),
        in_specs=[VMEM] * 2,
        out_specs=[VMEM] * 2,
        out_shape=[shape(half_b, F32), shape(half_b + scale_blocks(half_b), I16)],
        scratch_shapes=[scratch(half_b), scales(coded_b), scales(half_b), scales(half_b)],
        compiler_params=params(8 + total // 16),
        cost_estimate=meet_cost,
        name="meet_b",
    )(keep_b, got_b)
    keep_a, send_b = lax.optimization_barrier((keep_a, send_b))
    got_b = swap_rank(send_b, 2)
    received, others[0], got_b = lax.optimization_barrier((received, others[0], got_b))
    gathered = jnp.concatenate([gathered, received], axis=0)
    starts.append(blks // 2)
    others.append(swap_rank(owners(received, 0, blks // 2, 0, cells), 2))
    joined = pl.pallas_call(
        join_kernel,
        in_specs=[VMEM] * 2,
        out_specs=VMEM,
        out_shape=shape(coded_a, F32),
        scratch_shapes=[scales(coded_a)],
        compiler_params=params(8),
        cost_estimate=pl.CostEstimate(flops=0, bytes_accessed=3 << 20, transcendentals=0),
        name="join",
    )(keep_a, got_a)
    keep_a, send_a = pl.pallas_call(
        functools.partial(meet_a_kernel, halfc),
        in_specs=[VMEM] * (2 + PARTS),
        out_specs=[VMEM] * 2,
        out_shape=[shape(half_a, F32), shape(half_a + scale_blocks(half_a), I16)],
        scratch_shapes=[scratch(half_a), scales(half_a), scales(half_a)],
        compiler_params=params(8 + total // 16),
        cost_estimate=meet_cost,
        name="meet_a",
    )(joined, far_keep, *far_others)
    got_a = swap_blk(send_a, reduce_order[-1])

    moment_all_pair = swap_rank(owners(gathered, 0, blks, cells, stride), 1)
    target_keep, target_send = pl.pallas_call(
        functools.partial(far_target_kernel, stride, cells),
        in_specs=[SMEM] + [VMEM] * 3,
        out_specs=[VMEM] * 2,
        out_shape=[shape(halfc, F32), shape(halfc, F32)],
        scratch_shapes=[
            scratch(total, 4 * rows, BF16),
            pltpu.VMEM((cells, 4 * rows, terms // 2), F32),
        ],
        compiler_params=params(6 + total // 32),
        cost_estimate=meet_cost,
        name="far_target",
    )(idx, gathered, moment_all_pair, turned)
    target_other = swap_rank(target_send, 1)
    others[0], _ = lax.optimization_barrier((others[0], target_send))

    got_a, got_b, _ = lax.optimization_barrier((got_a, got_b, target_send))

    half = blks // 4 * stride
    keep, send = pl.pallas_call(
        functools.partial(meet_kernel, halfc),
        in_specs=[VMEM] * 4,
        out_specs=[VMEM] * 2,
        out_shape=[shape(half, F32), shape(half + scale_blocks(half), I16)],
        scratch_shapes=[scratch(half), scales(half_a), scales(half_b), scales(half), scales(half)],
        compiler_params=params(8 + total // 16),
        cost_estimate=meet_cost,
        name="meet",
    )(keep_a, got_a, keep_b, got_b)
    coded = swap_blk(send, reduce_order[-2])

    for bit in reversed(reduce_order[:-2]):
        now, half = half, half // 2
        keep, send = pl.pallas_call(
            add_kernel,
            in_specs=[VMEM] * 2,
            out_specs=[VMEM] * 2,
            out_shape=[shape(half, F32), shape(half + scale_blocks(half), I16)],
            scratch_shapes=[scratch(half), scales(now), scales(half), scales(half)],
            compiler_params=params(8 + total // 16),
            name="add",
        )(keep, coded)
        if bit != reduce_order[0]:
            coded = swap_blk(send, bit)

    first_keep, first_send = pl.pallas_call(
        functools.partial(near_first_kernel, stride, cells, starts),
        in_specs=[SMEM] + [VMEM] * (5 + len(others)),
        out_specs=[VMEM, VMEM],
        out_shape=[shape(cells, F32), shape(cells, F32)],
        scratch_shapes=[
            scratch(total, 2 * rows, BF16),
            scratch(cells, 2 * rows),
        ],
        compiler_params=params(4 + total // 32),
        cost_estimate=first_cost,
        name="near_first",
    )(idx, gathered, both, *others, tiles_low, tiles_high, other_tiles)
    first_send, send = lax.optimization_barrier((first_send, send))
    first_other = swap_rank(first_send, 2)
    coded = swap_blk(send, reduce_order[0])

    own_part = pl.pallas_call(
        self_kernel,
        in_specs=[VMEM] * 2,
        out_specs=VMEM,
        out_shape=shape(cells, F32),
        compiler_params=params(8),
        cost_estimate=meet_cost,
        name="self",
    )(charge_own, self_tiles)

    return pl.pallas_call(
        final_kernel,
        in_specs=[SMEM] + [VMEM] * 8,
        out_specs=VMEM,
        out_shape=jax.ShapeDtypeStruct(charges.shape, F32),
        scratch_shapes=[scales(stride)],
        compiler_params=params(8),
        name="final",
    )(
        counts, keep, coded, first_keep, first_other, target_keep, target_other, own_part, basis_t
    )


def solution(mesh):
    in_specs = (
        P("rhs", "blk"),
        P("blk"),
        P("blk", None, None),
        P("blk", None, None),
        P("blk"),
        P("blk"),
        P(("blk", "rhs"), None, None),
        P("blk"),
        P("blk"),
        P("blk", None, None),
    )
    out_specs = P("rhs", "blk")
    return jax.shard_map(body, mesh=mesh, in_specs=in_specs, out_specs=out_specs, check_vma=False)
```

```python
import functools

import jax
import jax.numpy as jnp
from jax import lax
from jax.experimental import pallas as pl
from jax.experimental.pallas import tpu as pltpu
from jax.sharding import PartitionSpec as P

F32, BF16, I16, I32 = jnp.float32, jnp.bfloat16, jnp.int16, jnp.int32
REACH = 48
GROUP = 16
TOP = 32767.0
VMEM = pl.BlockSpec(memory_space=pltpu.VMEM)
SMEM = pl.BlockSpec(memory_space=pltpu.SMEM)
HBM = pl.BlockSpec(memory_space=pltpu.HBM)
NAT = (((1,), (0,)), ((), ()))
TRN = (((1,), (1,)), ((), ()))


def params(mib):
    return pltpu.CompilerParams(vmem_limit_bytes=mib << 20)


def in_hbm(x):
    return pltpu.with_memory_space_constraint(x, pltpu.HBM)


def dot(lhs, rhs, dims):
    return lax.dot_general(lhs, rhs, dims, preferred_element_type=F32)


def scale_blocks(count):
    return -(-count // GROUP)


def encode(get, out, outer, inner, peak, inv):
    count = outer * inner
    peak[...] = jnp.zeros_like(peak)

    def find(o, _):
        for i in range(inner):
            peak[pl.ds(o * inner + i, 1), :] = jnp.max(jnp.abs(get(o, i)), axis=0, keepdims=True)
        return 0

    lax.fori_loop(0, outer, find, 0)
    code = jnp.ceil(jnp.log2(jnp.maximum(peak[...], 1e-30)) * 8.0) + 1.0
    inv[...] = TOP * jnp.exp2(code * -0.125)
    for s in range(scale_blocks(count)):
        out[count + s] = code[s * GROUP : (s + 1) * GROUP].astype(I32).astype(I16)

    def put(o, _):
        for i in range(inner):
            b = o * inner + i
            out[b] = jnp.round(get(o, i) * inv[pl.ds(b, 1), :]).astype(I32).astype(I16)
        return 0

    lax.fori_loop(0, outer, put, 0)


def decode_scales(coded, count, scale):
    for s in range(scale_blocks(count)):
        code = coded[count + s].astype(I32).astype(F32)
        scale[s * GROUP : (s + 1) * GROUP, :] = jnp.exp2(code * 0.125) * (1.0 / TOP)


def decode(coded, scale, b):
    return coded[b].astype(I32).astype(F32) * scale[pl.ds(b, 1), :]


def prep_kernel(
    place, counts_in, charges_in, basis_in, near_first, near_second, far_source, far_target, tiles_in,
    out, at_second, at_first, at_source, at_target, tiles, near_zero, counts, charges, basis_t, lists, counts_row, sems,
):
    moves = [(counts_in.at[0], counts), (charges_in, charges), (basis_in, basis_t), (counts_in, counts_row)]
    moves += [
        (src, lists.at[pl.ds(i, 1)]) for i, src in enumerate((near_first, near_second, far_source, far_target))
    ]
    moves += [(tiles_in.at[pl.ds(0, tiles.shape[0])], tiles)]
    copies = [pltpu.make_async_copy(src, dst, sems.at[i]) for i, (src, dst) in enumerate(moves)]
    for copy in copies:
        copy.start()
    for copy in copies[:-1]:
        copy.wait()
    cells, terms, size = basis_t.shape
    rows = charges.shape[0]
    lane = lax.broadcasted_iota(I32, (rows, size), 1)
    moments = []
    for c in range(cells):
        x = charges[:, c * size : (c + 1) * size]
        x = jnp.where(lane < counts[c], x, jnp.zeros_like(x))
        out[c] = x
        moments.append(dot(x, basis_t[c], TRN))
    for k in range(cells // 2):
        out[cells + k] = jnp.concatenate(moments[2 * k : 2 * k + 2], axis=1).astype(BF16)
    rank = lax.axis_index("rhs")
    pairs = tiles_in.shape[0]
    for flip in range(2):
        span = pl.ds(pl.multiple_of((rank ^ flip) * pairs, pairs), pairs)
        to = slice(flip * pairs, (flip + 1) * pairs)
        first, second = lists[0:1, span], lists[1:2, span]
        for at in (at_second, at_first):
            at[0:1, to] = lax.rem(first, cells)
        at_second[1:2, to] = place(second, 1)
        at_first[1:2, to] = place(second, 0)
    at_second[2:3, :cells] = counts_row[...]
    half = lists.shape[1] // 2
    span = pl.ds(pl.multiple_of((rank & 1) * half, half), half)
    source, target = lists[2:3, span], lists[3:4, span]
    for at, reduce in ((at_source, 1), (at_target, 0)):
        at[0:1, :] = lax.rem(target, cells)
        at[1:2, :] = place(source, reduce)
    near_zero[...] = jnp.zeros_like(near_zero)
    copies[-1].wait()


PITCH = 136
FAR_UNROLL = 64
NEAR_UNROLL = 64
PARTS = 4


def far_sources(step, idx, mine, theirs, tiles, turned, acc, flip, lhs):
    half = mine.shape[2] // 2
    pairs = half // 2
    chunk = turned.shape[0]
    for k in range(mine.shape[0]):
        x, y = mine[k], theirs[k]
        for h in range(2):
            at = h * half
            lhs[2 * k + h] = jnp.concatenate([x[:, at : at + half], y[:, at : at + half]], axis=0)
    span = pl.ds(pl.multiple_of((lax.axis_index("rhs") & 1) * 2 * chunk + step * chunk, chunk), chunk)
    for i in range(pairs):
        both = [tiles[(i + h * pairs) * half : (i + h * pairs + 1) * half, span] for h in range(2)]
        flip[i * PITCH : i * PITCH + chunk, :] = jnp.concatenate(both, axis=0).astype(F32).T

    def work(g, _):
        sums = []
        at = g * FAR_UNROLL
        for u in range(FAR_UNROLL):
            w = flip[pl.ds(at + u, pairs, stride=PITCH), :]
            turned[at + u] = w.astype(BF16)
            moved = pltpu.roll(w, half, 1)
            w = jnp.concatenate([w[:, :half], moved[:, :half]], axis=0).astype(BF16)
            sums.append(dot(lhs[idx[0, step * chunk + at + u]], w, NAT))
        for u in range(FAR_UNROLL):
            acc[idx[1, step * chunk + at + u]] += sums[u]
        return 0

    lax.fori_loop(0, chunk // FAR_UNROLL, work, 0)


def far_source_a_kernel(idx, mine, theirs, tiles, turned, acc, flip, lhs):
    acc[...] = jnp.zeros_like(acc)
    far_sources(0, idx, mine, theirs, tiles, turned, acc, flip, lhs)


def far_source_b_kernel(idx, mine, theirs, tiles, before, turned, acc, keep, *refs):
    *sends, flip, lhs = refs
    rows = mine.shape[1]
    far_sources(1, idx, mine, theirs, tiles, turned, acc, flip, lhs)
    count = sends[0].shape[0]
    for q, send in enumerate(sends):

        def fold(k, _, q=q, send=send):
            for u in range(4):
                at = q * count + 4 * k + u
                both = jnp.concatenate([acc[2 * at], acc[2 * at + 1]], axis=1)
                keep[at] = both[:rows]
                send[4 * k + u] = both[rows:]
            return 0

        lax.fori_loop(0, count // 4, fold, 0)


def far_target_kernel(stride, cells, idx, everyone, theirs, turned_a, turned_b, keep, send, lhs, acc):
    rows, lanes = everyone.shape[1], everyone.shape[2]
    half = lanes // 2
    chunk = turned_a.shape[0]
    owners = everyone.shape[0] // stride
    acc[...] = jnp.zeros_like(acc)
    low = lax.broadcasted_iota(I32, (2 * rows, lanes), 1) < half

    def spread(o, _):
        for k in range(cells // 2):
            x = jnp.concatenate([everyone[o * stride + cells + k], theirs[o * (cells // 2) + k]], axis=0)
            y = jnp.concatenate([x[:, half:], x[:, :half]], axis=1)
            zero = jnp.zeros_like(x)
            at = o * cells + 2 * k
            lhs[at] = jnp.concatenate([jnp.where(low, x, zero), jnp.where(low, zero, y)], axis=0)
            lhs[at + 1] = jnp.concatenate([jnp.where(low, y, zero), jnp.where(low, zero, x)], axis=0)
        return 0

    lax.fori_loop(0, owners, spread, 0)
    for step, turned in enumerate((turned_a, turned_b)):

        def work(g, _, base=step * chunk, turned=turned):
            sums = []
            for u in range(FAR_UNROLL):
                e = g * FAR_UNROLL + u
                sums.append(dot(lhs[idx[1, base + e]], turned[e], TRN))
            for u in range(FAR_UNROLL):
                acc[idx[0, base + g * FAR_UNROLL + u]] += sums[u]
            return 0

        lax.fori_loop(0, chunk // FAR_UNROLL, work, 0)
    for k in range(cells // 2):
        a, b = acc[2 * k], acc[2 * k + 1]
        for r, out in enumerate((keep, send)):
            at = (r * rows, (2 + r) * rows)
            out[k] = jnp.concatenate([x[i : i + rows] for x in (a, b) for i in at], axis=1)


def near_loop(idx, lhs, lhs_at, tiles, first, dims, acc, acc_at):
    count = tiles.shape[0]
    group = min(NEAR_UNROLL, count)
    for low in range(0, count, group):
        span = range(low, min(low + group, count))
        sums = [dot(lhs[idx[lhs_at, first + n]], tiles[n], dims) for n in span]
        for n in span:
            acc[idx[acc_at, first + n]] += sums[n - low]


def near_second_a_kernel(idx, mine, theirs, tiles, rest, zero, acc, both, tiles_high, sem):
    rows, size = mine.shape[1:]

    half, pairs = tiles.shape[0], rest.shape[0]
    copy = pltpu.make_async_copy(rest.at[pl.ds(half, pairs - half)], tiles_high, sem)
    copy.start()
    lane = lax.broadcasted_iota(I32, (rows, size), 1)
    for c in range(both.shape[0]):
        x = theirs[:, c * size : (c + 1) * size]
        x = jnp.where(lane < idx[2, c], x, jnp.zeros_like(x))
        both[c] = jnp.concatenate([mine[c], x], axis=0)
    near_loop(idx, both, 0, tiles, 0, NAT, acc, 1)
    copy.wait()
    near_loop(idx, both, 0, tiles_high, half, NAT, acc, 1)


def near_second_b_kernel(
    cells, idx, both, other, before, acc, keep_a, send_a, keep_b, send_b, peak, inv
):
    rows = both.shape[1] // 2
    half = cells // 2
    owners = acc.shape[0] // cells
    stay = keep_b.shape[0] // half
    near_loop(idx, both, 0, other, other.shape[0], NAT, acc, 1)
    encode(lambda o, c: acc[o * cells + c, rows:, :], send_a, owners, half, peak, inv)

    def part_b(o, i):
        return acc[(stay + o) * cells + half + i // 2, i % 2 * rows : (i % 2 + 1) * rows, :]

    encode(part_b, send_b, owners - stay, 2 * half, peak, inv)

    def own_a(o, _):
        for c in range(half):
            keep_a[o * half + c] = acc[o * cells + c, :rows, :]
        return 0

    def own_b(o, _):
        for c in range(half):
            keep_b[o * half + c] = acc[o * cells + half + c]
        return 0

    lax.fori_loop(0, owners, own_a, 0)
    lax.fori_loop(0, stay, own_b, 0)


def near_first_kernel(stride, cells, places, idx, everyone, both, *refs):
    *parts, tiles, tiles_high, other, keep, send, lhs, acc, peak, inv = refs
    rows = everyone.shape[1]

    acc[...] = jnp.zeros_like(acc)
    lhs[:cells] = both[...]
    for part, at in zip(parts, places):
        for i, p in enumerate(at):
            for c in range(cells):
                lhs[p * cells + c] = jnp.concatenate([everyone[p * stride + c], part[i * cells + c]], axis=0)
    near_loop(idx, lhs, 1, tiles, 0, TRN, acc, 0)
    near_loop(idx, lhs, 1, tiles_high, tiles.shape[0], TRN, acc, 0)
    near_loop(idx, lhs, 1, other, other.shape[0], TRN, acc, 0)
    for c in range(cells):
        keep[c] = acc[c, :rows, :]
    encode(lambda o, c: acc[c, rows:, :], send, 1, cells, peak, inv)


def join_kernel(mine, coded, out, scale):
    count = out.shape[0]
    decode_scales(coded, count, scale)

    def one(o, _):
        for i in range(8):
            b = o * 8 + i
            out[b] = mine[b] + decode(coded, scale, b)
        return 0

    lax.fori_loop(0, count // 8, one, 0)


def meet_a_kernel(half, mine, far, *refs):
    *far_others, keep, send, acc, peak, inv = refs
    count = far_others[0].shape[0]
    owners = far.shape[0] // half
    stay = owners // 2
    for p in range(owners):
        dst, at = (keep, p) if p < stay else (acc, p - stay)
        for c in range(half):
            b = p * half + c
            dst[at * 2 * half + c] = mine[b]
            dst[at * 2 * half + half + c] = far[b] + far_others[b // count][b % count]
    encode(lambda o, i: acc[o * 8 + i], send, acc.shape[0] // 8, 8, peak, inv)


def meet_b_kernel(half, mine, coded, keep, send, acc, scale, peak, inv):
    rows = keep.shape[1]
    owners = keep.shape[0] // half
    decode_scales(coded, 2 * keep.shape[0], scale)
    for p in range(owners):
        for c in range(half):
            b = p * half + c
            keep[b] = mine[b, :rows, :] + decode(coded, scale, 2 * b)
            acc[b] = mine[b, rows:, :] + decode(coded, scale, 2 * b + 1)
    encode(lambda o, i: acc[o * 8 + i], send, acc.shape[0] // 8, 8, peak, inv)


def meet_kernel(half, mine_a, coded_a, mine_b, coded_b, keep, send, acc, scale_a, scale_b, peak, inv):
    owners = mine_b.shape[0] // half
    stay = owners // 2
    decode_scales(coded_a, mine_a.shape[0], scale_a)
    decode_scales(coded_b, mine_b.shape[0], scale_b)
    for p in range(owners):
        dst, at = (keep, p * 3) if p < stay else (acc, (p - stay) * 3)
        for c in range(half):
            a, b = p * 2 * half + c, p * half + c
            dst[at * half + c] = mine_a[a] + decode(coded_a, scale_a, a)
            dst[(at + 1) * half + c] = mine_b[b] + decode(coded_b, scale_b, b)
            a = a + half
            dst[(at + 2) * half + c] = mine_a[a] + decode(coded_a, scale_a, a)
    encode(lambda o, i: acc[o * 8 + i], send, acc.shape[0] // 8, 8, peak, inv)


def add_kernel(mine, coded, keep, send, acc, scale, peak, inv):
    total = mine.shape[0]
    half = total // 2
    decode_scales(coded, total, scale)

    def one(b, _):
        keep[b] = mine[b] + decode(coded, scale, b)
        acc[b] = mine[half + b] + decode(coded, scale, half + b)
        return 0

    lax.fori_loop(0, half, one, 0, unroll=8)
    encode(lambda o, i: acc[o * 8 + i], send, half // 8, 8, peak, inv)


def self_kernel(moved, self_tiles, out):
    for c in range(out.shape[0]):
        out[c] = dot(moved[c], self_tiles[c], TRN)


def final_kernel(
    counts, mine, coded, first, first_other, target, target_other, own, basis_t, out, scale, first_scale
):
    cells, terms, size = basis_t.shape
    rows = out.shape[0]
    decode_scales(coded, mine.shape[0], scale)
    decode_scales(first_other, cells, first_scale)
    lane = lax.broadcasted_iota(I32, (rows, size), 1)
    for k in range(cells // 2):
        b = cells + k
        fields = (mine[b] + decode(coded, scale, b) + target[k] + target_other[k]).astype(BF16)
        for h in range(2):
            c = 2 * k + h
            near = mine[c] + decode(coded, scale, c) + first[c] + decode(first_other, first_scale, c)
            far = dot(fields[:, h * terms : (h + 1) * terms], basis_t[c], NAT)
            total = near + far + own[c]
            out[:, c * size : (c + 1) * size] = jnp.where(lane < counts[c], total, jnp.zeros_like(total))


def body(
    charges,
    counts,
    self_tiles,
    basis,
    near_first,
    near_second,
    near_tiles,
    far_source,
    far_target,
    far_tiles,
):
    blks = lax.axis_size("blk")
    ranks = lax.axis_size("rhs")
    me = lax.axis_index("blk")
    rank = lax.axis_index("rhs")
    cells, size, _ = self_tiles.shape
    terms = basis.shape[2]
    rows = charges.shape[0]
    pairs = near_tiles.shape[0]
    fars = far_tiles.shape[0]
    bits = blks.bit_length() - 1
    gather_order = [0, *range(bits - 1, 0, -1)]
    reduce_order = [*range(bits - 1, -1, -1)]
    halfc = cells // 2
    stride = cells + halfc
    total = blks * cells

    def reached(at):
        mask = sum(((at >> s) & 1) << bit for s, bit in enumerate(gather_order))
        gaps = [(o ^ mask) - o for o in range(blks)]
        return min(min(g % blks, -g % blks) for g in gaps) <= -(-REACH // cells)

    early = [at for at in range(1, blks // 2) if reached(at)]
    late = [at for at in range(blks // 2, blks) if reached(at)]

    def swap_rank(x, d):
        return lax.ppermute(x, "rhs", [(i, i ^ d) for i in range(ranks)])

    def swap_blk(x, bit):
        return lax.ppermute(x, "blk", [(i, i ^ (1 << bit)) for i in range(blks)])

    def place(block, reduce):
        other = lax.div(block, cells) ^ lax.axis_index("blk")
        order = reduce_order if reduce else gather_order
        at = sum(((other >> bit) & 1) << s for s, bit in enumerate(order))
        return at * cells + lax.rem(block, cells)

    def shape(n, dtype, r=rows):
        return jax.ShapeDtypeStruct((n, r, size), dtype)

    def scratch(n, r=rows, dtype=F32):
        return pltpu.VMEM((n, r, size), dtype)

    def scales(n):
        return pltpu.VMEM((scale_blocks(n) * GROUP, size), F32)

    def whole(n, r=rows):
        return pl.BlockSpec((n, r, size), lambda i, *_: (0, 0, 0))

    def owners(x, places, begin, end):
        x = x.reshape(-1, stride, rows, size)
        runs = []
        for at in places:
            if runs and runs[-1][1] == at:
                runs[-1][1] = at + 1
            else:
                runs.append([at, at + 1])
        return jnp.concatenate([x[low:high, begin:end] for low, high in runs], axis=0).reshape(-1, rows, size)

    near_acc = shape(total, F32, 2 * rows)
    other_tiles = swap_rank(near_tiles, 1)
    charge_other = swap_rank(charges, 2)
    basis_t = jnp.swapaxes(basis, 1, 2)

    width = max(near_first.shape[0], fars)
    lists = [x.reshape(1, -1) for x in (near_first, near_second, far_source, far_target)]
    own, at_second, at_first, at_source, at_target, tiles_low, near_zero = pl.pallas_call(
        functools.partial(prep_kernel, place),
        in_specs=[HBM] * 8,
        out_specs=[VMEM] * 7,
        out_shape=[
            shape(stride, BF16),
            *[jax.ShapeDtypeStruct((r, n), I32) for r, n in ((3, 2 * pairs), (2, 2 * pairs), (2, fars // 2), (2, fars // 2))],
            shape(pairs // 2, BF16, size),
            near_acc,
        ],
        scratch_shapes=[
            pltpu.SMEM(counts.shape, I32),
            pltpu.VMEM(charges.shape, BF16),
            pltpu.VMEM(basis_t.shape, BF16),
            pltpu.VMEM((4, width), I32),
            pltpu.VMEM((1, cells), I32),
            pltpu.SemaphoreType.DMA((9,)),
        ],
        compiler_params=params(8),
        cost_estimate=pl.CostEstimate(flops=0, bytes_accessed=12 << 20, transcendentals=0),
        name="prep",
    )(*[in_hbm(x) for x in (counts.reshape(1, -1), charges, basis_t, *lists, near_tiles)])
    charge_own = own[:cells]
    moment_own = own[cells:]
    moment_pair = swap_rank(moment_own, 1)

    far_cost = pl.CostEstimate(flops=2 * fars * rows * terms * terms, bytes_accessed=12 << 20, transcendentals=0)
    tiles_ij = jnp.transpose(far_tiles, (1, 2, 0)).reshape(terms * terms, fars)
    near_cost = pl.CostEstimate(flops=4 * pairs * rows * size * size, bytes_accessed=10 << 20, transcendentals=0)
    first_cost = pl.CostEstimate(flops=8 * pairs * rows * size * size, bytes_accessed=20 << 20, transcendentals=0)
    coded_a = total // 2
    coded_b = blks // 2 * cells
    stay = blks // 2
    near_sum, both, tiles_high = pl.pallas_call(
        near_second_a_kernel,
        in_specs=[SMEM, VMEM, VMEM, VMEM, HBM, VMEM],
        input_output_aliases={5: 0},
        out_specs=[VMEM] * 3,
        out_shape=[near_acc, shape(cells, BF16, 2 * rows), shape(pairs - pairs // 2, BF16, size)],
        scratch_shapes=[pltpu.SemaphoreType.DMA],
        compiler_params=params(4),
        cost_estimate=near_cost,
        name="near_second_a",
    )(at_second, charge_own, charge_other, tiles_low, in_hbm(near_tiles), near_zero)

    received = swap_blk(own, gather_order[0])
    received, near_sum = lax.optimization_barrier((received, near_sum))
    gathered = jnp.concatenate([own, received], axis=0)
    received = swap_blk(gathered, gather_order[1])
    near_sum, _ = lax.optimization_barrier((near_sum, gathered))

    _, keep_a, send_a, keep_b, send_b = pl.pallas_call(
        functools.partial(near_second_b_kernel, cells),
        in_specs=[SMEM, VMEM, VMEM, VMEM],
        out_specs=[VMEM] * 5,
        out_shape=[
            near_acc,
            shape(coded_a, F32),
            shape(coded_a + scale_blocks(coded_a), I16),
            shape(stay * halfc, F32, 2 * rows),
            shape(coded_b + scale_blocks(coded_b), I16),
        ],
        scratch_shapes=[
            scales(max(coded_a, coded_b)),
            scales(max(coded_a, coded_b)),
        ],
        input_output_aliases={3: 0},
        compiler_params=params(8),
        cost_estimate=near_cost,
        name="near_second_b",
    )(at_second, both, other_tiles, near_sum)
    moment_late, _ = lax.optimization_barrier((moment_pair, send_a))
    far_scratch = [
        pltpu.VMEM((terms // 2 * PITCH, size), F32),
        pltpu.VMEM((cells, 2 * rows, terms), BF16),
    ]
    far_sums = jax.ShapeDtypeStruct((total, 2 * rows, terms), F32)
    turned_a, far_acc = pl.pallas_call(
        far_source_a_kernel,
        in_specs=[SMEM] + [VMEM] * 3,
        out_specs=[VMEM] * 2,
        out_shape=[shape(fars // 4, BF16, terms // 2), far_sums],
        scratch_shapes=far_scratch,
        compiler_params=params(6),
        cost_estimate=far_cost,
        name="far_source_a",
    )(at_source, moment_own, moment_late, tiles_ij)
    received, far_acc = lax.optimization_barrier((received, far_acc))
    others, places = [], []
    for s, bit in enumerate(gather_order):
        if s > 1:
            received = swap_blk(gathered, bit)
        if 0 < s < bits - 1:
            gathered = jnp.concatenate([gathered, received], axis=0)
    places.append(early)
    others.append(swap_rank(owners(gathered, early, 0, cells), 2))
    far_acc, _ = lax.optimization_barrier((far_acc, gathered))
    turned_b, _, far_keep, *far_sends = pl.pallas_call(
        far_source_b_kernel,
        in_specs=[SMEM] + [VMEM] * 4,
        out_specs=[VMEM] * (3 + PARTS),
        out_shape=[
            shape(fars // 4, BF16, terms // 2),
            far_sums,
            shape(total // 2, F32),
            *[shape(total // 2 // PARTS, F32)] * PARTS,
        ],
        scratch_shapes=far_scratch,
        input_output_aliases={4: 1},
        compiler_params=params(6),
        cost_estimate=far_cost,
        name="far_source_b",
    )(at_source, moment_own, moment_late, tiles_ij, far_acc)
    far_others = [swap_rank(x, 1) for x in far_sends]

    got_a = swap_rank(send_a, 2)
    got_b = swap_blk(send_b, reduce_order[-1])
    got_b, got_a = lax.optimization_barrier((got_b, got_a))
    half_a = blks // 2 * cells
    half_b = blks // 2 * halfc
    meet_cost = pl.CostEstimate(flops=0, bytes_accessed=1 << 20, transcendentals=0)
    keep_b, send_b = pl.pallas_call(
        functools.partial(meet_b_kernel, halfc),
        in_specs=[VMEM] * 2,
        out_specs=[VMEM] * 2,
        out_shape=[shape(half_b, F32), shape(half_b + scale_blocks(half_b), I16)],
        scratch_shapes=[scratch(half_b), scales(coded_b), scales(half_b), scales(half_b)],
        compiler_params=params(8 + total // 16),
        cost_estimate=meet_cost,
        name="meet_b",
    )(keep_b, got_b)
    keep_a, _, others[0] = lax.optimization_barrier((keep_a, send_b, others[0]))
    got_b = swap_rank(send_b, 2)
    received, got_b = lax.optimization_barrier((received, got_b))
    gathered = jnp.concatenate([gathered, received], axis=0)
    places.append(late)
    others.append(swap_rank(owners(received, [at - blks // 2 for at in late], 0, cells), 2))
    joined = pl.pallas_call(
        join_kernel,
        in_specs=[VMEM] * 2,
        out_specs=VMEM,
        out_shape=shape(coded_a, F32),
        scratch_shapes=[scales(coded_a)],
        compiler_params=params(8),
        cost_estimate=pl.CostEstimate(flops=0, bytes_accessed=3 << 20, transcendentals=0),
        name="join",
    )(keep_a, got_a)
    keep_a, send_a = pl.pallas_call(
        functools.partial(meet_a_kernel, halfc),
        in_specs=[VMEM] * (2 + PARTS),
        out_specs=[VMEM] * 2,
        out_shape=[shape(half_a, F32), shape(half_a + scale_blocks(half_a), I16)],
        scratch_shapes=[scratch(half_a), scales(half_a), scales(half_a)],
        compiler_params=params(8 + total // 16),
        cost_estimate=meet_cost,
        name="meet_a",
    )(joined, far_keep, *far_others)
    got_a = swap_blk(send_a, reduce_order[-1])

    moment_all_pair = swap_rank(owners(gathered, range(blks), cells, stride), 1)
    target_keep, target_send = pl.pallas_call(
        functools.partial(far_target_kernel, stride, cells),
        in_specs=[SMEM] + [VMEM] * 4,
        out_specs=[VMEM] * 2,
        out_shape=[shape(halfc, F32), shape(halfc, F32)],
        scratch_shapes=[
            scratch(total, 4 * rows, BF16),
            pltpu.VMEM((cells, 4 * rows, terms // 2), F32),
        ],
        compiler_params=params(6 + total // 32),
        cost_estimate=meet_cost,
        name="far_target",
    )(at_target, gathered, moment_all_pair, turned_a, turned_b)
    target_other = swap_rank(target_send, 1)
    others[0], _ = lax.optimization_barrier((others[0], target_send))

    got_a, got_b, _ = lax.optimization_barrier((got_a, got_b, target_send))

    half = blks // 4 * stride
    keep, send = pl.pallas_call(
        functools.partial(meet_kernel, halfc),
        in_specs=[VMEM] * 4,
        out_specs=[VMEM] * 2,
        out_shape=[shape(half, F32), shape(half + scale_blocks(half), I16)],
        scratch_shapes=[scratch(half), scales(half_a), scales(half_b), scales(half), scales(half)],
        compiler_params=params(8 + total // 16),
        cost_estimate=meet_cost,
        name="meet",
    )(keep_a, got_a, keep_b, got_b)
    coded = swap_blk(send, reduce_order[-2])

    for bit in reversed(reduce_order[:-2]):
        now, half = half, half // 2
        keep, send = pl.pallas_call(
            add_kernel,
            in_specs=[VMEM] * 2,
            out_specs=[VMEM] * 2,
            out_shape=[shape(half, F32), shape(half + scale_blocks(half), I16)],
            scratch_shapes=[scratch(half), scales(now), scales(half), scales(half)],
            compiler_params=params(8 + total // 16),
            name="add",
        )(keep, coded)
        if bit != reduce_order[0]:
            coded = swap_blk(send, bit)

    first_keep, first_send = pl.pallas_call(
        functools.partial(near_first_kernel, stride, cells, places),
        in_specs=[SMEM] + [VMEM] * (5 + len(others)),
        out_specs=[VMEM, VMEM],
        out_shape=[shape(cells, F32), shape(cells + scale_blocks(cells), I16)],
        scratch_shapes=[
            scratch(total, 2 * rows, BF16),
            scratch(cells, 2 * rows),
            scales(cells),
            scales(cells),
        ],
        compiler_params=params(4 + total // 32),
        cost_estimate=first_cost,
        name="near_first",
    )(at_first, gathered, both, *others, tiles_low, tiles_high, other_tiles)
    first_send, send = lax.optimization_barrier((first_send, send))
    first_other = swap_rank(first_send, 2)
    coded = swap_blk(send, reduce_order[0])

    own_part = pl.pallas_call(
        self_kernel,
        in_specs=[VMEM] * 2,
        out_specs=VMEM,
        out_shape=shape(cells, F32),
        compiler_params=params(8),
        cost_estimate=meet_cost,
        name="self",
    )(charge_own, self_tiles)

    return pl.pallas_call(
        final_kernel,
        in_specs=[SMEM] + [VMEM] * 8,
        out_specs=VMEM,
        out_shape=jax.ShapeDtypeStruct(charges.shape, F32),
        scratch_shapes=[scales(stride), scales(cells)],
        compiler_params=params(8),
        name="final",
    )(
        counts, keep, coded, first_keep, first_other, target_keep, target_other, own_part, basis_t
    )


def solution(mesh):
    in_specs = (
        P("rhs", "blk"),
        P("blk"),
        P("blk", None, None),
        P("blk", None, None),
        P("blk"),
        P("blk"),
        P(("blk", "rhs"), None, None),
        P("blk"),
        P("blk"),
        P("blk", None, None),
    )
    out_specs = P("rhs", "blk")
    return jax.shard_map(body, mesh=mesh, in_specs=in_specs, out_specs=out_specs, check_vma=False)
```

```python
import functools

import jax
import jax.numpy as jnp
from jax import lax
from jax.experimental import pallas as pl
from jax.experimental.pallas import tpu as pltpu
from jax.sharding import PartitionSpec as P

F32, BF16, I16, I32 = jnp.float32, jnp.bfloat16, jnp.int16, jnp.int32
REACH = 48
GROUP = 16
TOP = 32767.0
VMEM = pl.BlockSpec(memory_space=pltpu.VMEM)
SMEM = pl.BlockSpec(memory_space=pltpu.SMEM)
HBM = pl.BlockSpec(memory_space=pltpu.HBM)
NAT = (((1,), (0,)), ((), ()))
TRN = (((1,), (1,)), ((), ()))


def params(mib):
    return pltpu.CompilerParams(vmem_limit_bytes=mib << 20)


def in_hbm(x):
    return pltpu.with_memory_space_constraint(x, pltpu.HBM)


def dot(lhs, rhs, dims):
    return lax.dot_general(lhs, rhs, dims, preferred_element_type=F32)


def scale_blocks(count):
    return -(-count // GROUP)


def encode(get, out, outer, inner, peak, inv):
    count = outer * inner
    peak[...] = jnp.zeros_like(peak)

    def find(o, _):
        for i in range(inner):
            peak[pl.ds(o * inner + i, 1), :] = jnp.max(jnp.abs(get(o, i)), axis=0, keepdims=True)
        return 0

    lax.fori_loop(0, outer, find, 0)
    code = jnp.ceil(jnp.log2(jnp.maximum(peak[...], 1e-30)) * 8.0) + 1.0
    inv[...] = TOP * jnp.exp2(code * -0.125)
    for s in range(scale_blocks(count)):
        out[count + s] = code[s * GROUP : (s + 1) * GROUP].astype(I32).astype(I16)

    def put(o, _):
        for i in range(inner):
            b = o * inner + i
            out[b] = jnp.round(get(o, i) * inv[pl.ds(b, 1), :]).astype(I32).astype(I16)
        return 0

    lax.fori_loop(0, outer, put, 0)


def decode_scales(coded, count, scale):
    for s in range(scale_blocks(count)):
        code = coded[count + s].astype(I32).astype(F32)
        scale[s * GROUP : (s + 1) * GROUP, :] = jnp.exp2(code * 0.125) * (1.0 / TOP)


def decode(coded, scale, b):
    return coded[b].astype(I32).astype(F32) * scale[pl.ds(b, 1), :]


def prep_kernel(
    place, counts_in, charges_in, basis_in, near_first, near_second, far_source, far_target, tiles_in,
    out, at_second, at_first, at_source, at_target, tiles, near_zero, counts, charges, basis_t, lists, counts_row, sems,
):
    moves = [(counts_in.at[0], counts), (charges_in, charges), (basis_in, basis_t), (counts_in, counts_row)]
    moves += [
        (src, lists.at[pl.ds(i, 1)]) for i, src in enumerate((near_first, near_second, far_source, far_target))
    ]
    count = tiles.shape[0] // TILE_COPIES
    spans = [pl.ds(i * count, count) for i in range(TILE_COPIES)]
    moves += [(tiles_in.at[span], tiles.at[span]) for span in spans]
    copies = [pltpu.make_async_copy(src, dst, sems.at[i]) for i, (src, dst) in enumerate(moves)]
    for copy in copies:
        copy.start()
    for copy in copies[:-TILE_COPIES]:
        copy.wait()
    cells, terms, size = basis_t.shape
    rows = charges.shape[0]
    lane = lax.broadcasted_iota(I32, (rows, size), 1)
    moments = []
    for c in range(cells):
        x = charges[:, c * size : (c + 1) * size]
        x = jnp.where(lane < counts[c], x, jnp.zeros_like(x))
        out[c] = x
        moments.append(dot(x, basis_t[c], TRN))
    for k in range(cells // 2):
        out[cells + k] = jnp.concatenate(moments[2 * k : 2 * k + 2], axis=1).astype(BF16)
    rank = lax.axis_index("rhs")
    pairs = tiles_in.shape[0]
    for flip in range(2):
        span = pl.ds(pl.multiple_of((rank ^ flip) * pairs, pairs), pairs)
        to = slice(flip * pairs, (flip + 1) * pairs)
        first, second = lists[0:1, span], lists[1:2, span]
        for at in (at_second, at_first):
            at[0:1, to] = lax.rem(first, cells)
        at_second[1:2, to] = place(second, 1)
        at_first[1:2, to] = place(second, 0)
    at_second[2:3, :cells] = counts_row[...]
    half = lists.shape[1] // 2
    span = pl.ds(pl.multiple_of((rank & 1) * half, half), half)
    source, target = lists[2:3, span], lists[3:4, span]
    for at, reduce in ((at_source, 1), (at_target, 0)):
        at[0:1, :] = lax.rem(target, cells)
        at[1:2, :] = place(source, reduce)
    near_zero[...] = jnp.zeros_like(near_zero)
    for copy in copies[-TILE_COPIES:]:
        copy.wait()


TILE_COPIES = 4
PITCH = 136
FAR_UNROLL = 64
NEAR_UNROLL = 64
PARTS = 4


def far_sources(step, idx, mine, theirs, tiles, turned, acc, flip, lhs):
    half = mine.shape[2] // 2
    pairs = half // 2
    chunk = turned.shape[0]
    for k in range(mine.shape[0]):
        x, y = mine[k], theirs[k]
        for h in range(2):
            at = h * half
            lhs[2 * k + h] = jnp.concatenate([x[:, at : at + half], y[:, at : at + half]], axis=0)
    span = pl.ds(pl.multiple_of((lax.axis_index("rhs") & 1) * 2 * chunk + step * chunk, chunk), chunk)
    for i in range(pairs):
        both = [tiles[(i + h * pairs) * half : (i + h * pairs + 1) * half, span] for h in range(2)]
        flip[i * PITCH : i * PITCH + chunk, :] = jnp.concatenate(both, axis=0).astype(F32).T

    def work(g, _):
        sums = []
        at = g * FAR_UNROLL
        for u in range(FAR_UNROLL):
            w = flip[pl.ds(at + u, pairs, stride=PITCH), :]
            turned[at + u] = w.astype(BF16)
            moved = pltpu.roll(w, half, 1)
            w = jnp.concatenate([w[:, :half], moved[:, :half]], axis=0).astype(BF16)
            sums.append(dot(lhs[idx[0, step * chunk + at + u]], w, NAT))
        for u in range(FAR_UNROLL):
            acc[idx[1, step * chunk + at + u]] += sums[u]
        return 0

    lax.fori_loop(0, chunk // FAR_UNROLL, work, 0)


def far_source_a_kernel(idx, mine, theirs, tiles, turned, acc, flip, lhs):
    acc[...] = jnp.zeros_like(acc)
    far_sources(0, idx, mine, theirs, tiles, turned, acc, flip, lhs)


def far_source_b_kernel(idx, mine, theirs, tiles, before, turned, acc, keep, *refs):
    *sends, flip, lhs = refs
    rows = mine.shape[1]
    far_sources(1, idx, mine, theirs, tiles, turned, acc, flip, lhs)
    count = sends[0].shape[0]
    for q, send in enumerate(sends):

        def fold(k, _, q=q, send=send):
            for u in range(4):
                at = q * count + 4 * k + u
                both = jnp.concatenate([acc[2 * at], acc[2 * at + 1]], axis=1)
                keep[at] = both[:rows]
                send[4 * k + u] = both[rows:]
            return 0

        lax.fori_loop(0, count // 4, fold, 0)


def far_target_kernel(stride, cells, idx, everyone, theirs, turned_a, turned_b, keep, send, lhs, acc):
    rows, lanes = everyone.shape[1], everyone.shape[2]
    half = lanes // 2
    chunk = turned_a.shape[0]
    owners = everyone.shape[0] // stride
    acc[...] = jnp.zeros_like(acc)
    low = lax.broadcasted_iota(I32, (2 * rows, lanes), 1) < half

    def spread(o, _):
        for k in range(cells // 2):
            x = jnp.concatenate([everyone[o * stride + cells + k], theirs[o * (cells // 2) + k]], axis=0)
            y = jnp.concatenate([x[:, half:], x[:, :half]], axis=1)
            zero = jnp.zeros_like(x)
            at = o * cells + 2 * k
            lhs[at] = jnp.concatenate([jnp.where(low, x, zero), jnp.where(low, zero, y)], axis=0)
            lhs[at + 1] = jnp.concatenate([jnp.where(low, y, zero), jnp.where(low, zero, x)], axis=0)
        return 0

    lax.fori_loop(0, owners, spread, 0)
    for step, turned in enumerate((turned_a, turned_b)):

        def work(g, _, base=step * chunk, turned=turned):
            sums = []
            for u in range(FAR_UNROLL):
                e = g * FAR_UNROLL + u
                sums.append(dot(lhs[idx[1, base + e]], turned[e], TRN))
            for u in range(FAR_UNROLL):
                acc[idx[0, base + g * FAR_UNROLL + u]] += sums[u]
            return 0

        lax.fori_loop(0, chunk // FAR_UNROLL, work, 0)
    for k in range(cells // 2):
        a, b = acc[2 * k], acc[2 * k + 1]
        for r, out in enumerate((keep, send)):
            at = (r * rows, (2 + r) * rows)
            out[k] = jnp.concatenate([x[i : i + rows] for x in (a, b) for i in at], axis=1)


def near_loop(idx, lhs, lhs_at, tiles, first, dims, acc, acc_at):
    count, size = tiles.shape[:2]
    rows = lhs.shape[1]
    group = min(NEAR_UNROLL, count)
    zero = jnp.zeros((rows, size), lhs.dtype)
    for low in range(0, count, group):
        high = min(low + group, count)
        sums = []
        for n in range(low, high, 2):
            a, b = (lhs[idx[lhs_at, first + n + i]] for i in range(2))
            both = jnp.concatenate([tiles[n], tiles[n + 1]], axis=0)
            if dims is TRN:
                out = dot(jnp.concatenate([a, b], axis=0), both, TRN)
                sums += [out[:rows, :size], out[rows:, size:]]
            else:
                wide = [jnp.concatenate(x, axis=1) for x in ((a, zero), (zero, b))]
                out = dot(jnp.concatenate(wide, axis=0), both, NAT)
                sums += [out[:rows], out[rows:]]
        for n in range(low, high):
            acc[idx[acc_at, first + n]] += sums[n - low]


def near_second_a_kernel(idx, mine, theirs, tiles, rest, zero, acc, both, tiles_high, sems):
    rows, size = mine.shape[1:]

    half, pairs = tiles.shape[0], rest.shape[0]
    count = (pairs - half) // TILE_COPIES
    copies = [
        pltpu.make_async_copy(
            rest.at[pl.ds(half + i * count, count)], tiles_high.at[pl.ds(i * count, count)], sems.at[i]
        )
        for i in range(TILE_COPIES)
    ]
    for copy in copies:
        copy.start()
    lane = lax.broadcasted_iota(I32, (rows, size), 1)
    for c in range(both.shape[0]):
        x = theirs[:, c * size : (c + 1) * size]
        x = jnp.where(lane < idx[2, c], x, jnp.zeros_like(x))
        both[c] = jnp.concatenate([mine[c], x], axis=0)
    near_loop(idx, both, 0, tiles, 0, NAT, acc, 1)
    for copy in copies:
        copy.wait()
    near_loop(idx, both, 0, tiles_high, half, NAT, acc, 1)


def near_second_b_kernel(
    cells, idx, both, other, before, acc, keep_a, send_a, keep_b, send_b, peak, inv
):
    rows = both.shape[1] // 2
    half = cells // 2
    owners = acc.shape[0] // cells
    stay = keep_b.shape[0] // half
    near_loop(idx, both, 0, other, other.shape[0], NAT, acc, 1)
    encode(lambda o, c: acc[o * cells + c, rows:, :], send_a, owners, half, peak, inv)

    def part_b(o, i):
        return acc[(stay + o) * cells + half + i // 2, i % 2 * rows : (i % 2 + 1) * rows, :]

    encode(part_b, send_b, owners - stay, 2 * half, peak, inv)

    def own_a(o, _):
        for c in range(half):
            keep_a[o * half + c] = acc[o * cells + c, :rows, :]
        return 0

    def own_b(o, _):
        for c in range(half):
            keep_b[o * half + c] = acc[o * cells + half + c]
        return 0

    lax.fori_loop(0, owners, own_a, 0)
    lax.fori_loop(0, stay, own_b, 0)


def near_first_kernel(stride, cells, places, idx, everyone, both, *refs):
    *parts, tiles, tiles_high, other, keep, send, lhs, acc, peak, inv = refs
    rows = everyone.shape[1]

    acc[...] = jnp.zeros_like(acc)
    lhs[:cells] = both[...]
    for part, at in zip(parts, places):
        for i, p in enumerate(at):
            for c in range(cells):
                lhs[p * cells + c] = jnp.concatenate([everyone[p * stride + c], part[i * cells + c]], axis=0)
    near_loop(idx, lhs, 1, tiles, 0, TRN, acc, 0)
    near_loop(idx, lhs, 1, tiles_high, tiles.shape[0], TRN, acc, 0)
    near_loop(idx, lhs, 1, other, other.shape[0], TRN, acc, 0)
    for c in range(cells):
        keep[c] = acc[c, :rows, :]
    encode(lambda o, c: acc[c, rows:, :], send, 1, cells, peak, inv)


def join_kernel(mine, coded, out, scale):
    count = out.shape[0]
    decode_scales(coded, count, scale)

    def one(o, _):
        for i in range(8):
            b = o * 8 + i
            out[b] = mine[b] + decode(coded, scale, b)
        return 0

    lax.fori_loop(0, count // 8, one, 0)


def meet_a_kernel(half, mine, far, *refs):
    *far_others, keep, send, acc, peak, inv = refs
    count = far_others[0].shape[0]
    owners = far.shape[0] // half
    stay = owners // 2
    for p in range(owners):
        dst, at = (keep, p) if p < stay else (acc, p - stay)
        for c in range(half):
            b = p * half + c
            dst[at * 2 * half + c] = mine[b]
            dst[at * 2 * half + half + c] = far[b] + far_others[b // count][b % count]
    encode(lambda o, i: acc[o * 8 + i], send, acc.shape[0] // 8, 8, peak, inv)


def meet_b_kernel(half, mine, coded, keep, send, acc, scale, peak, inv):
    rows = keep.shape[1]
    owners = keep.shape[0] // half
    decode_scales(coded, 2 * keep.shape[0], scale)
    for p in range(owners):
        for c in range(half):
            b = p * half + c
            keep[b] = mine[b, :rows, :] + decode(coded, scale, 2 * b)
            acc[b] = mine[b, rows:, :] + decode(coded, scale, 2 * b + 1)
    encode(lambda o, i: acc[o * 8 + i], send, acc.shape[0] // 8, 8, peak, inv)


def meet_kernel(half, mine_a, coded_a, mine_b, coded_b, keep, send, acc, scale_a, scale_b, peak, inv):
    owners = mine_b.shape[0] // half
    stay = owners // 2
    decode_scales(coded_a, mine_a.shape[0], scale_a)
    decode_scales(coded_b, mine_b.shape[0], scale_b)
    for p in range(owners):
        dst, at = (keep, p * 3) if p < stay else (acc, (p - stay) * 3)
        for c in range(half):
            a, b = p * 2 * half + c, p * half + c
            dst[at * half + c] = mine_a[a] + decode(coded_a, scale_a, a)
            dst[(at + 1) * half + c] = mine_b[b] + decode(coded_b, scale_b, b)
            a = a + half
            dst[(at + 2) * half + c] = mine_a[a] + decode(coded_a, scale_a, a)
    encode(lambda o, i: acc[o * 8 + i], send, acc.shape[0] // 8, 8, peak, inv)


def add_kernel(mine, coded, keep, send, acc, scale, peak, inv):
    total = mine.shape[0]
    half = total // 2
    decode_scales(coded, total, scale)

    def one(b, _):
        keep[b] = mine[b] + decode(coded, scale, b)
        acc[b] = mine[half + b] + decode(coded, scale, half + b)
        return 0

    lax.fori_loop(0, half, one, 0, unroll=8)
    encode(lambda o, i: acc[o * 8 + i], send, half // 8, 8, peak, inv)


def self_kernel(moved, self_tiles, out):
    for c in range(out.shape[0]):
        out[c] = dot(moved[c], self_tiles[c], TRN)


def final_kernel(
    counts, mine, coded, first, first_other, target, target_other, own, basis_t, out, scale, first_scale
):
    cells, terms, size = basis_t.shape
    rows = out.shape[0]
    decode_scales(coded, mine.shape[0], scale)
    decode_scales(first_other, cells, first_scale)
    lane = lax.broadcasted_iota(I32, (rows, size), 1)
    for k in range(cells // 2):
        b = cells + k
        fields = (mine[b] + decode(coded, scale, b) + target[k] + target_other[k]).astype(BF16)
        for h in range(2):
            c = 2 * k + h
            near = mine[c] + decode(coded, scale, c) + first[c] + decode(first_other, first_scale, c)
            far = dot(fields[:, h * terms : (h + 1) * terms], basis_t[c], NAT)
            total = near + far + own[c]
            out[:, c * size : (c + 1) * size] = jnp.where(lane < counts[c], total, jnp.zeros_like(total))


def body(
    charges,
    counts,
    self_tiles,
    basis,
    near_first,
    near_second,
    near_tiles,
    far_source,
    far_target,
    far_tiles,
):
    blks = lax.axis_size("blk")
    ranks = lax.axis_size("rhs")
    me = lax.axis_index("blk")
    rank = lax.axis_index("rhs")
    cells, size, _ = self_tiles.shape
    terms = basis.shape[2]
    rows = charges.shape[0]
    pairs = near_tiles.shape[0]
    fars = far_tiles.shape[0]
    bits = blks.bit_length() - 1
    gather_order = [0, *range(bits - 1, 0, -1)]
    reduce_order = [*range(bits - 1, -1, -1)]
    halfc = cells // 2
    stride = cells + halfc
    total = blks * cells

    def reached(at):
        mask = sum(((at >> s) & 1) << bit for s, bit in enumerate(gather_order))
        gaps = [(o ^ mask) - o for o in range(blks)]
        return min(min(g % blks, -g % blks) for g in gaps) <= -(-REACH // cells)

    early = [at for at in range(1, blks // 2) if reached(at)]
    late = [at for at in range(blks // 2, blks) if reached(at)]

    def swap_rank(x, d):
        return lax.ppermute(x, "rhs", [(i, i ^ d) for i in range(ranks)])

    def swap_blk(x, bit):
        return lax.ppermute(x, "blk", [(i, i ^ (1 << bit)) for i in range(blks)])

    def place(block, reduce):
        other = lax.div(block, cells) ^ lax.axis_index("blk")
        order = reduce_order if reduce else gather_order
        at = sum(((other >> bit) & 1) << s for s, bit in enumerate(order))
        return at * cells + lax.rem(block, cells)

    def shape(n, dtype, r=rows):
        return jax.ShapeDtypeStruct((n, r, size), dtype)

    def scratch(n, r=rows, dtype=F32):
        return pltpu.VMEM((n, r, size), dtype)

    def scales(n):
        return pltpu.VMEM((scale_blocks(n) * GROUP, size), F32)

    def whole(n, r=rows):
        return pl.BlockSpec((n, r, size), lambda i, *_: (0, 0, 0))

    def owners(x, places, begin, end):
        x = x.reshape(-1, stride, rows, size)
        runs = []
        for at in places:
            if runs and runs[-1][1] == at:
                runs[-1][1] = at + 1
            else:
                runs.append([at, at + 1])
        return jnp.concatenate([x[low:high, begin:end] for low, high in runs], axis=0).reshape(-1, rows, size)

    near_acc = shape(total, F32, 2 * rows)
    other_tiles = swap_rank(near_tiles, 1)
    charge_other = swap_rank(charges, 2)
    basis_t = jnp.swapaxes(basis, 1, 2)

    width = max(near_first.shape[0], fars)
    lists = [x.reshape(1, -1) for x in (near_first, near_second, far_source, far_target)]
    own, at_second, at_first, at_source, at_target, tiles_low, near_zero = pl.pallas_call(
        functools.partial(prep_kernel, place),
        in_specs=[HBM] * 8,
        out_specs=[VMEM] * 7,
        out_shape=[
            shape(stride, BF16),
            *[jax.ShapeDtypeStruct((r, n), I32) for r, n in ((3, 2 * pairs), (2, 2 * pairs), (2, fars // 2), (2, fars // 2))],
            shape(pairs // 2, BF16, size),
            near_acc,
        ],
        scratch_shapes=[
            pltpu.SMEM(counts.shape, I32),
            pltpu.VMEM(charges.shape, BF16),
            pltpu.VMEM(basis_t.shape, BF16),
            pltpu.VMEM((4, width), I32),
            pltpu.VMEM((1, cells), I32),
            pltpu.SemaphoreType.DMA((8 + TILE_COPIES,)),
        ],
        compiler_params=params(8),
        cost_estimate=pl.CostEstimate(flops=0, bytes_accessed=12 << 20, transcendentals=0),
        name="prep",
    )(*[in_hbm(x) for x in (counts.reshape(1, -1), charges, basis_t, *lists, near_tiles)])
    charge_own = own[:cells]
    moment_own = own[cells:]
    moment_pair = swap_rank(moment_own, 1)

    far_cost = pl.CostEstimate(flops=2 * fars * rows * terms * terms, bytes_accessed=12 << 20, transcendentals=0)
    tiles_ij = jnp.transpose(far_tiles, (1, 2, 0)).reshape(terms * terms, fars)
    near_cost = pl.CostEstimate(flops=4 * pairs * rows * size * size, bytes_accessed=10 << 20, transcendentals=0)
    first_cost = pl.CostEstimate(flops=8 * pairs * rows * size * size, bytes_accessed=20 << 20, transcendentals=0)
    coded_a = total // 2
    coded_b = blks // 2 * cells
    stay = blks // 2
    near_sum, both, tiles_high = pl.pallas_call(
        near_second_a_kernel,
        in_specs=[SMEM, VMEM, VMEM, VMEM, HBM, VMEM],
        input_output_aliases={5: 0},
        out_specs=[VMEM] * 3,
        out_shape=[near_acc, shape(cells, BF16, 2 * rows), shape(pairs - pairs // 2, BF16, size)],
        scratch_shapes=[pltpu.SemaphoreType.DMA((TILE_COPIES,))],
        compiler_params=params(4),
        cost_estimate=near_cost,
        name="near_second_a",
    )(at_second, charge_own, charge_other, tiles_low, in_hbm(near_tiles), near_zero)

    received = swap_blk(own, gather_order[0])
    received, near_sum = lax.optimization_barrier((received, near_sum))
    gathered = jnp.concatenate([own, received], axis=0)
    received = swap_blk(gathered, gather_order[1])
    near_sum, _ = lax.optimization_barrier((near_sum, gathered))

    _, keep_a, send_a, keep_b, send_b = pl.pallas_call(
        functools.partial(near_second_b_kernel, cells),
        in_specs=[SMEM, VMEM, VMEM, VMEM],
        out_specs=[VMEM] * 5,
        out_shape=[
            near_acc,
            shape(coded_a, F32),
            shape(coded_a + scale_blocks(coded_a), I16),
            shape(stay * halfc, F32, 2 * rows),
            shape(coded_b + scale_blocks(coded_b), I16),
        ],
        scratch_shapes=[
            scales(max(coded_a, coded_b)),
            scales(max(coded_a, coded_b)),
        ],
        input_output_aliases={3: 0},
        compiler_params=params(8),
        cost_estimate=near_cost,
        name="near_second_b",
    )(at_second, both, other_tiles, near_sum)
    moment_late, _ = lax.optimization_barrier((moment_pair, send_a))
    far_scratch = [
        pltpu.VMEM((terms // 2 * PITCH, size), F32),
        pltpu.VMEM((cells, 2 * rows, terms), BF16),
    ]
    far_sums = jax.ShapeDtypeStruct((total, 2 * rows, terms), F32)
    turned_a, far_acc = pl.pallas_call(
        far_source_a_kernel,
        in_specs=[SMEM] + [VMEM] * 3,
        out_specs=[VMEM] * 2,
        out_shape=[shape(fars // 4, BF16, terms // 2), far_sums],
        scratch_shapes=far_scratch,
        compiler_params=params(6),
        cost_estimate=far_cost,
        name="far_source_a",
    )(at_source, moment_own, moment_late, tiles_ij)
    received, far_acc = lax.optimization_barrier((received, far_acc))
    others, places = [], []
    for s, bit in enumerate(gather_order):
        if s > 1:
            received = swap_blk(gathered, bit)
        if 0 < s < bits - 1:
            gathered = jnp.concatenate([gathered, received], axis=0)
    places.append(early)
    others.append(swap_rank(owners(gathered, early, 0, cells), 2))
    far_acc, _ = lax.optimization_barrier((far_acc, gathered))
    turned_b, _, far_keep, *far_sends = pl.pallas_call(
        far_source_b_kernel,
        in_specs=[SMEM] + [VMEM] * 4,
        out_specs=[VMEM] * (3 + PARTS),
        out_shape=[
            shape(fars // 4, BF16, terms // 2),
            far_sums,
            shape(total // 2, F32),
            *[shape(total // 2 // PARTS, F32)] * PARTS,
        ],
        scratch_shapes=far_scratch,
        input_output_aliases={4: 1},
        compiler_params=params(6),
        cost_estimate=far_cost,
        name="far_source_b",
    )(at_source, moment_own, moment_late, tiles_ij, far_acc)
    far_others = [swap_rank(x, 1) for x in far_sends]

    got_a = swap_rank(send_a, 2)
    got_b = swap_blk(send_b, reduce_order[-1])
    got_b, got_a = lax.optimization_barrier((got_b, got_a))
    half_a = blks // 2 * cells
    half_b = blks // 2 * halfc
    meet_cost = pl.CostEstimate(flops=0, bytes_accessed=1 << 20, transcendentals=0)
    keep_b, send_b = pl.pallas_call(
        functools.partial(meet_b_kernel, halfc),
        in_specs=[VMEM] * 2,
        out_specs=[VMEM] * 2,
        out_shape=[shape(half_b, F32), shape(half_b + scale_blocks(half_b), I16)],
        scratch_shapes=[scratch(half_b), scales(coded_b), scales(half_b), scales(half_b)],
        compiler_params=params(8 + total // 16),
        cost_estimate=meet_cost,
        name="meet_b",
    )(keep_b, got_b)
    keep_a, _, others[0] = lax.optimization_barrier((keep_a, send_b, others[0]))
    got_b = swap_rank(send_b, 2)
    received, got_b = lax.optimization_barrier((received, got_b))
    gathered = jnp.concatenate([gathered, received], axis=0)
    places.append(late)
    others.append(swap_rank(owners(received, [at - blks // 2 for at in late], 0, cells), 2))
    joined = pl.pallas_call(
        join_kernel,
        in_specs=[VMEM] * 2,
        out_specs=VMEM,
        out_shape=shape(coded_a, F32),
        scratch_shapes=[scales(coded_a)],
        compiler_params=params(8),
        cost_estimate=pl.CostEstimate(flops=0, bytes_accessed=3 << 20, transcendentals=0),
        name="join",
    )(keep_a, got_a)
    keep_a, send_a = pl.pallas_call(
        functools.partial(meet_a_kernel, halfc),
        in_specs=[VMEM] * (2 + PARTS),
        out_specs=[VMEM] * 2,
        out_shape=[shape(half_a, F32), shape(half_a + scale_blocks(half_a), I16)],
        scratch_shapes=[scratch(half_a), scales(half_a), scales(half_a)],
        compiler_params=params(8 + total // 16),
        cost_estimate=meet_cost,
        name="meet_a",
    )(joined, far_keep, *far_others)
    got_a = swap_blk(send_a, reduce_order[-1])

    moment_all_pair = swap_rank(owners(gathered, range(blks), cells, stride), 1)
    target_keep, target_send = pl.pallas_call(
        functools.partial(far_target_kernel, stride, cells),
        in_specs=[SMEM] + [VMEM] * 4,
        out_specs=[VMEM] * 2,
        out_shape=[shape(halfc, F32), shape(halfc, F32)],
        scratch_shapes=[
            scratch(total, 4 * rows, BF16),
            pltpu.VMEM((cells, 4 * rows, terms // 2), F32),
        ],
        compiler_params=params(6 + total // 32),
        cost_estimate=meet_cost,
        name="far_target",
    )(at_target, gathered, moment_all_pair, turned_a, turned_b)
    target_other = swap_rank(target_send, 1)
    others[0], _ = lax.optimization_barrier((others[0], target_send))

    got_a, got_b, _ = lax.optimization_barrier((got_a, got_b, target_send))

    half = blks // 4 * stride
    keep, send = pl.pallas_call(
        functools.partial(meet_kernel, halfc),
        in_specs=[VMEM] * 4,
        out_specs=[VMEM] * 2,
        out_shape=[shape(half, F32), shape(half + scale_blocks(half), I16)],
        scratch_shapes=[scratch(half), scales(half_a), scales(half_b), scales(half), scales(half)],
        compiler_params=params(8 + total // 16),
        cost_estimate=meet_cost,
        name="meet",
    )(keep_a, got_a, keep_b, got_b)
    coded = swap_blk(send, reduce_order[-2])

    for bit in reversed(reduce_order[:-2]):
        now, half = half, half // 2
        keep, send = pl.pallas_call(
            add_kernel,
            in_specs=[VMEM] * 2,
            out_specs=[VMEM] * 2,
            out_shape=[shape(half, F32), shape(half + scale_blocks(half), I16)],
            scratch_shapes=[scratch(half), scales(now), scales(half), scales(half)],
            compiler_params=params(8 + total // 16),
            name="add",
        )(keep, coded)
        if bit != reduce_order[0]:
            coded = swap_blk(send, bit)

    first_keep, first_send = pl.pallas_call(
        functools.partial(near_first_kernel, stride, cells, places),
        in_specs=[SMEM] + [VMEM] * (5 + len(others)),
        out_specs=[VMEM, VMEM],
        out_shape=[shape(cells, F32), shape(cells + scale_blocks(cells), I16)],
        scratch_shapes=[
            scratch(total, 2 * rows, BF16),
            scratch(cells, 2 * rows),
            scales(cells),
            scales(cells),
        ],
        compiler_params=params(4 + total // 32),
        cost_estimate=first_cost,
        name="near_first",
    )(at_first, gathered, both, *others, tiles_low, tiles_high, other_tiles)
    first_send, send = lax.optimization_barrier((first_send, send))
    first_other = swap_rank(first_send, 2)
    coded = swap_blk(send, reduce_order[0])

    own_part = pl.pallas_call(
        self_kernel,
        in_specs=[VMEM] * 2,
        out_specs=VMEM,
        out_shape=shape(cells, F32),
        compiler_params=params(8),
        cost_estimate=meet_cost,
        name="self",
    )(charge_own, self_tiles)

    return pl.pallas_call(
        final_kernel,
        in_specs=[SMEM] + [VMEM] * 8,
        out_specs=VMEM,
        out_shape=jax.ShapeDtypeStruct(charges.shape, F32),
        scratch_shapes=[scales(stride), scales(cells)],
        compiler_params=params(8),
        name="final",
    )(
        counts, keep, coded, first_keep, first_other, target_keep, target_other, own_part, basis_t
    )


def solution(mesh):
    in_specs = (
        P("rhs", "blk"),
        P("blk"),
        P("blk", None, None),
        P("blk", None, None),
        P("blk"),
        P("blk"),
        P(("blk", "rhs"), None, None),
        P("blk"),
        P("blk"),
        P("blk", None, None),
    )
    out_specs = P("rhs", "blk")
    return jax.shard_map(body, mesh=mesh, in_specs=in_specs, out_specs=out_specs, check_vma=False)
```

```python
import functools

import jax
import jax.numpy as jnp
from jax import lax
from jax.experimental import pallas as pl
from jax.experimental.pallas import tpu as pltpu
from jax.sharding import PartitionSpec as P

F32, BF16, I16, I32 = jnp.float32, jnp.bfloat16, jnp.int16, jnp.int32
REACH = 48
GROUP = 16
TOP = 32767.0
VMEM = pl.BlockSpec(memory_space=pltpu.VMEM)
SMEM = pl.BlockSpec(memory_space=pltpu.SMEM)
HBM = pl.BlockSpec(memory_space=pltpu.HBM)
NAT = (((1,), (0,)), ((), ()))
TRN = (((1,), (1,)), ((), ()))


def params(mib):
    return pltpu.CompilerParams(vmem_limit_bytes=mib << 20)


def in_hbm(x):
    return pltpu.with_memory_space_constraint(x, pltpu.HBM)


def dot(lhs, rhs, dims):
    return lax.dot_general(lhs, rhs, dims, preferred_element_type=F32)


def scale_blocks(count):
    return -(-count // GROUP)


def encode(get, out, outer, inner, peak, inv):
    count = outer * inner
    peak[...] = jnp.zeros_like(peak)

    def find(o, _):
        for i in range(inner):
            peak[pl.ds(o * inner + i, 1), :] = jnp.max(jnp.abs(get(o, i)), axis=0, keepdims=True)
        return 0

    lax.fori_loop(0, outer, find, 0)
    code = jnp.ceil(jnp.log2(jnp.maximum(peak[...], 1e-30)) * 8.0) + 1.0
    inv[...] = TOP * jnp.exp2(code * -0.125)
    for s in range(scale_blocks(count)):
        out[count + s] = code[s * GROUP : (s + 1) * GROUP].astype(I32).astype(I16)

    def put(o, _):
        for i in range(inner):
            b = o * inner + i
            out[b] = jnp.round(get(o, i) * inv[pl.ds(b, 1), :]).astype(I32).astype(I16)
        return 0

    lax.fori_loop(0, outer, put, 0)


def decode_scales(coded, count, scale):
    for s in range(scale_blocks(count)):
        code = coded[count + s].astype(I32).astype(F32)
        scale[s * GROUP : (s + 1) * GROUP, :] = jnp.exp2(code * 0.125) * (1.0 / TOP)


def decode(coded, scale, b):
    return coded[b].astype(I32).astype(F32) * scale[pl.ds(b, 1), :]


def prep_kernel(
    place, counts_in, charges_in, basis_in, near_first, near_second, far_source, far_target, tiles_in,
    out, at_second, at_first, at_source, at_target, tiles, near_zero, counts, charges, basis_t, lists, counts_row, sems,
):
    moves = [(counts_in.at[0], counts), (charges_in, charges), (basis_in, basis_t), (counts_in, counts_row)]
    moves += [
        (src, lists.at[pl.ds(i, 1)]) for i, src in enumerate((near_first, near_second, far_source, far_target))
    ]
    count = tiles.shape[0] // TILE_COPIES
    spans = [pl.ds(i * count, count) for i in range(TILE_COPIES)]
    moves += [(tiles_in.at[span], tiles.at[span]) for span in spans]
    copies = [pltpu.make_async_copy(src, dst, sems.at[i]) for i, (src, dst) in enumerate(moves)]
    for copy in copies:
        copy.start()
    for copy in copies[:-TILE_COPIES]:
        copy.wait()
    cells, terms, size = basis_t.shape
    rows = charges.shape[0]
    lane = lax.broadcasted_iota(I32, (rows, size), 1)
    moments = []
    for c in range(cells):
        x = charges[:, c * size : (c + 1) * size]
        x = jnp.where(lane < counts[c], x, jnp.zeros_like(x))
        out[c] = x
        moments.append(dot(x, basis_t[c], TRN))
    for k in range(cells // 2):
        out[cells + k] = jnp.concatenate(moments[2 * k : 2 * k + 2], axis=1).astype(BF16)
    rank = lax.axis_index("rhs")
    pairs = tiles_in.shape[0]
    for flip in range(2):
        span = pl.ds(pl.multiple_of((rank ^ flip) * pairs, pairs), pairs)
        to = slice(flip * pairs, (flip + 1) * pairs)
        first, second = lists[0:1, span], lists[1:2, span]
        for at in (at_second, at_first):
            at[0:1, to] = lax.rem(first, cells)
        at_second[1:2, to] = place(second, 1)
        at_first[1:2, to] = place(second, 0)
    at_second[2:3, :cells] = counts_row[...]
    half = lists.shape[1] // 2
    span = pl.ds(pl.multiple_of((rank & 1) * half, half), half)
    source, target = lists[2:3, span], lists[3:4, span]
    for at, reduce in ((at_source, 1), (at_target, 0)):
        at[0:1, :] = lax.rem(target, cells)
        at[1:2, :] = place(source, reduce)
    near_zero[...] = jnp.zeros_like(near_zero)
    for copy in copies[-TILE_COPIES:]:
        copy.wait()


TILE_COPIES = 4
PITCH = 136
FAR_UNROLL = 64
NEAR_UNROLL = 64
PARTS = 4


def far_source_kernel(idx, mine, theirs, tiles, turned, acc, flip, lhs):
    half = mine.shape[2] // 2
    pairs = half // 2
    end = turned.shape[0]
    chunk = end // 2
    acc[...] = jnp.zeros_like(acc)
    for k in range(mine.shape[0]):
        x, y = mine[k], theirs[k]
        for h in range(2):
            at = h * half
            lhs[2 * k + h] = jnp.concatenate([x[:, at : at + half], y[:, at : at + half]], axis=0)
    for low in range(0, end, chunk):
        span = pl.ds(pl.multiple_of((lax.axis_index("rhs") & 1) * end + low, chunk), chunk)
        for i in range(pairs):
            both = [tiles[(i + h * pairs) * half : (i + h * pairs + 1) * half, span] for h in range(2)]
            flip[i * PITCH : i * PITCH + chunk, :] = jnp.concatenate(both, axis=0).astype(F32).T

        def work(g, _, low=low):
            sums = []
            at = low + g * FAR_UNROLL
            for u in range(FAR_UNROLL):
                w = flip[pl.ds(at - low + u, pairs, stride=PITCH), :]
                turned[at + u] = w.astype(BF16)
                moved = pltpu.roll(w, half, 1)
                w = jnp.concatenate([w[:, :half], moved[:, :half]], axis=0).astype(BF16)
                sums.append(dot(lhs[idx[0, at + u]], w, NAT))
            for u in range(FAR_UNROLL):
                acc[idx[1, at + u]] += sums[u]
            return 0

        lax.fori_loop(0, chunk // FAR_UNROLL, work, 0)


def far_fold_kernel(acc, keep, *sends):
    rows = keep.shape[1]
    count = sends[0].shape[0]
    for q, send in enumerate(sends):

        def fold(k, _, q=q, send=send):
            for u in range(4):
                at = q * count + 4 * k + u
                both = jnp.concatenate([acc[2 * at], acc[2 * at + 1]], axis=1)
                keep[at] = both[:rows]
                send[4 * k + u] = both[rows:]
            return 0

        lax.fori_loop(0, count // 4, fold, 0)


def far_target_kernel(stride, cells, idx, everyone, theirs, turned, keep, send, lhs, acc):
    rows, lanes = everyone.shape[1], everyone.shape[2]
    half = lanes // 2
    owners = everyone.shape[0] // stride
    acc[...] = jnp.zeros_like(acc)
    low = lax.broadcasted_iota(I32, (2 * rows, lanes), 1) < half

    def spread(o, _):
        for k in range(cells // 2):
            x = jnp.concatenate([everyone[o * stride + cells + k], theirs[o * (cells // 2) + k]], axis=0)
            y = jnp.concatenate([x[:, half:], x[:, :half]], axis=1)
            zero = jnp.zeros_like(x)
            at = o * cells + 2 * k
            lhs[at] = jnp.concatenate([jnp.where(low, x, zero), jnp.where(low, zero, y)], axis=0)
            lhs[at + 1] = jnp.concatenate([jnp.where(low, y, zero), jnp.where(low, zero, x)], axis=0)
        return 0

    lax.fori_loop(0, owners, spread, 0)

    def work(g, _):
        sums = []
        for u in range(FAR_UNROLL):
            e = g * FAR_UNROLL + u
            sums.append(dot(lhs[idx[1, e]], turned[e], TRN))
        for u in range(FAR_UNROLL):
            acc[idx[0, g * FAR_UNROLL + u]] += sums[u]
        return 0

    lax.fori_loop(0, turned.shape[0] // FAR_UNROLL, work, 0)
    for k in range(cells // 2):
        a, b = acc[2 * k], acc[2 * k + 1]
        for r, out in enumerate((keep, send)):
            at = (r * rows, (2 + r) * rows)
            out[k] = jnp.concatenate([x[i : i + rows] for x in (a, b) for i in at], axis=1)


def near_loop(idx, lhs, lhs_at, tiles, first, dims, acc, acc_at):
    count, size = tiles.shape[:2]
    rows = lhs.shape[1]
    group = min(NEAR_UNROLL, count)
    zero = jnp.zeros((rows, size), lhs.dtype)
    for low in range(0, count, group):
        high = min(low + group, count)
        sums = []
        for n in range(low, high, 2):
            a, b = (lhs[idx[lhs_at, first + n + i]] for i in range(2))
            both = jnp.concatenate([tiles[n], tiles[n + 1]], axis=0)
            if dims is TRN:
                out = dot(jnp.concatenate([a, b], axis=0), both, TRN)
                sums += [out[:rows, :size], out[rows:, size:]]
            else:
                wide = [jnp.concatenate(x, axis=1) for x in ((a, zero), (zero, b))]
                out = dot(jnp.concatenate(wide, axis=0), both, NAT)
                sums += [out[:rows], out[rows:]]
        for n in range(low, high):
            acc[idx[acc_at, first + n]] += sums[n - low]


def near_second_a_kernel(idx, mine, theirs, tiles, rest, zero, acc, both, tiles_high, sems):
    rows, size = mine.shape[1:]

    half, pairs = tiles.shape[0], rest.shape[0]
    count = (pairs - half) // TILE_COPIES
    copies = [
        pltpu.make_async_copy(
            rest.at[pl.ds(half + i * count, count)], tiles_high.at[pl.ds(i * count, count)], sems.at[i]
        )
        for i in range(TILE_COPIES)
    ]
    for copy in copies:
        copy.start()
    lane = lax.broadcasted_iota(I32, (rows, size), 1)
    for c in range(both.shape[0]):
        x = theirs[:, c * size : (c + 1) * size]
        x = jnp.where(lane < idx[2, c], x, jnp.zeros_like(x))
        both[c] = jnp.concatenate([mine[c], x], axis=0)
    near_loop(idx, both, 0, tiles, 0, NAT, acc, 1)
    for copy in copies:
        copy.wait()
    near_loop(idx, both, 0, tiles_high, half, NAT, acc, 1)


def near_second_b_kernel(
    cells, idx, both, other, before, acc, keep_a, send_a, keep_b, send_b, peak, inv
):
    rows = both.shape[1] // 2
    half = cells // 2
    owners = acc.shape[0] // cells
    stay = keep_b.shape[0] // half
    near_loop(idx, both, 0, other, other.shape[0], NAT, acc, 1)
    encode(lambda o, c: acc[o * cells + c, rows:, :], send_a, owners, half, peak, inv)

    def part_b(o, i):
        return acc[(stay + o) * cells + half + i // 2, i % 2 * rows : (i % 2 + 1) * rows, :]

    encode(part_b, send_b, owners - stay, 2 * half, peak, inv)

    def own_a(o, _):
        for c in range(half):
            keep_a[o * half + c] = acc[o * cells + c, :rows, :]
        return 0

    def own_b(o, _):
        for c in range(half):
            keep_b[o * half + c] = acc[o * cells + half + c]
        return 0

    lax.fori_loop(0, owners, own_a, 0)
    lax.fori_loop(0, stay, own_b, 0)


def near_first_kernel(stride, cells, places, idx, everyone, both, *refs):
    *parts, tiles, tiles_high, other, keep, send, lhs, acc, peak, inv = refs
    rows = everyone.shape[1]

    acc[...] = jnp.zeros_like(acc)
    lhs[:cells] = both[...]
    for part, at in zip(parts, places):
        for i, p in enumerate(at):
            for c in range(cells):
                lhs[p * cells + c] = jnp.concatenate([everyone[p * stride + c], part[i * cells + c]], axis=0)
    near_loop(idx, lhs, 1, tiles, 0, TRN, acc, 0)
    near_loop(idx, lhs, 1, tiles_high, tiles.shape[0], TRN, acc, 0)
    near_loop(idx, lhs, 1, other, other.shape[0], TRN, acc, 0)
    for c in range(cells):
        keep[c] = acc[c, :rows, :]
    encode(lambda o, c: acc[c, rows:, :], send, 1, cells, peak, inv)


def join_kernel(mine, coded, out, scale):
    count = out.shape[0]
    decode_scales(coded, count, scale)

    def one(o, _):
        for i in range(8):
            b = o * 8 + i
            out[b] = mine[b] + decode(coded, scale, b)
        return 0

    lax.fori_loop(0, count // 8, one, 0)


def meet_a_kernel(half, mine, far, *refs):
    *far_others, keep, send, acc, peak, inv = refs
    count = far_others[0].shape[0]
    owners = far.shape[0] // half
    stay = owners // 2
    for p in range(owners):
        dst, at = (keep, p) if p < stay else (acc, p - stay)
        for c in range(half):
            b = p * half + c
            dst[at * 2 * half + c] = mine[b]
            dst[at * 2 * half + half + c] = far[b] + far_others[b // count][b % count]
    encode(lambda o, i: acc[o * 8 + i], send, acc.shape[0] // 8, 8, peak, inv)


def meet_b_kernel(half, mine, coded, keep, send, acc, scale, peak, inv):
    rows = keep.shape[1]
    owners = keep.shape[0] // half
    decode_scales(coded, 2 * keep.shape[0], scale)
    for p in range(owners):
        for c in range(half):
            b = p * half + c
            keep[b] = mine[b, :rows, :] + decode(coded, scale, 2 * b)
            acc[b] = mine[b, rows:, :] + decode(coded, scale, 2 * b + 1)
    encode(lambda o, i: acc[o * 8 + i], send, acc.shape[0] // 8, 8, peak, inv)


def meet_kernel(half, mine_a, coded_a, mine_b, coded_b, keep, send, acc, scale_a, scale_b, peak, inv):
    owners = mine_b.shape[0] // half
    stay = owners // 2
    decode_scales(coded_a, mine_a.shape[0], scale_a)
    decode_scales(coded_b, mine_b.shape[0], scale_b)
    for p in range(owners):
        dst, at = (keep, p * 3) if p < stay else (acc, (p - stay) * 3)
        for c in range(half):
            a, b = p * 2 * half + c, p * half + c
            dst[at * half + c] = mine_a[a] + decode(coded_a, scale_a, a)
            dst[(at + 1) * half + c] = mine_b[b] + decode(coded_b, scale_b, b)
            a = a + half
            dst[(at + 2) * half + c] = mine_a[a] + decode(coded_a, scale_a, a)
    encode(lambda o, i: acc[o * 8 + i], send, acc.shape[0] // 8, 8, peak, inv)


def add_kernel(mine, coded, keep, send, acc, scale, peak, inv):
    total = mine.shape[0]
    half = total // 2
    decode_scales(coded, total, scale)

    def one(b, _):
        keep[b] = mine[b] + decode(coded, scale, b)
        acc[b] = mine[half + b] + decode(coded, scale, half + b)
        return 0

    lax.fori_loop(0, half, one, 0, unroll=8)
    encode(lambda o, i: acc[o * 8 + i], send, half // 8, 8, peak, inv)


def self_kernel(moved, self_tiles, out):
    for c in range(out.shape[0]):
        out[c] = dot(moved[c], self_tiles[c], TRN)


def final_kernel(
    counts, mine, coded, first, first_other, target, target_other, own, basis_t, out, scale, first_scale
):
    cells, terms, size = basis_t.shape
    rows = out.shape[0]
    decode_scales(coded, mine.shape[0], scale)
    decode_scales(first_other, cells, first_scale)
    lane = lax.broadcasted_iota(I32, (rows, size), 1)
    for k in range(cells // 2):
        b = cells + k
        fields = (mine[b] + decode(coded, scale, b) + target[k] + target_other[k]).astype(BF16)
        for h in range(2):
            c = 2 * k + h
            near = mine[c] + decode(coded, scale, c) + first[c] + decode(first_other, first_scale, c)
            far = dot(fields[:, h * terms : (h + 1) * terms], basis_t[c], NAT)
            total = near + far + own[c]
            out[:, c * size : (c + 1) * size] = jnp.where(lane < counts[c], total, jnp.zeros_like(total))


def body(
    charges,
    counts,
    self_tiles,
    basis,
    near_first,
    near_second,
    near_tiles,
    far_source,
    far_target,
    far_tiles,
):
    blks = lax.axis_size("blk")
    ranks = lax.axis_size("rhs")
    me = lax.axis_index("blk")
    rank = lax.axis_index("rhs")
    cells, size, _ = self_tiles.shape
    terms = basis.shape[2]
    rows = charges.shape[0]
    pairs = near_tiles.shape[0]
    fars = far_tiles.shape[0]
    bits = blks.bit_length() - 1
    gather_order = [0, *range(bits - 1, 0, -1)]
    reduce_order = [*range(bits - 1, -1, -1)]
    halfc = cells // 2
    stride = cells + halfc
    total = blks * cells

    def reached(at):
        mask = sum(((at >> s) & 1) << bit for s, bit in enumerate(gather_order))
        gaps = [(o ^ mask) - o for o in range(blks)]
        return min(min(g % blks, -g % blks) for g in gaps) <= -(-REACH // cells)

    early = [at for at in range(1, blks // 2) if reached(at)]
    late = [at for at in range(blks // 2, blks) if reached(at)]

    def swap_rank(x, d):
        return lax.ppermute(x, "rhs", [(i, i ^ d) for i in range(ranks)])

    def swap_blk(x, bit):
        return lax.ppermute(x, "blk", [(i, i ^ (1 << bit)) for i in range(blks)])

    def place(block, reduce):
        other = lax.div(block, cells) ^ lax.axis_index("blk")
        order = reduce_order if reduce else gather_order
        at = sum(((other >> bit) & 1) << s for s, bit in enumerate(order))
        return at * cells + lax.rem(block, cells)

    def shape(n, dtype, r=rows):
        return jax.ShapeDtypeStruct((n, r, size), dtype)

    def scratch(n, r=rows, dtype=F32):
        return pltpu.VMEM((n, r, size), dtype)

    def scales(n):
        return pltpu.VMEM((scale_blocks(n) * GROUP, size), F32)

    def whole(n, r=rows):
        return pl.BlockSpec((n, r, size), lambda i, *_: (0, 0, 0))

    def owners(x, places, begin, end):
        x = x.reshape(-1, stride, rows, size)
        runs = []
        for at in places:
            if runs and runs[-1][1] == at:
                runs[-1][1] = at + 1
            else:
                runs.append([at, at + 1])
        return jnp.concatenate([x[low:high, begin:end] for low, high in runs], axis=0).reshape(-1, rows, size)

    near_acc = shape(total, F32, 2 * rows)
    other_tiles = swap_rank(near_tiles, 1)
    charge_other = swap_rank(charges, 2)
    basis_t = jnp.swapaxes(basis, 1, 2)

    width = max(near_first.shape[0], fars)
    lists = [x.reshape(1, -1) for x in (near_first, near_second, far_source, far_target)]
    own, at_second, at_first, at_source, at_target, tiles_low, near_zero = pl.pallas_call(
        functools.partial(prep_kernel, place),
        in_specs=[HBM] * 8,
        out_specs=[VMEM] * 7,
        out_shape=[
            shape(stride, BF16),
            *[jax.ShapeDtypeStruct((r, n), I32) for r, n in ((3, 2 * pairs), (2, 2 * pairs), (2, fars // 2), (2, fars // 2))],
            shape(pairs // 2, BF16, size),
            near_acc,
        ],
        scratch_shapes=[
            pltpu.SMEM(counts.shape, I32),
            pltpu.VMEM(charges.shape, BF16),
            pltpu.VMEM(basis_t.shape, BF16),
            pltpu.VMEM((4, width), I32),
            pltpu.VMEM((1, cells), I32),
            pltpu.SemaphoreType.DMA((8 + TILE_COPIES,)),
        ],
        compiler_params=params(8),
        cost_estimate=pl.CostEstimate(flops=0, bytes_accessed=12 << 20, transcendentals=0),
        name="prep",
    )(*[in_hbm(x) for x in (counts.reshape(1, -1), charges, basis_t, *lists, near_tiles)])
    charge_own = own[:cells]
    moment_own = own[cells:]
    moment_pair = swap_rank(moment_own, 1)

    far_cost = pl.CostEstimate(flops=2 * fars * rows * terms * terms, bytes_accessed=12 << 20, transcendentals=0)
    tiles_ij = jnp.transpose(far_tiles, (1, 2, 0)).reshape(terms * terms, fars)
    near_cost = pl.CostEstimate(flops=4 * pairs * rows * size * size, bytes_accessed=10 << 20, transcendentals=0)
    first_cost = pl.CostEstimate(flops=8 * pairs * rows * size * size, bytes_accessed=20 << 20, transcendentals=0)
    coded_a = total // 2
    coded_b = blks // 2 * cells
    stay = blks // 2
    near_sum, both, tiles_high = pl.pallas_call(
        near_second_a_kernel,
        in_specs=[SMEM, VMEM, VMEM, VMEM, HBM, VMEM],
        input_output_aliases={5: 0},
        out_specs=[VMEM] * 3,
        out_shape=[near_acc, shape(cells, BF16, 2 * rows), shape(pairs - pairs // 2, BF16, size)],
        scratch_shapes=[pltpu.SemaphoreType.DMA((TILE_COPIES,))],
        compiler_params=params(4),
        cost_estimate=near_cost,
        name="near_second_a",
    )(at_second, charge_own, charge_other, tiles_low, in_hbm(near_tiles), near_zero)

    received = swap_blk(own, gather_order[0])
    received, near_sum = lax.optimization_barrier((received, near_sum))
    gathered = jnp.concatenate([own, received], axis=0)
    received = swap_blk(gathered, gather_order[1])
    near_sum, _ = lax.optimization_barrier((near_sum, gathered))

    _, keep_a, send_a, keep_b, send_b = pl.pallas_call(
        functools.partial(near_second_b_kernel, cells),
        in_specs=[SMEM, VMEM, VMEM, VMEM],
        out_specs=[VMEM] * 5,
        out_shape=[
            near_acc,
            shape(coded_a, F32),
            shape(coded_a + scale_blocks(coded_a), I16),
            shape(stay * halfc, F32, 2 * rows),
            shape(coded_b + scale_blocks(coded_b), I16),
        ],
        scratch_shapes=[
            scales(max(coded_a, coded_b)),
            scales(max(coded_a, coded_b)),
        ],
        input_output_aliases={3: 0},
        compiler_params=params(8),
        cost_estimate=near_cost,
        name="near_second_b",
    )(at_second, both, other_tiles, near_sum)
    moment_late, _ = lax.optimization_barrier((moment_pair, send_a))
    far_scratch = [
        pltpu.VMEM((terms // 2 * PITCH, size), F32),
        pltpu.VMEM((cells, 2 * rows, terms), BF16),
    ]
    far_sums = jax.ShapeDtypeStruct((total, 2 * rows, terms), F32)
    turned, far_acc = pl.pallas_call(
        far_source_kernel,
        in_specs=[SMEM] + [VMEM] * 3,
        out_specs=[VMEM] * 2,
        out_shape=[shape(fars // 2, BF16, terms // 2), far_sums],
        scratch_shapes=far_scratch,
        compiler_params=params(6),
        cost_estimate=far_cost,
        name="far_source",
    )(at_source, moment_own, moment_late, tiles_ij)
    received, far_acc = lax.optimization_barrier((received, far_acc))
    others, places = [], []
    for s, bit in enumerate(gather_order):
        if s > 1:
            received = swap_blk(gathered, bit)
        if 0 < s < bits - 1:
            gathered = jnp.concatenate([gathered, received], axis=0)
    places.append(early)
    others.append(swap_rank(owners(gathered, early, 0, cells), 2))
    far_acc, _ = lax.optimization_barrier((far_acc, gathered))
    far_keep, *far_sends = pl.pallas_call(
        far_fold_kernel,
        in_specs=[VMEM],
        out_specs=[VMEM] * (1 + PARTS),
        out_shape=[shape(total // 2, F32), *[shape(total // 2 // PARTS, F32)] * PARTS],
        compiler_params=params(4),
        cost_estimate=far_cost,
        name="far_fold",
    )(far_acc)
    far_others = [swap_rank(x, 1) for x in far_sends]

    got_a = swap_rank(send_a, 2)
    got_b = swap_blk(send_b, reduce_order[-1])
    got_b, got_a = lax.optimization_barrier((got_b, got_a))
    half_a = blks // 2 * cells
    half_b = blks // 2 * halfc
    meet_cost = pl.CostEstimate(flops=0, bytes_accessed=1 << 20, transcendentals=0)
    keep_b, send_b = pl.pallas_call(
        functools.partial(meet_b_kernel, halfc),
        in_specs=[VMEM] * 2,
        out_specs=[VMEM] * 2,
        out_shape=[shape(half_b, F32), shape(half_b + scale_blocks(half_b), I16)],
        scratch_shapes=[scratch(half_b), scales(coded_b), scales(half_b), scales(half_b)],
        compiler_params=params(8 + total // 16),
        cost_estimate=meet_cost,
        name="meet_b",
    )(keep_b, got_b)
    keep_a, _, others[0] = lax.optimization_barrier((keep_a, send_b, others[0]))
    got_b = swap_rank(send_b, 2)
    received, got_b = lax.optimization_barrier((received, got_b))
    gathered = jnp.concatenate([gathered, received], axis=0)
    places.append(late)
    others.append(swap_rank(owners(received, [at - blks // 2 for at in late], 0, cells), 2))
    joined = pl.pallas_call(
        join_kernel,
        in_specs=[VMEM] * 2,
        out_specs=VMEM,
        out_shape=shape(coded_a, F32),
        scratch_shapes=[scales(coded_a)],
        compiler_params=params(8),
        cost_estimate=pl.CostEstimate(flops=0, bytes_accessed=3 << 20, transcendentals=0),
        name="join",
    )(keep_a, got_a)
    keep_a, send_a = pl.pallas_call(
        functools.partial(meet_a_kernel, halfc),
        in_specs=[VMEM] * (2 + PARTS),
        out_specs=[VMEM] * 2,
        out_shape=[shape(half_a, F32), shape(half_a + scale_blocks(half_a), I16)],
        scratch_shapes=[scratch(half_a), scales(half_a), scales(half_a)],
        compiler_params=params(8 + total // 16),
        cost_estimate=meet_cost,
        name="meet_a",
    )(joined, far_keep, *far_others)
    got_a = swap_blk(send_a, reduce_order[-1])

    moment_all_pair = swap_rank(owners(gathered, range(blks), cells, stride), 1)
    target_keep, target_send = pl.pallas_call(
        functools.partial(far_target_kernel, stride, cells),
        in_specs=[SMEM] + [VMEM] * 3,
        out_specs=[VMEM] * 2,
        out_shape=[shape(halfc, F32), shape(halfc, F32)],
        scratch_shapes=[
            scratch(total, 4 * rows, BF16),
            pltpu.VMEM((cells, 4 * rows, terms // 2), F32),
        ],
        compiler_params=params(6 + total // 32),
        cost_estimate=meet_cost,
        name="far_target",
    )(at_target, gathered, moment_all_pair, turned)
    target_other = swap_rank(target_send, 1)
    others[0], _ = lax.optimization_barrier((others[0], target_send))

    got_a, got_b, _ = lax.optimization_barrier((got_a, got_b, target_send))

    half = blks // 4 * stride
    keep, send = pl.pallas_call(
        functools.partial(meet_kernel, halfc),
        in_specs=[VMEM] * 4,
        out_specs=[VMEM] * 2,
        out_shape=[shape(half, F32), shape(half + scale_blocks(half), I16)],
        scratch_shapes=[scratch(half), scales(half_a), scales(half_b), scales(half), scales(half)],
        compiler_params=params(8 + total // 16),
        cost_estimate=meet_cost,
        name="meet",
    )(keep_a, got_a, keep_b, got_b)
    coded = swap_blk(send, reduce_order[-2])

    for bit in reversed(reduce_order[:-2]):
        now, half = half, half // 2
        keep, send = pl.pallas_call(
            add_kernel,
            in_specs=[VMEM] * 2,
            out_specs=[VMEM] * 2,
            out_shape=[shape(half, F32), shape(half + scale_blocks(half), I16)],
            scratch_shapes=[scratch(half), scales(now), scales(half), scales(half)],
            compiler_params=params(8 + total // 16),
            name="add",
        )(keep, coded)
        if bit != reduce_order[0]:
            coded = swap_blk(send, bit)

    first_keep, first_send = pl.pallas_call(
        functools.partial(near_first_kernel, stride, cells, places),
        in_specs=[SMEM] + [VMEM] * (5 + len(others)),
        out_specs=[VMEM, VMEM],
        out_shape=[shape(cells, F32), shape(cells + scale_blocks(cells), I16)],
        scratch_shapes=[
            scratch(total, 2 * rows, BF16),
            scratch(cells, 2 * rows),
            scales(cells),
            scales(cells),
        ],
        compiler_params=params(4 + total // 32),
        cost_estimate=first_cost,
        name="near_first",
    )(at_first, gathered, both, *others, tiles_low, tiles_high, other_tiles)
    first_send, send = lax.optimization_barrier((first_send, send))
    first_other = swap_rank(first_send, 2)
    coded = swap_blk(send, reduce_order[0])

    own_part = pl.pallas_call(
        self_kernel,
        in_specs=[VMEM] * 2,
        out_specs=VMEM,
        out_shape=shape(cells, F32),
        compiler_params=params(8),
        cost_estimate=meet_cost,
        name="self",
    )(charge_own, self_tiles)

    return pl.pallas_call(
        final_kernel,
        in_specs=[SMEM] + [VMEM] * 8,
        out_specs=VMEM,
        out_shape=jax.ShapeDtypeStruct(charges.shape, F32),
        scratch_shapes=[scales(stride), scales(cells)],
        compiler_params=params(8),
        name="final",
    )(
        counts, keep, coded, first_keep, first_other, target_keep, target_other, own_part, basis_t
    )


def solution(mesh):
    in_specs = (
        P("rhs", "blk"),
        P("blk"),
        P("blk", None, None),
        P("blk", None, None),
        P("blk"),
        P("blk"),
        P(("blk", "rhs"), None, None),
        P("blk"),
        P("blk"),
        P("blk", None, None),
    )
    out_specs = P("rhs", "blk")
    return jax.shard_map(body, mesh=mesh, in_specs=in_specs, out_specs=out_specs, check_vma=False)
```

```python
import functools

import jax
import jax.numpy as jnp
from jax import lax
from jax.experimental import pallas as pl
from jax.experimental.pallas import tpu as pltpu
from jax.sharding import PartitionSpec as P

F32, BF16, I16, I32 = jnp.float32, jnp.bfloat16, jnp.int16, jnp.int32
REACH = 48
GROUP = 16
TOP = 32767.0
VMEM = pl.BlockSpec(memory_space=pltpu.VMEM)
SMEM = pl.BlockSpec(memory_space=pltpu.SMEM)
HBM = pl.BlockSpec(memory_space=pltpu.HBM)
NAT = (((1,), (0,)), ((), ()))
TRN = (((1,), (1,)), ((), ()))


def params(mib):
    return pltpu.CompilerParams(vmem_limit_bytes=mib << 20)


def in_hbm(x):
    return pltpu.with_memory_space_constraint(x, pltpu.HBM)


def dot(lhs, rhs, dims):
    return lax.dot_general(lhs, rhs, dims, preferred_element_type=F32)


def scale_blocks(count):
    return -(-count // GROUP)


def encode(get, out, outer, inner, peak, inv):
    count = outer * inner
    peak[...] = jnp.zeros_like(peak)

    def find(o, _):
        for i in range(inner):
            peak[pl.ds(o * inner + i, 1), :] = jnp.max(jnp.abs(get(o, i)), axis=0, keepdims=True)
        return 0

    lax.fori_loop(0, outer, find, 0)
    code = jnp.ceil(jnp.log2(jnp.maximum(peak[...], 1e-30)) * 8.0) + 1.0
    inv[...] = TOP * jnp.exp2(code * -0.125)
    for s in range(scale_blocks(count)):
        out[count + s] = code[s * GROUP : (s + 1) * GROUP].astype(I32).astype(I16)

    def put(o, _):
        for i in range(inner):
            b = o * inner + i
            out[b] = jnp.round(get(o, i) * inv[pl.ds(b, 1), :]).astype(I32).astype(I16)
        return 0

    lax.fori_loop(0, outer, put, 0)


def decode_scales(coded, count, scale):
    for s in range(scale_blocks(count)):
        code = coded[count + s].astype(I32).astype(F32)
        scale[s * GROUP : (s + 1) * GROUP, :] = jnp.exp2(code * 0.125) * (1.0 / TOP)


def decode(coded, scale, b):
    return coded[b].astype(I32).astype(F32) * scale[pl.ds(b, 1), :]


def prep_kernel(
    place, counts_in, charges_in, basis_in, near_first, near_second, far_source, far_target, tiles_in,
    out, at_second, at_first, at_source, at_target, tiles, near_zero, counts, charges, basis_t, lists, counts_row, sems,
):
    moves = [(counts_in.at[0], counts), (charges_in, charges), (basis_in, basis_t), (counts_in, counts_row)]
    moves += [
        (src, lists.at[pl.ds(i, 1)]) for i, src in enumerate((near_first, near_second, far_source, far_target))
    ]
    count = tiles.shape[0] // TILE_COPIES
    spans = [pl.ds(i * count, count) for i in range(TILE_COPIES)]
    moves += [(tiles_in.at[span], tiles.at[span]) for span in spans]
    copies = [pltpu.make_async_copy(src, dst, sems.at[i]) for i, (src, dst) in enumerate(moves)]
    for copy in copies:
        copy.start()
    for copy in copies[:-TILE_COPIES]:
        copy.wait()
    cells, terms, size = basis_t.shape
    rows = charges.shape[0]
    lane = lax.broadcasted_iota(I32, (rows, size), 1)
    moments = []
    for c in range(cells):
        x = charges[:, c * size : (c + 1) * size]
        x = jnp.where(lane < counts[c], x, jnp.zeros_like(x))
        out[c] = x
        moments.append(dot(x, basis_t[c], TRN))
    for k in range(cells // 2):
        out[cells + k] = jnp.concatenate(moments[2 * k : 2 * k + 2], axis=1).astype(BF16)
    rank = lax.axis_index("rhs")
    pairs = tiles_in.shape[0]
    for flip in range(2):
        span = pl.ds(pl.multiple_of((rank ^ flip) * pairs, pairs), pairs)
        to = slice(flip * pairs, (flip + 1) * pairs)
        first, second = lists[0:1, span], lists[1:2, span]
        for at in (at_second, at_first):
            at[0:1, to] = lax.rem(first, cells)
        at_second[1:2, to] = place(second, 1)
        at_first[1:2, to] = place(second, 0)
    at_second[2:3, :cells] = counts_row[...]
    half = lists.shape[1] // 2
    span = pl.ds(pl.multiple_of((rank & 1) * half, half), half)
    source, target = lists[2:3, span], lists[3:4, span]
    for at, reduce in ((at_source, 1), (at_target, 0)):
        at[0:1, :] = lax.rem(target, cells)
        at[1:2, :] = place(source, reduce)
    near_zero[...] = jnp.zeros_like(near_zero)
    for copy in copies[-TILE_COPIES:]:
        copy.wait()


TILE_COPIES = 4
PITCH = 132
FAR_UNROLL = 64
NEAR_UNROLL = 32
PARTS = 4


def far_source_kernel(idx, mine, theirs, tiles, turned, acc, flip, lhs):
    half = mine.shape[2] // 2
    pairs = half // 2
    end = turned.shape[0]
    chunk = end // 2
    acc[...] = jnp.zeros_like(acc)
    for k in range(mine.shape[0]):
        x, y = mine[k], theirs[k]
        for h in range(2):
            at = h * half
            lhs[2 * k + h] = jnp.concatenate([x[:, at : at + half], y[:, at : at + half]], axis=0)
    for low in range(0, end, chunk):
        span = pl.ds(pl.multiple_of((lax.axis_index("rhs") & 1) * end + low, chunk), chunk)
        for i in range(pairs):
            both = [tiles[(i + h * pairs) * half : (i + h * pairs + 1) * half, span] for h in range(2)]
            flip[i * PITCH : i * PITCH + chunk, :] = jnp.concatenate(both, axis=0).astype(F32).T

        def work(g, _, low=low):
            sums = []
            at = low + g * FAR_UNROLL
            for u in range(FAR_UNROLL):
                w = flip[pl.ds(at - low + u, pairs, stride=PITCH), :]
                turned[at + u] = w.astype(BF16)
                moved = pltpu.roll(w, half, 1)
                w = jnp.concatenate([w[:, :half], moved[:, :half]], axis=0).astype(BF16)
                sums.append(dot(lhs[idx[0, at + u]], w, NAT))
            for u in range(FAR_UNROLL):
                acc[idx[1, at + u]] += sums[u]
            return 0

        lax.fori_loop(0, chunk // FAR_UNROLL, work, 0)


def far_fold_kernel(acc, keep, *sends):
    rows = keep.shape[1]
    count = sends[0].shape[0]
    for q, send in enumerate(sends):

        def fold(k, _, q=q, send=send):
            for u in range(4):
                at = q * count + 4 * k + u
                both = jnp.concatenate([acc[2 * at], acc[2 * at + 1]], axis=1)
                keep[at] = both[:rows]
                send[4 * k + u] = both[rows:]
            return 0

        lax.fori_loop(0, count // 4, fold, 0)


def far_target_kernel(stride, cells, idx, everyone, theirs, turned, keep, send, lhs, acc):
    rows, lanes = everyone.shape[1], everyone.shape[2]
    half = lanes // 2
    owners = everyone.shape[0] // stride
    acc[...] = jnp.zeros_like(acc)
    low = lax.broadcasted_iota(I32, (2 * rows, lanes), 1) < half

    def spread(o, _):
        for k in range(cells // 2):
            x = jnp.concatenate([everyone[o * stride + cells + k], theirs[o * (cells // 2) + k]], axis=0)
            y = jnp.concatenate([x[:, half:], x[:, :half]], axis=1)
            zero = jnp.zeros_like(x)
            at = o * cells + 2 * k
            lhs[at] = jnp.concatenate([jnp.where(low, x, zero), jnp.where(low, zero, y)], axis=0)
            lhs[at + 1] = jnp.concatenate([jnp.where(low, y, zero), jnp.where(low, zero, x)], axis=0)
        return 0

    lax.fori_loop(0, owners, spread, 0)

    def work(g, _):
        sums = []
        for u in range(FAR_UNROLL):
            e = g * FAR_UNROLL + u
            sums.append(dot(lhs[idx[1, e]], turned[e], TRN))
        for u in range(FAR_UNROLL):
            acc[idx[0, g * FAR_UNROLL + u]] += sums[u]
        return 0

    lax.fori_loop(0, turned.shape[0] // FAR_UNROLL, work, 0)
    for k in range(cells // 2):
        a, b = acc[2 * k], acc[2 * k + 1]
        for r, out in enumerate((keep, send)):
            at = (r * rows, (2 + r) * rows)
            out[k] = jnp.concatenate([x[i : i + rows] for x in (a, b) for i in at], axis=1)


def near_loop(idx, lhs, lhs_at, tiles, first, dims, acc, acc_at):
    count, size = tiles.shape[:2]
    rows = lhs.shape[1]
    group = min(NEAR_UNROLL, count)
    zero = jnp.zeros((rows, size), lhs.dtype)
    for low in range(0, count, group):
        high = min(low + group, count)
        sums = []
        for n in range(low, high, 2):
            a, b = (lhs[idx[lhs_at, first + n + i]] for i in range(2))
            both = jnp.concatenate([tiles[n], tiles[n + 1]], axis=0)
            if dims is TRN:
                out = dot(jnp.concatenate([a, b], axis=0), both, TRN)
                sums += [out[:rows, :size], out[rows:, size:]]
            else:
                wide = [jnp.concatenate(x, axis=1) for x in ((a, zero), (zero, b))]
                out = dot(jnp.concatenate(wide, axis=0), both, NAT)
                sums += [out[:rows], out[rows:]]
        for n in range(low, high):
            acc[idx[acc_at, first + n]] += sums[n - low]


def near_second_a_kernel(idx, mine, theirs, tiles, rest, zero, acc, both, tiles_high, sems):
    rows, size = mine.shape[1:]

    half, pairs = tiles.shape[0], rest.shape[0]
    count = (pairs - half) // TILE_COPIES
    copies = [
        pltpu.make_async_copy(
            rest.at[pl.ds(half + i * count, count)], tiles_high.at[pl.ds(i * count, count)], sems.at[i]
        )
        for i in range(TILE_COPIES)
    ]
    for copy in copies:
        copy.start()
    lane = lax.broadcasted_iota(I32, (rows, size), 1)
    for c in range(both.shape[0]):
        x = theirs[:, c * size : (c + 1) * size]
        x = jnp.where(lane < idx[2, c], x, jnp.zeros_like(x))
        both[c] = jnp.concatenate([mine[c], x], axis=0)
    near_loop(idx, both, 0, tiles, 0, NAT, acc, 1)
    for copy in copies:
        copy.wait()
    near_loop(idx, both, 0, tiles_high, half, NAT, acc, 1)


def near_second_b_kernel(
    cells, idx, both, other, before, acc, keep_a, send_a, keep_b, send_b, peak, inv
):
    rows = both.shape[1] // 2
    half = cells // 2
    owners = acc.shape[0] // cells
    stay = keep_b.shape[0] // half
    near_loop(idx, both, 0, other, other.shape[0], NAT, acc, 1)
    encode(lambda o, c: acc[o * cells + c, rows:, :], send_a, owners, half, peak, inv)

    def part_b(o, i):
        return acc[(stay + o) * cells + half + i // 2, i % 2 * rows : (i % 2 + 1) * rows, :]

    encode(part_b, send_b, owners - stay, 2 * half, peak, inv)

    def own_a(o, _):
        for c in range(half):
            keep_a[o * half + c] = acc[o * cells + c, :rows, :]
        return 0

    def own_b(o, _):
        for c in range(half):
            keep_b[o * half + c] = acc[o * cells + half + c]
        return 0

    lax.fori_loop(0, owners, own_a, 0)
    lax.fori_loop(0, stay, own_b, 0)


def near_first_kernel(stride, cells, places, idx, everyone, both, *refs):
    *parts, tiles, tiles_high, other, keep, send, lhs, acc, peak, inv = refs
    rows = everyone.shape[1]

    acc[...] = jnp.zeros_like(acc)
    lhs[:cells] = both[...]
    for part, at in zip(parts, places):
        for i, p in enumerate(at):
            for c in range(cells):
                lhs[p * cells + c] = jnp.concatenate([everyone[p * stride + c], part[i * cells + c]], axis=0)
    near_loop(idx, lhs, 1, tiles, 0, TRN, acc, 0)
    near_loop(idx, lhs, 1, tiles_high, tiles.shape[0], TRN, acc, 0)
    near_loop(idx, lhs, 1, other, other.shape[0], TRN, acc, 0)
    for c in range(cells):
        keep[c] = acc[c, :rows, :]
    encode(lambda o, c: acc[c, rows:, :], send, 1, cells, peak, inv)


def join_kernel(mine, coded, out, scale):
    count = out.shape[0]
    decode_scales(coded, count, scale)

    def one(o, _):
        for i in range(8):
            b = o * 8 + i
            out[b] = mine[b] + decode(coded, scale, b)
        return 0

    lax.fori_loop(0, count // 8, one, 0)


def meet_a_kernel(half, mine, far, *refs):
    *far_others, keep, send, acc, peak, inv = refs
    count = far_others[0].shape[0]
    owners = far.shape[0] // half
    stay = owners // 2
    for p in range(owners):
        dst, at = (keep, p) if p < stay else (acc, p - stay)
        for c in range(half):
            b = p * half + c
            dst[at * 2 * half + c] = mine[b]
            dst[at * 2 * half + half + c] = far[b] + far_others[b // count][b % count]
    encode(lambda o, i: acc[o * 8 + i], send, acc.shape[0] // 8, 8, peak, inv)


def meet_b_kernel(half, mine, coded, keep, send, acc, scale, peak, inv):
    rows = keep.shape[1]
    owners = keep.shape[0] // half
    decode_scales(coded, 2 * keep.shape[0], scale)
    for p in range(owners):
        for c in range(half):
            b = p * half + c
            keep[b] = mine[b, :rows, :] + decode(coded, scale, 2 * b)
            acc[b] = mine[b, rows:, :] + decode(coded, scale, 2 * b + 1)
    encode(lambda o, i: acc[o * 8 + i], send, acc.shape[0] // 8, 8, peak, inv)


def meet_kernel(half, mine_a, coded_a, mine_b, coded_b, keep, send, acc, scale_a, scale_b, peak, inv):
    owners = mine_b.shape[0] // half
    stay = owners // 2
    decode_scales(coded_a, mine_a.shape[0], scale_a)
    decode_scales(coded_b, mine_b.shape[0], scale_b)
    for p in range(owners):
        dst, at = (keep, p * 3) if p < stay else (acc, (p - stay) * 3)
        for c in range(half):
            a, b = p * 2 * half + c, p * half + c
            dst[at * half + c] = mine_a[a] + decode(coded_a, scale_a, a)
            dst[(at + 1) * half + c] = mine_b[b] + decode(coded_b, scale_b, b)
            a = a + half
            dst[(at + 2) * half + c] = mine_a[a] + decode(coded_a, scale_a, a)
    encode(lambda o, i: acc[o * 8 + i], send, acc.shape[0] // 8, 8, peak, inv)


def add_kernel(mine, coded, keep, send, acc, scale, peak, inv):
    total = mine.shape[0]
    half = total // 2
    decode_scales(coded, total, scale)

    def one(b, _):
        keep[b] = mine[b] + decode(coded, scale, b)
        acc[b] = mine[half + b] + decode(coded, scale, half + b)
        return 0

    lax.fori_loop(0, half, one, 0, unroll=8)
    encode(lambda o, i: acc[o * 8 + i], send, half // 8, 8, peak, inv)


def self_kernel(moved, self_tiles, out):
    for c in range(out.shape[0]):
        out[c] = dot(moved[c], self_tiles[c], TRN)


def final_kernel(
    counts, mine, coded, first, first_other, target, target_other, own, basis_t, out, scale, first_scale
):
    cells, terms, size = basis_t.shape
    rows = out.shape[0]
    decode_scales(coded, mine.shape[0], scale)
    decode_scales(first_other, cells, first_scale)
    lane = lax.broadcasted_iota(I32, (rows, size), 1)
    for k in range(cells // 2):
        b = cells + k
        fields = (mine[b] + decode(coded, scale, b) + target[k] + target_other[k]).astype(BF16)
        for h in range(2):
            c = 2 * k + h
            near = mine[c] + decode(coded, scale, c) + first[c] + decode(first_other, first_scale, c)
            far = dot(fields[:, h * terms : (h + 1) * terms], basis_t[c], NAT)
            total = near + far + own[c]
            out[:, c * size : (c + 1) * size] = jnp.where(lane < counts[c], total, jnp.zeros_like(total))


def body(
    charges,
    counts,
    self_tiles,
    basis,
    near_first,
    near_second,
    near_tiles,
    far_source,
    far_target,
    far_tiles,
):
    blks = lax.axis_size("blk")
    ranks = lax.axis_size("rhs")
    me = lax.axis_index("blk")
    rank = lax.axis_index("rhs")
    cells, size, _ = self_tiles.shape
    terms = basis.shape[2]
    rows = charges.shape[0]
    pairs = near_tiles.shape[0]
    fars = far_tiles.shape[0]
    bits = blks.bit_length() - 1
    gather_order = [0, *range(bits - 1, 0, -1)]
    reduce_order = [*range(bits - 1, -1, -1)]
    halfc = cells // 2
    stride = cells + halfc
    total = blks * cells

    def reached(at):
        mask = sum(((at >> s) & 1) << bit for s, bit in enumerate(gather_order))
        gaps = [(o ^ mask) - o for o in range(blks)]
        return min(min(g % blks, -g % blks) for g in gaps) <= -(-REACH // cells)

    early = [at for at in range(1, blks // 2) if reached(at)]
    late = [at for at in range(blks // 2, blks) if reached(at)]

    def swap_rank(x, d):
        return lax.ppermute(x, "rhs", [(i, i ^ d) for i in range(ranks)])

    def swap_blk(x, bit):
        return lax.ppermute(x, "blk", [(i, i ^ (1 << bit)) for i in range(blks)])

    def place(block, reduce):
        other = lax.div(block, cells) ^ lax.axis_index("blk")
        order = reduce_order if reduce else gather_order
        at = sum(((other >> bit) & 1) << s for s, bit in enumerate(order))
        return at * cells + lax.rem(block, cells)

    def shape(n, dtype, r=rows):
        return jax.ShapeDtypeStruct((n, r, size), dtype)

    def scratch(n, r=rows, dtype=F32):
        return pltpu.VMEM((n, r, size), dtype)

    def scales(n):
        return pltpu.VMEM((scale_blocks(n) * GROUP, size), F32)

    def whole(n, r=rows):
        return pl.BlockSpec((n, r, size), lambda i, *_: (0, 0, 0))

    def owners(x, places, begin, end):
        x = x.reshape(-1, stride, rows, size)
        runs = []
        for at in places:
            if runs and runs[-1][1] == at:
                runs[-1][1] = at + 1
            else:
                runs.append([at, at + 1])
        return jnp.concatenate([x[low:high, begin:end] for low, high in runs], axis=0).reshape(-1, rows, size)

    near_acc = shape(total, F32, 2 * rows)
    other_tiles = swap_rank(near_tiles, 1)
    charge_other = swap_rank(charges, 2)
    basis_t = jnp.swapaxes(basis, 1, 2)

    width = max(near_first.shape[0], fars)
    lists = [x.reshape(1, -1) for x in (near_first, near_second, far_source, far_target)]
    own, at_second, at_first, at_source, at_target, tiles_low, near_zero = pl.pallas_call(
        functools.partial(prep_kernel, place),
        in_specs=[HBM] * 8,
        out_specs=[VMEM] * 7,
        out_shape=[
            shape(stride, BF16),
            *[jax.ShapeDtypeStruct((r, n), I32) for r, n in ((3, 2 * pairs), (2, 2 * pairs), (2, fars // 2), (2, fars // 2))],
            shape(pairs // 2, BF16, size),
            near_acc,
        ],
        scratch_shapes=[
            pltpu.SMEM(counts.shape, I32),
            pltpu.VMEM(charges.shape, BF16),
            pltpu.VMEM(basis_t.shape, BF16),
            pltpu.VMEM((4, width), I32),
            pltpu.VMEM((1, cells), I32),
            pltpu.SemaphoreType.DMA((8 + TILE_COPIES,)),
        ],
        compiler_params=params(8),
        cost_estimate=pl.CostEstimate(flops=0, bytes_accessed=12 << 20, transcendentals=0),
        name="prep",
    )(*[in_hbm(x) for x in (counts.reshape(1, -1), charges, basis_t, *lists, near_tiles)])
    charge_own = own[:cells]
    moment_own = own[cells:]
    moment_pair = swap_rank(moment_own, 1)

    far_cost = pl.CostEstimate(flops=2 * fars * rows * terms * terms, bytes_accessed=12 << 20, transcendentals=0)
    tiles_ij = jnp.transpose(far_tiles, (1, 2, 0)).reshape(terms * terms, fars)
    near_cost = pl.CostEstimate(flops=4 * pairs * rows * size * size, bytes_accessed=10 << 20, transcendentals=0)
    first_cost = pl.CostEstimate(flops=8 * pairs * rows * size * size, bytes_accessed=20 << 20, transcendentals=0)
    coded_a = total // 2
    coded_b = blks // 2 * cells
    stay = blks // 2
    near_sum, both, tiles_high = pl.pallas_call(
        near_second_a_kernel,
        in_specs=[SMEM, VMEM, VMEM, VMEM, HBM, VMEM],
        input_output_aliases={5: 0},
        out_specs=[VMEM] * 3,
        out_shape=[near_acc, shape(cells, BF16, 2 * rows), shape(pairs - pairs // 2, BF16, size)],
        scratch_shapes=[pltpu.SemaphoreType.DMA((TILE_COPIES,))],
        compiler_params=params(4),
        cost_estimate=near_cost,
        name="near_second_a",
    )(at_second, charge_own, charge_other, tiles_low, in_hbm(near_tiles), near_zero)

    received = swap_blk(own, gather_order[0])
    received, near_sum = lax.optimization_barrier((received, near_sum))
    gathered = jnp.concatenate([own, received], axis=0)
    received = swap_blk(gathered, gather_order[1])
    near_sum, _ = lax.optimization_barrier((near_sum, gathered))

    _, keep_a, send_a, keep_b, send_b = pl.pallas_call(
        functools.partial(near_second_b_kernel, cells),
        in_specs=[SMEM, VMEM, VMEM, VMEM],
        out_specs=[VMEM] * 5,
        out_shape=[
            near_acc,
            shape(coded_a, F32),
            shape(coded_a + scale_blocks(coded_a), I16),
            shape(stay * halfc, F32, 2 * rows),
            shape(coded_b + scale_blocks(coded_b), I16),
        ],
        scratch_shapes=[
            scales(max(coded_a, coded_b)),
            scales(max(coded_a, coded_b)),
        ],
        input_output_aliases={3: 0},
        compiler_params=params(8),
        cost_estimate=near_cost,
        name="near_second_b",
    )(at_second, both, other_tiles, near_sum)
    moment_late, _ = lax.optimization_barrier((moment_pair, send_a))
    far_scratch = [
        pltpu.VMEM((terms // 2 * PITCH, size), F32),
        pltpu.VMEM((cells, 2 * rows, terms), BF16),
    ]
    far_sums = jax.ShapeDtypeStruct((total, 2 * rows, terms), F32)
    turned, far_acc = pl.pallas_call(
        far_source_kernel,
        in_specs=[SMEM] + [VMEM] * 3,
        out_specs=[VMEM] * 2,
        out_shape=[shape(fars // 2, BF16, terms // 2), far_sums],
        scratch_shapes=far_scratch,
        compiler_params=params(6),
        cost_estimate=far_cost,
        name="far_source",
    )(at_source, moment_own, moment_late, tiles_ij)
    received, far_acc = lax.optimization_barrier((received, far_acc))
    others, places = [], []
    for s, bit in enumerate(gather_order):
        if s > 1:
            received = swap_blk(gathered, bit)
        if 0 < s < bits - 1:
            gathered = jnp.concatenate([gathered, received], axis=0)
    places.append(early)
    others.append(swap_rank(owners(gathered, early, 0, cells), 2))
    far_acc, _ = lax.optimization_barrier((far_acc, gathered))
    far_keep, *far_sends = pl.pallas_call(
        far_fold_kernel,
        in_specs=[VMEM],
        out_specs=[VMEM] * (1 + PARTS),
        out_shape=[shape(total // 2, F32), *[shape(total // 2 // PARTS, F32)] * PARTS],
        compiler_params=params(4),
        cost_estimate=far_cost,
        name="far_fold",
    )(far_acc)
    far_others = [swap_rank(x, 1) for x in far_sends]

    got_a = swap_rank(send_a, 2)
    got_b = swap_blk(send_b, reduce_order[-1])
    got_b, got_a = lax.optimization_barrier((got_b, got_a))
    half_a = blks // 2 * cells
    half_b = blks // 2 * halfc
    meet_cost = pl.CostEstimate(flops=0, bytes_accessed=1 << 20, transcendentals=0)
    keep_b, send_b = pl.pallas_call(
        functools.partial(meet_b_kernel, halfc),
        in_specs=[VMEM] * 2,
        out_specs=[VMEM] * 2,
        out_shape=[shape(half_b, F32), shape(half_b + scale_blocks(half_b), I16)],
        scratch_shapes=[scratch(half_b), scales(coded_b), scales(half_b), scales(half_b)],
        compiler_params=params(8 + total // 16),
        cost_estimate=meet_cost,
        name="meet_b",
    )(keep_b, got_b)
    keep_a, _, others[0] = lax.optimization_barrier((keep_a, send_b, others[0]))
    got_b = swap_rank(send_b, 2)
    received, got_b = lax.optimization_barrier((received, got_b))
    gathered = jnp.concatenate([gathered, received], axis=0)
    places.append(late)
    others.append(swap_rank(owners(received, [at - blks // 2 for at in late], 0, cells), 2))
    joined = pl.pallas_call(
        join_kernel,
        in_specs=[VMEM] * 2,
        out_specs=VMEM,
        out_shape=shape(coded_a, F32),
        scratch_shapes=[scales(coded_a)],
        compiler_params=params(8),
        cost_estimate=pl.CostEstimate(flops=0, bytes_accessed=3 << 20, transcendentals=0),
        name="join",
    )(keep_a, got_a)
    keep_a, send_a = pl.pallas_call(
        functools.partial(meet_a_kernel, halfc),
        in_specs=[VMEM] * (2 + PARTS),
        out_specs=[VMEM] * 2,
        out_shape=[shape(half_a, F32), shape(half_a + scale_blocks(half_a), I16)],
        scratch_shapes=[scratch(half_a), scales(half_a), scales(half_a)],
        compiler_params=params(8 + total // 16),
        cost_estimate=meet_cost,
        name="meet_a",
    )(joined, far_keep, *far_others)
    got_a = swap_blk(send_a, reduce_order[-1])

    moment_all_pair = swap_rank(owners(gathered, range(blks), cells, stride), 1)
    target_keep, target_send = pl.pallas_call(
        functools.partial(far_target_kernel, stride, cells),
        in_specs=[SMEM] + [VMEM] * 3,
        out_specs=[VMEM] * 2,
        out_shape=[shape(halfc, F32), shape(halfc, F32)],
        scratch_shapes=[
            scratch(total, 4 * rows, BF16),
            pltpu.VMEM((cells, 4 * rows, terms // 2), F32),
        ],
        compiler_params=params(6 + total // 32),
        cost_estimate=meet_cost,
        name="far_target",
    )(at_target, gathered, moment_all_pair, turned)
    target_other = swap_rank(target_send, 1)
    others[0], _ = lax.optimization_barrier((others[0], target_send))

    got_a, got_b, _ = lax.optimization_barrier((got_a, got_b, target_send))

    half = blks // 4 * stride
    keep, send = pl.pallas_call(
        functools.partial(meet_kernel, halfc),
        in_specs=[VMEM] * 4,
        out_specs=[VMEM] * 2,
        out_shape=[shape(half, F32), shape(half + scale_blocks(half), I16)],
        scratch_shapes=[scratch(half), scales(half_a), scales(half_b), scales(half), scales(half)],
        compiler_params=params(8 + total // 16),
        cost_estimate=meet_cost,
        name="meet",
    )(keep_a, got_a, keep_b, got_b)
    coded = swap_blk(send, reduce_order[-2])

    for bit in reversed(reduce_order[:-2]):
        now, half = half, half // 2
        keep, send = pl.pallas_call(
            add_kernel,
            in_specs=[VMEM] * 2,
            out_specs=[VMEM] * 2,
            out_shape=[shape(half, F32), shape(half + scale_blocks(half), I16)],
            scratch_shapes=[scratch(half), scales(now), scales(half), scales(half)],
            compiler_params=params(8 + total // 16),
            name="add",
        )(keep, coded)
        if bit != reduce_order[0]:
            coded = swap_blk(send, bit)

    first_keep, first_send = pl.pallas_call(
        functools.partial(near_first_kernel, stride, cells, places),
        in_specs=[SMEM] + [VMEM] * (5 + len(others)),
        out_specs=[VMEM, VMEM],
        out_shape=[shape(cells, F32), shape(cells + scale_blocks(cells), I16)],
        scratch_shapes=[
            scratch(total, 2 * rows, BF16),
            scratch(cells, 2 * rows),
            scales(cells),
            scales(cells),
        ],
        compiler_params=params(4 + total // 32),
        cost_estimate=first_cost,
        name="near_first",
    )(at_first, gathered, both, *others, tiles_low, tiles_high, other_tiles)
    first_send, send = lax.optimization_barrier((first_send, send))
    first_other = swap_rank(first_send, 2)
    coded = swap_blk(send, reduce_order[0])

    own_part = pl.pallas_call(
        self_kernel,
        in_specs=[VMEM] * 2,
        out_specs=VMEM,
        out_shape=shape(cells, F32),
        compiler_params=params(8),
        cost_estimate=meet_cost,
        name="self",
    )(charge_own, self_tiles)

    return pl.pallas_call(
        final_kernel,
        in_specs=[SMEM] + [VMEM] * 8,
        out_specs=VMEM,
        out_shape=jax.ShapeDtypeStruct(charges.shape, F32),
        scratch_shapes=[scales(stride), scales(cells)],
        compiler_params=params(8),
        name="final",
    )(
        counts, keep, coded, first_keep, first_other, target_keep, target_other, own_part, basis_t
    )


def solution(mesh):
    in_specs = (
        P("rhs", "blk"),
        P("blk"),
        P("blk", None, None),
        P("blk", None, None),
        P("blk"),
        P("blk"),
        P(("blk", "rhs"), None, None),
        P("blk"),
        P("blk"),
        P("blk", None, None),
    )
    out_specs = P("rhs", "blk")
    return jax.shard_map(body, mesh=mesh, in_specs=in_specs, out_specs=out_specs, check_vma=False)
```
